32 devices in a mesh: wide: 8 (over y, x, core), narrow: 4 (over z).
Axes of the slice: x: 2, y: 2, z: 4, core: 2. Of those that a mesh axis runs over, the one named last changes fastest.
Arguments:
- source: bfloat16 [32, 1024, 512], P(('wide', 'narrow')), may hold values from -6 to 6
- target: bfloat16 [32, 1024, 512], P(('wide', 'narrow')), may hold values from -6 to 6
- source_segments: int32 [32, 1024], P(('wide', 'narrow')), may hold values from -1 to 773, as said below
- target_segments: int32 [32, 1024], P(('wide', 'narrow')), may hold values from -1 to 773, as said below
- encoder_proj: bfloat16 [3, 512, 512], P(None, ('wide', 'narrow')), may hold values from -0.25 to 0.25
- encoder_mix: bfloat16 [512, 512], P(('wide', 'narrow')), may hold values from -1 to 1
- encoder_up: bfloat16 [512, 2048], P(('wide', 'narrow')), may hold values from -0.25 to 0.25
- encoder_down: bfloat16 [2048, 512], P(('wide', 'narrow')), may hold values from -0.125 to 0.125
- self_proj: bfloat16 [3, 512, 512], P(None, ('wide', 'narrow')), may hold values from -0.25 to 0.25
- self_mix: bfloat16 [512, 512], P(('wide', 'narrow')), may hold values from -1 to 1
- cross_proj: bfloat16 [3, 512, 512], P(None, ('wide', 'narrow')), may hold values from -0.25 to 0.25
- cross_mix: bfloat16 [512, 512], P(('wide', 'narrow')), may hold values from -1 to 1
- decoder_up: bfloat16 [512, 2048], P(('wide', 'narrow')), may hold values from -0.25 to 0.25
- decoder_down: bfloat16 [2048, 512], P(('wide', 'narrow')), may hold values from -0.125 to 0.125
- norm_gain: bfloat16 [5, 512], P(None, ('wide', 'narrow')), may hold values from 0.5 to 1.5
- norm_bias: bfloat16 [5, 512], P(None, ('wide', 'narrow')), may hold values from -1.5 to 1.5
- cotangent: bfloat16 [32, 1024, 512], P(('wide', 'narrow')), may hold values from -6 to 6
Outputs:
- decoded: bfloat16 [32, 1024, 512], P(('wide', 'narrow'))
- source_grad: bfloat16 [32, 1024, 512], P(('wide', 'narrow'))
- target_grad: bfloat16 [32, 1024, 512], P(('wide', 'narrow'))
- encoder_proj_grad: float32 [3, 512, 512], P(None, ('wide', 'narrow'))
- encoder_mix_grad: float32 [512, 512], P(('wide', 'narrow'))
- encoder_up_grad: float32 [512, 2048], P(('wide', 'narrow'))
- encoder_down_grad: float32 [2048, 512], P(('wide', 'narrow'))
- self_proj_grad: float32 [3, 512, 512], P(None, ('wide', 'narrow'))
- self_mix_grad: float32 [512, 512], P(('wide', 'narrow'))
- cross_proj_grad: float32 [3, 512, 512], P(None, ('wide', 'narrow'))
- cross_mix_grad: float32 [512, 512], P(('wide', 'narrow'))
- decoder_up_grad: float32 [512, 2048], P(('wide', 'narrow'))
- decoder_down_grad: float32 [2048, 512], P(('wide', 'narrow'))
- norm_gain_grad: float32 [5, 512], P(None, ('wide', 'narrow'))
- norm_bias_grad: float32 [5, 512], P(None, ('wide', 'narrow'))
The draws below stay inside these ranges and needn't reach their ends.
Inputs may be any that keep to these rules, and one draw needn't show every extreme that they name: `source_segments`: source sentence k and target sentence k of the same row are a translation pair; in each row sentence numbers start at 0 and rise by one, both rows of a pair hold the same number of sentences, and -1 marks the padding at the end of each row (at least one position). Each sentence has 1 to 250 tokens, and one sentence of each row has exactly 250. `target_segments`: as for source_segments: the pairs of sentences match by number, -1 marks the padding at the end of each row, and one sentence of each row has exactly 250 tokens.
All inputs are finite; a program needn't handle non-finite values.
Results may differ from the reference program's by a relative error of at most 0.024.
Values may be sent and summed in bfloat16 or wider, within the bound.
No kernel may reach another device: no remote copies, remote signals or barrier semaphores. Data moves between devices by JAX's collectives and lax.ppermute only.
A program may use at most 256 MiB of HBM per device.

```python
from functools import partial
import jax
import jax.numpy as jnp
from jax import lax

D = 512
HEADS = 8
FF = 2048
ROW_LEN = 1024
SENT_MAX = 250
ROWS = 32


def sentence_plan(key):
    dense_row = jax.random.randint(jax.random.fold_in(key, 3), (), 0, ROWS)
    row_ids = jnp.arange(ROWS)[:, None]
    slot_ids = jnp.arange(ROW_LEN)[None, :]

    def sentence_ends(subkey):
        tries = jax.random.randint(subkey, (ROWS, 3, ROW_LEN), 1, SENT_MAX + 1)
        sizes = jnp.min(tries, axis=1)
        sizes = jnp.where(row_ids == dense_row, 1, sizes)
        longest = jax.random.randint(jax.random.fold_in(key, 7), (ROWS, 1), 0, 4)
        sizes = jnp.where(slot_ids == longest, SENT_MAX, sizes)
        return jnp.cumsum(sizes, axis=1)
    source_ends = sentence_ends(jax.random.fold_in(key, 1))
    target_ends = sentence_ends(jax.random.fold_in(key, 2))
    fitting = (source_ends <= ROW_LEN - 1) & (target_ends <= ROW_LEN - 1)
    number = jnp.sum(fitting.astype(jnp.int32), axis=1, keepdims=True)

    def segment_ids(ends):
        last_end = jnp.take_along_axis(ends, number - 1, axis=1)
        inside = (ends < ROW_LEN).astype(jnp.int32)
        clipped = jnp.minimum(ends, ROW_LEN - 1)
        marks = jnp.zeros((ROWS, ROW_LEN), jnp.int32).at[jnp.broadcast_to(row_ids, ends.shape), clipped].add(inside)
        before = jnp.cumsum(marks, axis=1)
        return jnp.where(slot_ids < last_end, before, -1).astype(jnp.int32)
    return (segment_ids(source_ends), segment_ids(target_ends))


def draw_source_segments(key, part):
    plan = sentence_plan(key)
    return plan[0]


def draw_target_segments(key, part):
    plan = sentence_plan(key)
    return plan[1]


def spiked(array, stream_key, source, target, shards_of, factor):
    def block_of(position):
        return (jnp.arange(array.shape[position]) // (array.shape[position] // shards_of)).reshape((-1,) + (1,) * (array.ndim - 1 - position))

    near = jax.random.permutation(stream_key, shards_of)[block_of(target)]
    other_side = (block_of(target) + shards_of // 2) % shards_of
    return jnp.where((block_of(source) == near) | (block_of(source) == other_side), factor * array, array)


def levels(key, dims, cuts, low, top_value):
    factor_of = 1.0
    for position, parts in cuts:
        heights = jax.random.uniform(jax.random.fold_in(jax.random.fold_in(key, 6), position), (parts,), jnp.float32, low / len(cuts), top_value / len(cuts))
        factor_of = factor_of * jnp.repeat(jnp.exp(heights), dims[position] // parts).reshape((-1,) + (1,) * (len(dims) - 1 - position))
    return factor_of


def gaussian(rng, extent, deviation, limit, split=(), kind=jnp.bfloat16):
    values = deviation * jax.random.normal(rng, extent, jnp.float32)
    if split:
        values = values * levels(rng, extent, split, -0.22, 0.18)
    return jnp.clip(values, -limit, limit).astype(kind)


def bell_draw_with(own_key, shape, spread, bound, cuts, heavy, dtype=jnp.bfloat16):
    values = spread * jax.random.normal(own_key, shape, jnp.float32)
    if cuts:
        values = values * levels(own_key, shape, cuts, -0.22, 0.18)
    return jnp.clip(spiked(values, jax.random.fold_in(own_key, 3), *heavy), -bound, bound).astype(dtype)


def setup_inputs(seed: int = 0) -> dict:
    seeds = jax.random.split(jax.random.key(seed), 18)
    return {
        "source": bell_draw_with(seeds[0], (ROWS, ROW_LEN, D), 1.0, 6.0, ((0, 32),), (0, 2, 32, 2.75)),
        "target": bell_draw_with(seeds[1], (ROWS, ROW_LEN, D), 1.0, 6.0, ((0, 32),), (0, 2, 32, 2.75)),
        "source_segments": draw_source_segments(jax.random.fold_in(seeds[17], 71), 0),
        "target_segments": draw_target_segments(jax.random.fold_in(seeds[17], 71), 0),
        "encoder_proj": gaussian(seeds[4], (3, D, D), D ** -0.5, 0.25, ((1, 32),)),
        "encoder_mix": gaussian(seeds[5], (D, D), (D // 16) ** -0.5, 1.0, ((0, 32),)),
        "encoder_up": gaussian(seeds[6], (D, FF), D ** -0.5, 0.25, ((0, 32),)),
        "encoder_down": gaussian(seeds[7], (FF, D), FF ** -0.5, 0.125, ((0, 32),)),
        "self_proj": gaussian(seeds[8], (3, D, D), D ** -0.5, 0.25, ((1, 32),)),
        "self_mix": gaussian(seeds[9], (D, D), (D // 16) ** -0.5, 1.0, ((0, 32),)),
        "cross_proj": gaussian(seeds[10], (3, D, D), D ** -0.5, 0.25, ((1, 32),)),
        "cross_mix": gaussian(seeds[11], (D, D), (D // 16) ** -0.5, 1.0, ((0, 32),)),
        "decoder_up": gaussian(seeds[12], (D, FF), D ** -0.5, 0.25, ((0, 32),)),
        "decoder_down": gaussian(seeds[13], (FF, D), FF ** -0.5, 0.125, ((0, 32),)),
        "norm_gain": jnp.clip(1.0 + 0.1 * jax.random.normal(seeds[14], (5, D), jnp.float32), 0.5, 1.5).astype(jnp.bfloat16),
        "norm_bias": gaussian(seeds[15], (5, D), 0.3, 1.5, ((1, 32),)),
        "cotangent": gaussian(seeds[16], (ROWS, ROW_LEN, D), 1.0, 6.0, ((0, 32),)),
    }


@jax.custom_vjp
def low(v):
    return lax.optimization_barrier(v.astype(jnp.bfloat16)).astype(jnp.float32)

@jax.custom_vjp
def low_back(v):
    return v

def low_keep(v):
    return (low(v), None)

def low_pass(kept, grad):
    return (grad,)

def back_keep(v):
    return (v, None)

def back_low(kept, grad):
    return (low(grad),)
low.defvjp(low_keep, low_pass)
low_back.defvjp(back_keep, back_low)
norm_eps = 1e-05
masked_score = -1e+30
highest = lax.Precision.HIGHEST

def product(left, right):
    return jnp.dot(left, right, precision=highest)

def layer_norm(resid, gain, bias):
    mean = lax.optimization_barrier(jnp.mean(resid, axis=-1, keepdims=True))
    centred = resid - mean
    scale_inv = lax.rsqrt(lax.optimization_barrier(jnp.mean(centred * centred, axis=-1, keepdims=True)) + norm_eps)
    return centred * scale_inv * gain + bias

def row_attention(query, key, value, query_segments, key_segments, causal):
    scale = query.shape[-1] ** (-0.5)
    scores = low_back(jnp.einsum('qhd,khd->hqk', query, key, precision=highest) * scale)
    allowed = query_segments[:, None] == key_segments[None, :]
    if causal:
        allowed = allowed & (jnp.arange(query.shape[0])[:, None] >= jnp.arange(key.shape[0])[None, :])
    scores = jnp.where(allowed[None], scores, masked_score)
    total = jax.nn.logsumexp(scores, axis=-1, keepdims=True)
    probs = low(jnp.exp(scores - total))
    return jnp.einsum('hqk,khd->qhd', probs, value, precision=highest)

def attention(query_in, source_in, weights, mix, query_segments, key_segments, causal):
    rows = query_segments.shape[0]

    def heads(flat):
        return flat.reshape(rows, -1, HEADS, flat.shape[-1] // HEADS)
    query = low(low_back(product(query_in, weights[0])))
    key = low(low_back(product(source_in, weights[1])))
    value = low(low_back(product(source_in, weights[2])))
    inner = jax.checkpoint(partial(row_attention, causal=causal))
    mixed = lax.map(lambda items: inner(*items), (heads(query), heads(key), heads(value), query_segments, key_segments))
    mixed = low(low_back(mixed.reshape(query_in.shape)))
    return low_back(product(mixed, mix))

def feed_forward(normed_in, rows, up_weight, down_weight):

    def row_block(block):
        hidden_pre = low_back(product(block, up_weight))
        active = low(jax.nn.gelu(hidden_pre, approximate=True))
        return low_back(product(active, down_weight))
    blocks = normed_in.reshape(rows, -1, normed_in.shape[-1])
    return lax.map(jax.checkpoint(row_block), blocks).reshape(normed_in.shape)

def forward(source_segments, target_segments, source, target, encoder_proj, encoder_mix, encoder_up, encoder_down, self_proj, self_mix, cross_proj, cross_mix, decoder_up, decoder_down, gains, biases):
    rows = source.shape[0]
    width = source.shape[-1]
    source_flat = source.reshape(-1, width)
    source_low = low(source_flat)
    first = layer_norm(source_flat + attention(source_low, source_low, encoder_proj, encoder_mix, source_segments, source_segments, False), gains[0], biases[0])
    encoded = layer_norm(first + feed_forward(low(first), rows, encoder_up, encoder_down), gains[1], biases[1])
    encoded_low = low(encoded)
    target_flat = target.reshape(-1, width)
    target_low = low(target_flat)
    second = layer_norm(target_flat + attention(target_low, target_low, self_proj, self_mix, target_segments, target_segments, True), gains[2], biases[2])
    second_low = low(second)
    third = layer_norm(second + attention(second_low, encoded_low, cross_proj, cross_mix, target_segments, source_segments, False), gains[3], biases[3])
    final = layer_norm(third + feed_forward(low(third), rows, decoder_up, decoder_down), gains[4], biases[4])
    return final.reshape(target.shape)

def reference(source, target, source_segments, target_segments, encoder_proj, encoder_mix, encoder_up, encoder_down, self_proj, self_mix, cross_proj, cross_mix, decoder_up, decoder_down, norm_gain, norm_bias, cotangent):
    floats = tuple((item.astype(jnp.float32) for item in (source, target, encoder_proj, encoder_mix, encoder_up, encoder_down, self_proj, self_mix, cross_proj, cross_mix, decoder_up, decoder_down, norm_gain, norm_bias)))
    decoded, pullback = jax.vjp(partial(forward, source_segments, target_segments), *floats)
    valid = (target_segments >= 0).astype(jnp.float32)[:, :, None]
    grads = pullback(cotangent.astype(jnp.float32) * valid)
    return (decoded.astype(jnp.bfloat16), grads[0].astype(jnp.bfloat16), grads[1].astype(jnp.bfloat16), grads[2], grads[3], grads[4], grads[5], grads[6], grads[7], grads[8], grads[9], grads[10], grads[11], grads[12], grads[13])
```

```python
from functools import partial

import jax
import jax.numpy as jnp
from jax import lax
from jax.sharding import PartitionSpec as P

HEADS = 8


norm_eps = 1e-05
masked_score = -1e30


def project(left, weight):
    return jnp.dot(left, weight, preferred_element_type=jnp.float32)


def project_back(grad, weight):
    return jnp.einsum("nf,df->nd", grad, weight, preferred_element_type=jnp.float32)


def outer_sum(left, grad):
    return jnp.einsum("nd,nf->df", left, grad, preferred_element_type=jnp.float32)


def layer_norm(resid, gain, bias):
    mean = jnp.mean(resid, axis=-1, keepdims=True)
    centred = resid - mean
    scale_inv = lax.rsqrt(jnp.mean(centred * centred, axis=-1, keepdims=True) + norm_eps)
    normed = centred * scale_inv
    return (normed * gain + bias, (normed, scale_inv))


def layer_norm_back(grad, saved, gain):
    normed, scale_inv = saved
    scaled = grad * gain
    mean_plain = jnp.mean(scaled, axis=-1, keepdims=True)
    mean_normed = jnp.mean(scaled * normed, axis=-1, keepdims=True)
    grad_resid = scale_inv * (scaled - mean_plain - normed * mean_normed)
    return (grad_resid, jnp.sum(grad * normed, axis=0), jnp.sum(grad, axis=0))


def allowed_keys(query_segments, key_segments, start, causal):
    allowed = query_segments[:, None] == key_segments[None, :]
    if causal:
        query_place = start + lax.broadcasted_iota(jnp.int32, allowed.shape, 0)
        key_place = lax.broadcasted_iota(jnp.int32, allowed.shape, 1)
        allowed = allowed & (query_place >= key_place)
    return allowed


def block_scores(query_block, key_row, allowed, scale):
    scores = (
        jnp.einsum("qhd,khd->hqk", query_block, key_row, preferred_element_type=jnp.float32) * scale
    )
    return jnp.where(allowed[None], scores, masked_score)


def block_layout(query, query_segments):
    rows, length = query_segments.shape
    block = min(512, length)
    count = length // block
    width = query.shape[-1] // HEADS
    return (rows, block, count, width)


def attend_forward(query, key, value, query_segments, key_segments, causal):
    rows, block, count, width = block_layout(query, query_segments)
    scale = width ** (-0.5)
    key_rows = key.reshape(rows, -1, HEADS, width)
    value_rows = value.reshape(rows, -1, HEADS, width)
    query_blocks = query.reshape(rows * count, block, HEADS, width)
    segment_blocks = query_segments.reshape(rows * count, block)

    def one_block(items):
        index, query_block, segment_block = items
        row = index // count
        start = index % count * block
        key_row = lax.dynamic_index_in_dim(key_rows, row, 0, keepdims=False)
        value_row = lax.dynamic_index_in_dim(value_rows, row, 0, keepdims=False)
        key_segment = lax.dynamic_index_in_dim(key_segments, row, 0, keepdims=False)
        scores = block_scores(
            query_block, key_row, allowed_keys(segment_block, key_segment, start, causal), scale
        )
        peak = jnp.max(scores, axis=-1, keepdims=True)
        total = peak + jnp.log(jnp.sum(jnp.exp(scores - peak), axis=-1, keepdims=True))
        probs = jnp.exp(scores - total).astype(jnp.bfloat16)
        mixed = jnp.einsum("hqk,khd->qhd", probs, value_row, preferred_element_type=jnp.float32)
        return (mixed.astype(jnp.bfloat16), total[..., 0])

    indices = jnp.arange(rows * count, dtype=jnp.int32)
    mixed, totals = lax.map(one_block, (indices, query_blocks, segment_blocks))
    return (mixed.reshape(query.shape), totals)


def attend_backward(query, key, value, query_segments, key_segments, causal, totals, grad_mixed):
    rows, block, count, width = block_layout(query, query_segments)
    scale = width ** (-0.5)
    key_length = key.shape[0] // rows
    key_rows = key.reshape(rows, key_length, HEADS, width)
    value_rows = value.reshape(rows, key_length, HEADS, width)
    query_blocks = query.reshape(rows * count, block, HEADS, width)
    grad_blocks = grad_mixed.reshape(rows * count, block, HEADS, width)
    segment_blocks = query_segments.reshape(rows * count, block)

    def one_block(items):
        index, query_block, segment_block, total, grad_block = items
        row = index // count
        start = index % count * block
        key_row = lax.dynamic_index_in_dim(key_rows, row, 0, keepdims=False)
        value_row = lax.dynamic_index_in_dim(value_rows, row, 0, keepdims=False)
        key_segment = lax.dynamic_index_in_dim(key_segments, row, 0, keepdims=False)
        scores = block_scores(
            query_block, key_row, allowed_keys(segment_block, key_segment, start, causal), scale
        )
        probs = jnp.exp(scores - total[..., None])
        grad_probs = jnp.einsum(
            "qhd,khd->hqk", grad_block, value_row, preferred_element_type=jnp.float32
        )
        inner = jnp.sum(probs * grad_probs, axis=-1, keepdims=True)
        grad_scores = (probs * (grad_probs - inner)).astype(jnp.bfloat16)
        grad_query = (
            jnp.einsum("hqk,khd->qhd", grad_scores, key_row, preferred_element_type=jnp.float32)
            * scale
        )
        grad_key = (
            jnp.einsum("hqk,qhd->khd", grad_scores, query_block, preferred_element_type=jnp.float32)
            * scale
        )
        grad_value = jnp.einsum(
            "hqk,qhd->khd",
            probs.astype(jnp.bfloat16),
            grad_block,
            preferred_element_type=jnp.float32,
        )
        return (grad_query.astype(jnp.bfloat16), grad_key, grad_value)

    indices = jnp.arange(rows * count, dtype=jnp.int32)
    grad_query, grad_key, grad_value = lax.map(
        one_block, (indices, query_blocks, segment_blocks, totals, grad_blocks)
    )
    grad_key = jnp.sum(grad_key.reshape(rows, count, key_length, HEADS * width), axis=1)
    grad_value = jnp.sum(grad_value.reshape(rows, count, key_length, HEADS * width), axis=1)
    return (
        grad_query.reshape(query.shape),
        grad_key.reshape(key.shape).astype(jnp.bfloat16),
        grad_value.reshape(value.shape).astype(jnp.bfloat16),
    )


def attention_forward(query_in, source_in, weights, mix, query_segments, key_segments, causal):
    query = project(query_in, weights[0]).astype(jnp.bfloat16)
    key = project(source_in, weights[1]).astype(jnp.bfloat16)
    value = project(source_in, weights[2]).astype(jnp.bfloat16)
    mixed, totals = attend_forward(query, key, value, query_segments, key_segments, causal)
    return (project(mixed, mix), (query, key, value, mixed, totals))


def attention_backward(
    grad, query_in, source_in, weights, mix, saved, query_segments, key_segments, causal
):
    query, key, value, mixed, totals = saved
    grad_low = grad.astype(jnp.bfloat16)
    mix_grad = outer_sum(mixed, grad_low)
    grad_mixed = project_back(grad_low, mix).astype(jnp.bfloat16)
    grad_query, grad_key, grad_value = attend_backward(
        query, key, value, query_segments, key_segments, causal, totals, grad_mixed
    )
    proj_grad = jnp.stack(
        [
            outer_sum(query_in, grad_query),
            outer_sum(source_in, grad_key),
            outer_sum(source_in, grad_value),
        ]
    )
    query_side = project_back(grad_query, weights[0])
    source_side = project_back(grad_key, weights[1]) + project_back(grad_value, weights[2])
    return (query_side, source_side, proj_grad, mix_grad)


def ffn_forward(normed_in, up_weight, down_weight):
    hidden_pre = project(normed_in, up_weight)
    active = jax.nn.gelu(hidden_pre, approximate=True).astype(jnp.bfloat16)
    return (project(active, down_weight), (hidden_pre, active))


def ffn_backward(grad, normed_in, up_weight, down_weight, saved):
    hidden_pre, active = saved
    grad_low = grad.astype(jnp.bfloat16)
    down_grad = outer_sum(active, grad_low)
    grad_active = project_back(grad_low, down_weight)
    unused, pullback = jax.vjp(partial(jax.nn.gelu, approximate=True), hidden_pre)
    grad_hidden = pullback(grad_active)[0].astype(jnp.bfloat16)
    up_grad = outer_sum(normed_in, grad_hidden)
    return (project_back(grad_hidden, up_weight), up_grad, down_grad)


def gather_all(shards):
    count = lax.axis_size(("wide", "narrow"))
    flat = [jnp.reshape(item, (-1, 512)) for item in shards]
    whole = lax.all_gather(jnp.concatenate(flat), ("wide", "narrow"), axis=0, tiled=False)
    whole = whole.reshape(count, -1, 512)
    parts = []
    start = 0
    for item, piece in zip(shards, flat):
        stop = start + piece.shape[0]
        block = whole[:, start:stop]
        start = stop
        if item.ndim == 3:
            block = block.reshape(count, item.shape[0], -1, item.shape[2])
            block = jnp.moveaxis(block, 0, 1)
            parts.append(block.reshape(item.shape[0], -1, item.shape[2]))
        else:
            parts.append(block.reshape(-1, item.shape[1]))
    return parts


def scatter_all(grads, shards):
    count = lax.axis_size(("wide", "narrow"))
    flat = []
    for grad in grads:
        if grad.ndim == 3:
            block = grad.reshape(grad.shape[0], count, -1, grad.shape[2])
            block = jnp.moveaxis(block, 1, 0)
        else:
            block = grad
        flat.append(block.astype(jnp.bfloat16).reshape(count, -1, 512))
    whole = jnp.concatenate(flat, axis=1)
    whole = lax.psum_scatter(whole, "wide", scatter_dimension=0, tiled=True)
    whole = lax.psum_scatter(whole, "narrow", scatter_dimension=0, tiled=True)[0]
    parts = []
    start = 0
    for item in shards:
        stop = start + item.size // 512
        parts.append(whole[start:stop].astype(jnp.float32).reshape(item.shape))
        start = stop
    return parts


def on_device(
    source,
    target,
    source_segments,
    target_segments,
    encoder_proj,
    encoder_mix,
    encoder_up,
    encoder_down,
    self_proj,
    self_mix,
    cross_proj,
    cross_mix,
    decoder_up,
    decoder_down,
    norm_gain,
    norm_bias,
    cotangent,
):
    width = source.shape[-1]
    source_low = source.reshape(-1, width)
    target_low = target.reshape(-1, width)
    shards = (encoder_proj, encoder_mix, encoder_up, encoder_down, self_proj, self_mix)
    shards += (cross_proj, cross_mix, decoder_up, decoder_down)
    weights = gather_all(shards)
    enc_proj_all, enc_mix_all = weights[:2]
    norm_all = lax.all_gather(
        jnp.concatenate([norm_gain, norm_bias]), ("wide", "narrow"), axis=1, tiled=True
    )
    gain_all, bias_all = norm_all[:5], norm_all[5:]
    gains = gain_all.astype(jnp.float32)
    biases = bias_all.astype(jnp.float32)
    branch, enc_attn_saved = attention_forward(
        source_low, source_low, enc_proj_all, enc_mix_all, source_segments, source_segments, False
    )
    first, norm_first = layer_norm(source_low.astype(jnp.float32) + branch, gains[0], biases[0])
    first_low = first.astype(jnp.bfloat16)
    enc_ffn_all = weights[2:4]
    branch, enc_ffn_saved = ffn_forward(first_low, enc_ffn_all[0], enc_ffn_all[1])
    encoded, norm_encoded = layer_norm(first + branch, gains[1], biases[1])
    encoded_low = encoded.astype(jnp.bfloat16)
    self_all = weights[4:6]
    branch, self_saved = attention_forward(
        target_low, target_low, self_all[0], self_all[1], target_segments, target_segments, True
    )
    second, norm_second = layer_norm(target_low.astype(jnp.float32) + branch, gains[2], biases[2])
    second_low = second.astype(jnp.bfloat16)
    cross_all = weights[6:8]
    branch, cross_saved = attention_forward(
        second_low, encoded_low, cross_all[0], cross_all[1], target_segments, source_segments, False
    )
    third, norm_third = layer_norm(second + branch, gains[3], biases[3])
    third_low = third.astype(jnp.bfloat16)
    dec_ffn_all = weights[8:10]
    branch, dec_ffn_saved = ffn_forward(third_low, dec_ffn_all[0], dec_ffn_all[1])
    final, norm_final = layer_norm(third + branch, gains[4], biases[4])
    valid = (target_segments >= 0).reshape(-1, 1).astype(jnp.float32)
    grad_final = cotangent.reshape(-1, width).astype(jnp.float32) * valid
    grad_resid, gain_four, bias_four = layer_norm_back(grad_final, norm_final, gains[4])
    dec_ffn_back = weights[8:10]
    grad_input, up_grad, down_grad = ffn_backward(
        grad_resid, third_low, dec_ffn_back[0], dec_ffn_back[1], dec_ffn_saved
    )
    dec_ffn_grads = [up_grad, down_grad]
    grad_resid, gain_three, bias_three = layer_norm_back(
        grad_resid + grad_input, norm_third, gains[3]
    )
    cross_back = weights[6:8]
    query_side, source_side, proj_grad, mix_grad = attention_backward(
        grad_resid,
        second_low,
        encoded_low,
        cross_back[0],
        cross_back[1],
        cross_saved,
        target_segments,
        source_segments,
        False,
    )
    cross_grads = [proj_grad, mix_grad]
    grad_encoded = source_side
    grad_resid, gain_two, bias_two = layer_norm_back(grad_resid + query_side, norm_second, gains[2])
    self_back = weights[4:6]
    query_side, source_side, proj_grad, mix_grad = attention_backward(
        grad_resid,
        target_low,
        target_low,
        self_back[0],
        self_back[1],
        self_saved,
        target_segments,
        target_segments,
        True,
    )
    self_grads = [proj_grad, mix_grad]
    target_grad = grad_resid + query_side + source_side
    grad_resid, gain_one, bias_one = layer_norm_back(grad_encoded, norm_encoded, gains[1])
    enc_ffn_back = weights[2:4]
    grad_input, up_grad, down_grad = ffn_backward(
        grad_resid, first_low, enc_ffn_back[0], enc_ffn_back[1], enc_ffn_saved
    )
    enc_ffn_grads = [up_grad, down_grad]
    grad_resid, gain_zero, bias_zero = layer_norm_back(
        grad_resid + grad_input, norm_first, gains[0]
    )
    enc_back = weights[0:2]
    query_side, source_side, proj_grad, mix_grad = attention_backward(
        grad_resid,
        source_low,
        source_low,
        enc_back[0],
        enc_back[1],
        enc_attn_saved,
        source_segments,
        source_segments,
        False,
    )
    source_grad = grad_resid + query_side + source_side
    gain_grad = jnp.stack([gain_zero, gain_one, gain_two, gain_three, gain_four])
    bias_grad = jnp.stack([bias_zero, bias_one, bias_two, bias_three, bias_four])
    norm_grad = lax.psum_scatter(
        jnp.concatenate([gain_grad, bias_grad]), ("wide", "narrow"), scatter_dimension=1, tiled=True
    )
    gain_shard, bias_shard = norm_grad[:5], norm_grad[5:]
    grads = [proj_grad, mix_grad] + enc_ffn_grads + self_grads + cross_grads + dec_ffn_grads
    (
        enc_proj_grad,
        enc_mix_grad,
        enc_up_grad,
        enc_down_grad,
        self_proj_grad,
        self_mix_grad,
        cross_proj_grad,
        cross_mix_grad,
        dec_up_grad,
        dec_down_grad,
    ) = scatter_all(grads, shards)
    return (
        final.reshape(target.shape).astype(jnp.bfloat16),
        source_grad.reshape(source.shape).astype(jnp.bfloat16),
        target_grad.reshape(target.shape).astype(jnp.bfloat16),
        enc_proj_grad,
        enc_mix_grad,
        enc_up_grad,
        enc_down_grad,
        self_proj_grad,
        self_mix_grad,
        cross_proj_grad,
        cross_mix_grad,
        dec_up_grad,
        dec_down_grad,
        gain_shard,
        bias_shard,
    )


def solution(mesh):
    return jax.shard_map(
        on_device,
        mesh=mesh,
        in_specs=(
            P(("wide", "narrow"), None, None),
            P(("wide", "narrow"), None, None),
            P(("wide", "narrow"), None),
            P(("wide", "narrow"), None),
            P(None, ("wide", "narrow"), None),
            P(("wide", "narrow"), None),
            P(("wide", "narrow"), None),
            P(("wide", "narrow"), None),
            P(None, ("wide", "narrow"), None),
            P(("wide", "narrow"), None),
            P(None, ("wide", "narrow"), None),
            P(("wide", "narrow"), None),
            P(("wide", "narrow"), None),
            P(("wide", "narrow"), None),
            P(None, ("wide", "narrow")),
            P(None, ("wide", "narrow")),
            P(("wide", "narrow"), None, None),
        ),
        out_specs=(
            P(("wide", "narrow"), None, None),
            P(("wide", "narrow"), None, None),
            P(("wide", "narrow"), None, None),
            P(None, ("wide", "narrow"), None),
            P(("wide", "narrow"), None),
            P(("wide", "narrow"), None),
            P(("wide", "narrow"), None),
            P(None, ("wide", "narrow"), None),
            P(("wide", "narrow"), None),
            P(None, ("wide", "narrow"), None),
            P(("wide", "narrow"), None),
            P(("wide", "narrow"), None),
            P(("wide", "narrow"), None),
            P(None, ("wide", "narrow")),
            P(None, ("wide", "narrow")),
        ),
        check_vma=False,
    )
```

```python
from functools import partial

import jax
import jax.numpy as jnp
from jax import lax
from jax.experimental import pallas as pl
from jax.experimental.pallas import tpu as pltpu
from jax.sharding import PartitionSpec as P

HEADS = 8
norm_eps = 1e-05
masked_score = -1e30
lowest = -3e38
log2_e = 1.4426950408889634
BLOCK = 128
TILE = 256
PAIR = 2
f32 = jnp.float32
bf16 = jnp.bfloat16


def dot(left, right, left_dim=1, right_dim=0):
    dims = (((left_dim,), (right_dim,)), ((), ()))
    return lax.dot_general(left, right, dims, preferred_element_type=f32)


def normalise(resid):
    mean = jnp.mean(resid, axis=-1, keepdims=True)
    centred = resid - mean
    scale_inv = lax.rsqrt(jnp.mean(centred * centred, axis=-1, keepdims=True) + norm_eps)
    return centred * scale_inv, scale_inv


def norm_back(grad, normed, scale_inv, gain):
    scaled = grad * gain
    mean_plain = jnp.mean(scaled, axis=-1, keepdims=True)
    mean_normed = jnp.mean(scaled * normed, axis=-1, keepdims=True)
    return scale_inv * (scaled - mean_plain - normed * mean_normed)


def key_ranges(query_segments, key_segments, causal):
    big = jnp.int32(1 << 30)
    query_order = jnp.where(query_segments < 0, big, query_segments).reshape(-1, BLOCK)
    key_order = jnp.where(key_segments < 0, big, key_segments).reshape(1, -1)
    first = jnp.sum((key_order < query_order[:, :1]).astype(jnp.int32), axis=1)
    stop = jnp.sum((key_order <= query_order[:, -1:]).astype(jnp.int32), axis=1)
    real = jnp.sum((key_order < big).astype(jnp.int32))
    if causal:
        stop = jnp.minimum(stop, (jnp.arange(stop.shape[0]) + 1) * BLOCK)
    start = first // 16 * 16
    tiles = (stop - start + TILE - 1) // TILE
    real_tiles = jnp.maximum((jnp.minimum(stop, real) - start + TILE - 1) // TILE, 0)
    real_tiles = jnp.where(first >= real, 0, real_tiles)
    return jnp.stack([start, tiles, real_tiles]).astype(jnp.int32)


def key_columns(key_segments):
    flat = jnp.pad(key_segments.reshape(-1), (0, TILE), constant_values=-2)
    return jnp.broadcast_to(flat[:, None], (flat.shape[0], 128))


def head_pair_mask():
    lane = lax.broadcasted_iota(jnp.int32, (1, 128), 1)
    return lane < 64


def stack_heads(block, even):
    zero = jnp.zeros_like(block)
    return jnp.concatenate([jnp.where(even, block, zero), jnp.where(even, zero, block)], axis=0)


def tile_bias(bias_ref, key_col_ref, query_row, key_start, query_start, causal):
    allowed = key_col_ref[pl.ds(key_start, TILE), :] == query_row
    if causal:
        key_place = key_start + lax.broadcasted_iota(jnp.int32, (TILE, BLOCK), 0)
        query_place = query_start + lax.broadcasted_iota(jnp.int32, (TILE, BLOCK), 1)
        allowed = allowed & (key_place <= query_place)
    bias_ref[...] = jnp.where(allowed, 0.0, masked_score).astype(f32)


def forward_kernel(causal, fresh, ranges, *refs):
    if fresh:
        (own, key_col, query_seg, proj, mix, norm_out,
         resid_out, low_out, q_out, k_out, v_out, o_out, lse_out,
         stacked, bias, acc, peak, total) = refs
    else:
        (own, norm_own, other, key_col, query_seg, proj, mix, norm_out,
         resid_out, low_out, q_out, k_out, v_out, o_out, lse_out,
         stacked, bias, acc, peak, total) = refs
    rows = own.shape[0]
    even = head_pair_mask()
    scale = 0.125 * log2_e

    def fill(step, carry):
        at = pl.multiple_of(step * TILE, TILE)
        block = own[pl.ds(at, TILE), :]
        if fresh:
            block_low = block
            key_block = block
        else:
            normed, _ = normalise(block)
            block_low = (normed * norm_own[0:1, :] + norm_own[1:2, :]).astype(bf16)
            low_out[pl.ds(at, TILE), :] = block_low
            key_block = other[pl.ds(at, TILE), :]
        query = dot(block_low, proj[0]).astype(bf16)
        q_out[pl.ds(at, TILE), :] = query
        for sub in range(TILE // BLOCK):
            for pair in range(4):
                part = query[sub * BLOCK : (sub + 1) * BLOCK, pair * 128 : (pair + 1) * 128]
                stacked[step * (TILE // BLOCK) + sub, pair] = stack_heads(part, even)
        k_out[pl.ds(at, TILE), :] = dot(key_block, proj[1]).astype(bf16)
        v_out[pl.ds(at, TILE), :] = dot(key_block, proj[2]).astype(bf16)
        return carry

    lax.fori_loop(0, rows // TILE, fill, 0)
    k_out[rows:, :] = jnp.zeros((TILE, k_out.shape[1]), bf16)
    v_out[rows:, :] = jnp.zeros((TILE, v_out.shape[1]), bf16)

    def one_block(index, carry):
        start = ranges[0, index]
        tiles = ranges[1, index]
        query_start = pl.multiple_of(index * BLOCK, BLOCK)
        query_row = query_seg[index]
        peak[...] = jnp.full(peak.shape, lowest, f32)
        total[...] = jnp.zeros(total.shape, f32)
        acc[...] = jnp.zeros(acc.shape, f32)

        def one_tile(tile, inner):
            at = pl.multiple_of(start + tile * TILE, 16)
            tile_bias(bias, key_col, query_row, at, query_start, causal)
            for pair in range(4):
                lanes = slice(pair * 128, (pair + 1) * 128)
                scores = dot(k_out[pl.ds(at, TILE), lanes], stacked[index, pair], 1, 1)
                blocked = bias[...]
                scores = scores * scale + jnp.concatenate([blocked, blocked], axis=1)
                before = peak[pair : pair + 1, :]
                after = jnp.maximum(before, jnp.max(scores, axis=0, keepdims=True))
                probs = jnp.exp2(scores - after)
                shrink = jnp.exp2(before - after)
                peak[pair : pair + 1, :] = after
                total[pair : pair + 1, :] = total[pair : pair + 1, :] * shrink + jnp.sum(
                    probs, axis=0, keepdims=True
                )
                mixed = dot(v_out[pl.ds(at, TILE), lanes], probs.astype(bf16), 0, 0)
                top = pair * 128
                acc[top : top + 64, :] = acc[top : top + 64, :] * shrink[:, :128] + mixed[:64, :128]
                acc[top + 64 : top + 128, :] = (
                    acc[top + 64 : top + 128, :] * shrink[:, 128:] + mixed[64:, 128:]
                )
            return inner

        lax.fori_loop(0, tiles, one_tile, 0)
        for pair in range(4):
            inverse = 1.0 / total[pair : pair + 1, :]
            top = pair * 128
            o_out[top : top + 64, pl.ds(query_start, BLOCK)] = (
                acc[top : top + 64, :] * inverse[:, :128]
            ).astype(bf16)
            o_out[top + 64 : top + 128, pl.ds(query_start, BLOCK)] = (
                acc[top + 64 : top + 128, :] * inverse[:, 128:]
            ).astype(bf16)
        lse_out[index] = peak[...] + jnp.log2(total[...])
        return carry

    lax.fori_loop(0, rows // BLOCK, one_block, 0)

    def finish(step, carry):
        at = pl.multiple_of(step * TILE, TILE)
        block = own[pl.ds(at, TILE), :]
        if fresh:
            block = block.astype(f32)
        else:
            normed, _ = normalise(block)
            block = normed * norm_own[0:1, :] + norm_own[1:2, :]
        resid = block + dot(o_out[:, pl.ds(at, TILE)], mix[...], 0, 0)
        resid_out[pl.ds(at, TILE), :] = resid
        if fresh:
            normed, _ = normalise(resid)
            low_out[pl.ds(at, TILE), :] = (normed * norm_out[0:1, :] + norm_out[1:2, :]).astype(bf16)
        return carry

    lax.fori_loop(0, rows // TILE, finish, 0)


def vmem(count):
    return [pl.BlockSpec(memory_space=pltpu.VMEM)] * count


def cost(flops, moved):
    return pl.CostEstimate(flops=int(flops), bytes_accessed=int(moved), transcendentals=0)


def attend_forward(own, norm_own, other, key_col, query_seg, ranges, weights, norm_out, causal):
    fresh = norm_own is None
    rows, width = own.shape
    blocks = rows // BLOCK
    ins = [own] if fresh else [own, norm_own, other]
    ins += [key_col, query_seg, *weights, norm_out]
    shapes = [
        jax.ShapeDtypeStruct((rows, width), f32),
        jax.ShapeDtypeStruct((rows, width), bf16),
        jax.ShapeDtypeStruct((rows, width), bf16),
        jax.ShapeDtypeStruct((rows + TILE, width), bf16),
        jax.ShapeDtypeStruct((rows + TILE, width), bf16),
        jax.ShapeDtypeStruct((width, rows), bf16),
        jax.ShapeDtypeStruct((blocks, 4, 2 * BLOCK), f32),
    ]
    return pl.pallas_call(
        partial(forward_kernel, causal, fresh),
        out_shape=shapes,
        in_specs=[pl.BlockSpec(memory_space=pltpu.SMEM)] + vmem(len(ins)),
        out_specs=vmem(len(shapes)),
        scratch_shapes=[
            pltpu.VMEM((blocks, 4, 2 * BLOCK, 128), bf16),
            pltpu.VMEM((TILE, BLOCK), f32),
            pltpu.VMEM((width, BLOCK), f32),
            pltpu.VMEM((4, 2 * BLOCK), f32),
            pltpu.VMEM((4, 2 * BLOCK), f32),
        ],
        compiler_params=pltpu.CompilerParams(vmem_limit_bytes=32 * 2**20),
        cost_estimate=cost(4e9, 12e6),
        name="attend_forward",
    )(ranges, *ins)


def backward_kernel(causal, same, ranges, *refs):
    if same:
        (grad, resid, norm, own, q_in, k_in, v_in, o_in, lse, key_col, query_seg, proj, mix,
         own_grad, weight_grad, norm_grad,
         sums, low, stacked, grad_stacked, inner_rows, bias, acc, dq, dk, dv) = refs
        other = own
        other_grad = None
    else:
        (grad, resid, norm, own, other, q_in, k_in, v_in, o_in, lse, key_col, query_seg, proj, mix,
         own_grad, other_grad, weight_grad, norm_grad,
         low, stacked, grad_stacked, inner_rows, bias, acc, dq, dk, dv) = refs
        sums = own_grad
    rows = own.shape[0]
    even = head_pair_mask()
    scale = 0.125 * log2_e
    norm_grad[...] = jnp.zeros(norm_grad.shape, f32)

    def prepare(step, carry):
        at = pl.multiple_of(step * TILE, TILE)
        block = grad[pl.ds(at, TILE), :]
        normed, scale_inv = normalise(resid[pl.ds(at, TILE), :])
        norm_grad[0:1, :] += jnp.sum(block * normed, axis=0, keepdims=True)
        norm_grad[1:2, :] += jnp.sum(block, axis=0, keepdims=True)
        block = norm_back(block, normed, scale_inv, norm[0:1, :])
        sums[pl.ds(at, TILE), :] = block
        block = block.astype(bf16)
        low[pl.ds(at, TILE), :] = block
        grad_mixed = dot(block, mix[...], 1, 1).astype(bf16)
        flipped = dot(mix[...], block, 1, 1).astype(bf16).astype(f32)
        flipped = flipped * o_in[:, pl.ds(at, TILE)].astype(f32)
        inner = [jnp.sum(flipped[head * 64 : (head + 1) * 64, :], axis=0, keepdims=True) for head in range(HEADS)]
        query = q_in[pl.ds(at, TILE), :]
        for sub in range(TILE // BLOCK):
            spot = step * (TILE // BLOCK) + sub
            span = slice(sub * BLOCK, (sub + 1) * BLOCK)
            rows_of = []
            for pair in range(4):
                lanes = slice(pair * 128, (pair + 1) * 128)
                stacked[spot, pair] = stack_heads(query[span, lanes], even)
                grad_stacked[spot, pair] = stack_heads(grad_mixed[span, lanes], even)
                rows_of.append(jnp.concatenate([inner[2 * pair][:, span], inner[2 * pair + 1][:, span]], axis=1))
            inner_rows[spot] = jnp.concatenate(rows_of, axis=0)
        return carry

    lax.fori_loop(0, rows // TILE, prepare, 0)
    weight_grad[3] = dot(o_in[...], low[...]).astype(bf16)
    dk[...] = jnp.zeros(dk.shape, f32)
    dv[...] = jnp.zeros(dv.shape, f32)

    def one_block(index, carry):
        start = ranges[0, index]
        tiles = ranges[2, index]
        query_start = pl.multiple_of(index * BLOCK, BLOCK)
        query_row = query_seg[index]
        acc[...] = jnp.zeros(acc.shape, f32)

        def one_tile(tile, inner):
            at = pl.multiple_of(start + tile * TILE, 16)
            tile_bias(bias, key_col, query_row, at, query_start, causal)
            for pair in range(4):
                lanes = slice(pair * 128, (pair + 1) * 128)
                key = k_in[pl.ds(at, TILE), lanes]
                query = stacked[index, pair]
                grad_out = grad_stacked[index, pair]
                scores = dot(key, query, 1, 1)
                blocked = bias[...]
                scores = scores * scale + jnp.concatenate([blocked, blocked], axis=1)
                probs = jnp.exp2(scores - lse[index, pair : pair + 1, :])
                grad_probs = dot(v_in[pl.ds(at, TILE), lanes], grad_out, 1, 1)
                grad_scores = (probs * (grad_probs - inner_rows[index, pair : pair + 1, :])).astype(bf16)
                dv[pl.ds(at, TILE), lanes] += dot(probs.astype(bf16), grad_out)
                dk[pl.ds(at, TILE), lanes] += dot(grad_scores, query)
                mixed = dot(key, grad_scores, 0, 0)
                top = pair * 128
                acc[top : top + 64, :] += mixed[:64, :128]
                acc[top + 64 : top + 128, :] += mixed[64:, 128:]
            return inner

        lax.fori_loop(0, tiles, one_tile, 0)
        dq[pl.ds(query_start, BLOCK), :] = (acc[...].T * 0.125).astype(bf16)
        return carry

    lax.fori_loop(0, rows // BLOCK, one_block, 0)
    dk_low = (dk[:rows, :] * 0.125).astype(bf16)
    dv_low = dv[:rows, :].astype(bf16)
    low[...] = dk_low
    weight_grad[0] = dot(own[...], dq[...], 0, 0).astype(bf16)
    weight_grad[1] = dot(other[...], low[...], 0, 0).astype(bf16)
    query_side = sums[...] + dot(dq[...], proj[0], 1, 1)
    source_side = dot(low[...], proj[1], 1, 1)
    if not same:
        own_grad[...] = query_side
        other_grad[...] = source_side
    else:
        sums[...] = query_side + source_side
    low[...] = dv_low
    weight_grad[2] = dot(other[...], low[...], 0, 0).astype(bf16)
    source_side = dot(low[...], proj[2], 1, 1)
    if not same:
        other_grad[...] += source_side
    else:
        own_grad[...] = (sums[...] + source_side).astype(own_grad.dtype)


def attend_backward(grad, resid, norm, own, other, saved, key_col, query_seg, ranges, weights, causal, out_dtype):
    same = other is None
    rows, width = own.shape
    blocks = rows // BLOCK
    ins = [grad, resid, norm, own] + ([] if same else [other])
    ins += [*saved, key_col, query_seg, *weights]
    shapes = [jax.ShapeDtypeStruct((rows, width), out_dtype)]
    if not same:
        shapes.append(jax.ShapeDtypeStruct((rows, width), f32))
    shapes.append(jax.ShapeDtypeStruct((4, width, width), bf16))
    shapes.append(jax.ShapeDtypeStruct((2, width), f32))
    return pl.pallas_call(
        partial(backward_kernel, causal, same),
        out_shape=shapes,
        in_specs=[pl.BlockSpec(memory_space=pltpu.SMEM)] + vmem(len(ins)),
        out_specs=vmem(len(shapes)),
        scratch_shapes=([pltpu.VMEM((rows, width), f32)] if same else [])
        + [
            pltpu.VMEM((rows, width), bf16),
            pltpu.VMEM((blocks, 4, 2 * BLOCK, 128), bf16),
            pltpu.VMEM((blocks, 4, 2 * BLOCK, 128), bf16),
            pltpu.VMEM((blocks, 4, 2 * BLOCK), f32),
            pltpu.VMEM((TILE, BLOCK), f32),
            pltpu.VMEM((width, BLOCK), f32),
            pltpu.VMEM((rows, width), bf16),
            pltpu.VMEM((rows + TILE, width), f32),
            pltpu.VMEM((rows + TILE, width), f32),
        ],
        compiler_params=pltpu.CompilerParams(vmem_limit_bytes=48 * 2**20),
        cost_estimate=cost(10e9, 20e6),
        name="attend_backward",
    )(ranges, *ins)


root_two_pi = 0.7978845608028654
CHUNK = 512


def gelu(pre):
    square = pre * pre
    flat = jnp.tanh(pre * (root_two_pi + (root_two_pi * 0.044715) * square))
    return pre * (0.5 + 0.5 * flat), square, flat


def gelu_slope(pre, square, flat):
    half = 0.5 + 0.5 * flat
    inner = (0.5 * root_two_pi) + (1.5 * root_two_pi * 0.044715) * square
    return half + pre * ((1.0 - flat * flat) * inner)


def ffn_forward_kernel(resid_in, norm_in, up, down, norm_out, resid_out, low_out):
    rows = resid_in.shape[0]

    def one_block(step, carry):
        at = pl.multiple_of(step * TILE, TILE)
        normed, _ = normalise(resid_in[pl.ds(at, TILE), :])
        block = normed * norm_in[0:1, :] + norm_in[1:2, :]
        block_low = block.astype(bf16)
        for chunk in range(up.shape[1] // CHUNK):
            lanes = slice(chunk * CHUNK, (chunk + 1) * CHUNK)
            active, _, _ = gelu(dot(block_low, up[:, lanes]))
            block = block + dot(active.astype(bf16), down[lanes, :])
        resid_out[pl.ds(at, TILE), :] = block
        normed, _ = normalise(block)
        low_out[pl.ds(at, TILE), :] = (normed * norm_out[0:1, :] + norm_out[1:2, :]).astype(bf16)
        return carry

    lax.fori_loop(0, rows // TILE, one_block, 0)


def ffn_forward(resid, norm_in, up, down, norm_out):
    rows, width = resid.shape
    shapes = [jax.ShapeDtypeStruct((rows, width), f32), jax.ShapeDtypeStruct((rows, width), bf16)]
    return pl.pallas_call(
        ffn_forward_kernel,
        out_shape=shapes,
        in_specs=vmem(5),
        out_specs=vmem(2),
        compiler_params=pltpu.CompilerParams(vmem_limit_bytes=32 * 2**20),
        cost_estimate=cost(6e9, 9e6),
        name="ffn_forward",
    )(resid, norm_in, up, down, norm_out)


def ffn_grads(step, active, grad_low, block_low, grad_pre, up_grad, down_grad):
    at = pl.multiple_of(step * CHUNK, CHUNK)
    down_grad[pl.ds(at, CHUNK), :] = dot(active[:, pl.ds(at, CHUNK)], grad_low[...], 0, 0).astype(bf16)
    up_grad[:, pl.ds(at, CHUNK)] = dot(block_low[...], grad_pre[:, pl.ds(at, CHUNK)], 0, 0).astype(bf16)


def ffn_turn_kernel(
    resid_in, norm_in, up, down, norm_out, cotangent, valid,
    final_out, grad_out, up_grad, down_grad, norm_grad,
    active, grad_pre, slopes, grad_low, low,
):
    rows = resid_in.shape[0]
    norm_grad[...] = jnp.zeros(norm_grad.shape, f32)

    def one_block(step, carry):
        at = pl.multiple_of(step * TILE, TILE)
        span = pl.ds(at, TILE)
        normed, _ = normalise(resid_in[span, :])
        block = normed * norm_in[0:1, :] + norm_in[1:2, :]
        block_low = block.astype(bf16)
        low[span, :] = block_low
        for chunk in range(up.shape[1] // CHUNK):
            lanes = slice(chunk * CHUNK, (chunk + 1) * CHUNK)
            pre = dot(block_low, up[:, lanes])
            value, square, flat = gelu(pre)
            value = value.astype(bf16)
            slopes[:, lanes] = gelu_slope(pre, square, flat)
            active[span, lanes] = value
            block = block + dot(value, down[lanes, :])
        normed, scale_inv = normalise(block)
        final_out[span, :] = (normed * norm_out[0:1, :] + norm_out[1:2, :]).astype(bf16)
        grad = cotangent[span, :].astype(f32) * jnp.concatenate([valid[span, :]] * 4, axis=1)
        norm_grad[0:1, :] += jnp.sum(grad * normed, axis=0, keepdims=True)
        norm_grad[1:2, :] += jnp.sum(grad, axis=0, keepdims=True)
        grad = norm_back(grad, normed, scale_inv, norm_out[0:1, :])
        block_grad = grad.astype(bf16)
        grad_low[span, :] = block_grad
        for chunk in range(up.shape[1] // CHUNK):
            lanes = slice(chunk * CHUNK, (chunk + 1) * CHUNK)
            value = (dot(block_grad, down[lanes, :], 1, 1) * slopes[:, lanes]).astype(bf16)
            grad_pre[span, lanes] = value
            grad = grad + dot(value, up[:, lanes], 1, 1)
        grad_out[span, :] = grad
        return carry

    lax.fori_loop(0, rows // TILE, one_block, 0)

    def weights(step, carry):
        ffn_grads(step, active, grad_low, low, grad_pre, up_grad, down_grad)
        return carry

    lax.fori_loop(0, up.shape[1] // CHUNK, weights, 0)


def ffn_turn(resid, norm_in, up, down, norm_out, cotangent, valid):
    rows, width = resid.shape
    hidden = up.shape[1]
    shapes = [
        jax.ShapeDtypeStruct((rows, width), bf16),
        jax.ShapeDtypeStruct((rows, width), f32),
        jax.ShapeDtypeStruct(up.shape, bf16),
        jax.ShapeDtypeStruct(down.shape, bf16),
        jax.ShapeDtypeStruct((2, width), f32),
    ]
    return pl.pallas_call(
        ffn_turn_kernel,
        out_shape=shapes,
        in_specs=vmem(7),
        out_specs=vmem(5),
        scratch_shapes=[
            pltpu.VMEM((rows, hidden), bf16),
            pltpu.VMEM((rows, hidden), bf16),
            pltpu.VMEM((TILE, hidden), f32),
            pltpu.VMEM((rows, width), bf16),
            pltpu.VMEM((rows, width), bf16),
        ],
        compiler_params=pltpu.CompilerParams(vmem_limit_bytes=48 * 2**20),
        cost_estimate=cost(13e9, 18e6),
        name="ffn_turn",
    )(resid, norm_in, up, down, norm_out, cotangent, valid)


def ffn_backward_kernel(
    grad_in, resid_out, norm_out, resid_in, norm_in, up, down,
    grad_out, up_grad, down_grad, norm_grad,
    active, grad_pre, grad_low, low,
):
    rows = resid_in.shape[0]
    norm_grad[...] = jnp.zeros(norm_grad.shape, f32)

    def one_block(step, carry):
        at = pl.multiple_of(step * TILE, TILE)
        span = pl.ds(at, TILE)
        normed, _ = normalise(resid_in[span, :])
        block_low = (normed * norm_in[0:1, :] + norm_in[1:2, :]).astype(bf16)
        low[span, :] = block_low
        normed, scale_inv = normalise(resid_out[span, :])
        grad = grad_in[span, :]
        norm_grad[0:1, :] += jnp.sum(grad * normed, axis=0, keepdims=True)
        norm_grad[1:2, :] += jnp.sum(grad, axis=0, keepdims=True)
        grad = norm_back(grad, normed, scale_inv, norm_out[0:1, :])
        block_grad = grad.astype(bf16)
        grad_low[span, :] = block_grad
        for chunk in range(up.shape[1] // CHUNK):
            lanes = slice(chunk * CHUNK, (chunk + 1) * CHUNK)
            pre = dot(block_low, up[:, lanes])
            value, square, flat = gelu(pre)
            active[span, lanes] = value.astype(bf16)
            slope = gelu_slope(pre, square, flat)
            value = (dot(block_grad, down[lanes, :], 1, 1) * slope).astype(bf16)
            grad_pre[span, lanes] = value
            grad = grad + dot(value, up[:, lanes], 1, 1)
        grad_out[span, :] = grad
        return carry

    lax.fori_loop(0, rows // TILE, one_block, 0)

    def weights(step, carry):
        ffn_grads(step, active, grad_low, low, grad_pre, up_grad, down_grad)
        return carry

    lax.fori_loop(0, up.shape[1] // CHUNK, weights, 0)


def ffn_backward(grad, resid_out, norm_out, resid_in, norm_in, up, down):
    rows, width = resid_in.shape
    hidden = up.shape[1]
    shapes = [
        jax.ShapeDtypeStruct((rows, width), f32),
        jax.ShapeDtypeStruct(up.shape, bf16),
        jax.ShapeDtypeStruct(down.shape, bf16),
        jax.ShapeDtypeStruct((2, width), f32),
    ]
    return pl.pallas_call(
        ffn_backward_kernel,
        out_shape=shapes,
        in_specs=vmem(7),
        out_specs=vmem(4),
        scratch_shapes=[
            pltpu.VMEM((rows, hidden), bf16),
            pltpu.VMEM((rows, hidden), bf16),
            pltpu.VMEM((rows, width), bf16),
            pltpu.VMEM((rows, width), bf16),
        ],
        compiler_params=pltpu.CompilerParams(vmem_limit_bytes=48 * 2**20),
        cost_estimate=cost(11e9, 18e6),
        name="ffn_backward",
    )(grad, resid_out, norm_out, resid_in, norm_in, up, down)


AXES = ("wide", "narrow")


def exchange_phases(mesh):
    devices = list(mesh.devices.reshape(-1))
    count = len(devices)
    bits = [1 << place for place in range(count.bit_length() - 1)]
    spots = [tuple(getattr(device, "coords", None) or ()) for device in devices]
    core, along, across = [], [], []
    for bit in bits:
        moved = [i for i, (p, q) in enumerate(zip(spots[0], spots[bit])) if p != q]
        if spots[0] and not moved:
            core.append(bit)
        elif moved == [2]:
            along.append(bit)
        else:
            across.append(bit)
    phases = []
    for group in (along, across, core):
        phases += [group[i : i + 2] for i in range(0, len(group), 2)]
    return count, bits[::-1], phases


def masks_of(bits):
    masks = [0]
    for bit in bits:
        masks += [mask | bit for mask in masks]
    return masks


def swap(value, count, mask):
    return lax.ppermute(value, AXES, [(i, i ^ mask) for i in range(count)])


def gather_blocks(plan, shard, axis):
    count, order, phases = plan
    me = lax.axis_index(AXES)
    lead, tail = shard.shape[:axis], shard.shape[axis:]
    held = []
    value = shard
    for bits in phases:
        wider = [bit for bit in order if bit in held or bit in bits]
        shape = lead + (2,) * len(wider) + tail
        full = None
        for mask in masks_of(bits):
            piece = swap(value, count, mask) if mask else value
            piece = piece.reshape(lead + tuple(1 if bit in bits else 2 for bit in wider) + tail)
            spot = [0] * len(lead)
            for bit in wider:
                spot.append(jnp.where((me ^ mask) & bit != 0, 1, 0) if bit in bits else 0)
            spot += [0] * len(tail)
            if full is None:
                full = jnp.zeros(shape, shard.dtype)
            full = lax.dynamic_update_slice(full, piece, spot)
        value = full
        held = wider
    return value.reshape(lead + (count * tail[0],) + tail[1:])


def scatter_sums(plan, value, axis):
    count, order, phases = plan
    me = lax.axis_index(AXES)
    lead, tail = value.shape[:axis], value.shape[axis:]
    tail = (tail[0] // count,) + tail[1:]
    held = list(order)
    value = value.reshape(lead + (2,) * len(held) + tail)
    for bits in phases[::-1]:
        left = [bit for bit in held if bit not in bits]
        sizes = lead + tuple(1 if bit in bits else 2 for bit in held) + tail
        total = None
        for mask in masks_of(bits):
            spot = [0] * len(lead)
            for bit in held:
                spot.append(jnp.where((me ^ mask) & bit != 0, 1, 0) if bit in bits else 0)
            spot += [0] * len(tail)
            piece = lax.dynamic_slice(value, spot, sizes).reshape(lead + (2,) * len(left) + tail)
            piece = (swap(piece, count, mask) if mask else piece).astype(f32)
            total = piece if total is None else total + piece
        held = left
        value = total.astype(bf16) if held else total
    return value


def gather_offloaded(shards):
    count = lax.axis_size(AXES)
    flat = [jnp.reshape(item, (-1, 512)) for item in shards]
    whole = lax.all_gather(jnp.concatenate(flat), AXES, axis=0, tiled=False)
    parts = []
    start = 0
    for item, piece in zip(shards, flat):
        stop = start + piece.shape[0]
        block = whole[:, start:stop]
        start = stop
        if item.ndim == 3:
            block = block.reshape(count, item.shape[0], -1, item.shape[2])
            block = jnp.moveaxis(block, 0, 1)
            parts.append(block.reshape(item.shape[0], -1, item.shape[2]))
        else:
            parts.append(block.reshape(-1, item.shape[1]))
    return parts


def scatter_offloaded(grads):
    count = lax.axis_size(AXES)
    flat = []
    for grad in grads:
        if grad.ndim == 3:
            block = grad.reshape(grad.shape[0], count, -1, grad.shape[2])
            block = jnp.moveaxis(block, 1, 0)
        else:
            block = grad
        flat.append(block.reshape(count, -1, 512))
    whole = jnp.concatenate(flat, axis=1)
    whole = lax.psum_scatter(whole, "wide", scatter_dimension=0, tiled=True)
    whole = lax.psum_scatter(whole, "narrow", scatter_dimension=0, tiled=True)[0].astype(f32)
    parts = []
    start = 0
    for grad, block in zip(grads, flat):
        stop = start + block.shape[1]
        if grad.ndim == 3:
            parts.append(whole[start:stop].reshape(grad.shape[0], -1, grad.shape[2]))
        else:
            parts.append(whole[start:stop].reshape(-1, grad.shape[1]))
        start = stop
    return parts


def on_device(
    plan,
    source,
    target,
    source_segments,
    target_segments,
    encoder_proj,
    encoder_mix,
    encoder_up,
    encoder_down,
    self_proj,
    self_mix,
    cross_proj,
    cross_mix,
    decoder_up,
    decoder_down,
    norm_gain,
    norm_bias,
    cotangent,
):
    width = source.shape[-1]
    source_low = source.reshape(-1, width)
    target_low = target.reshape(-1, width)
    enc_mix = gather_blocks(plan, encoder_mix, 0)
    enc_proj = gather_blocks(plan, encoder_proj, 1)
    shard = jnp.stack([norm_gain, norm_bias], axis=1)
    norms = gather_blocks(plan, shard.reshape(1, -1), 0).reshape(-1, 5, 2, norm_gain.shape[1])
    norms = jnp.moveaxis(norms, 0, 2).reshape(5, 2, width).astype(f32)
    own_proj = gather_blocks(plan, self_proj, 1)
    own_mix = gather_blocks(plan, self_mix, 0)
    enc_up = gather_blocks(plan, encoder_up, 0)
    enc_down = gather_blocks(plan, encoder_down, 0)
    far_proj, far_mix, dec_up, dec_down = gather_offloaded(
        [cross_proj, cross_mix, decoder_up, decoder_down]
    )

    source_cols = key_columns(source_segments)
    target_cols = key_columns(target_segments)
    source_rows = source_segments.reshape(-1, 1, BLOCK)
    target_rows = target_segments.reshape(-1, 1, BLOCK)
    enc_ranges = key_ranges(source_segments, source_segments, False)
    own_ranges = key_ranges(target_segments, target_segments, True)
    far_ranges = key_ranges(target_segments, source_segments, False)

    enc_one, _, *enc_saved = attend_forward(
        source_low, None, None, source_cols, source_rows, enc_ranges, (enc_proj, enc_mix), norms[0], False
    )
    own_sum, _, *own_saved = attend_forward(
        target_low, None, None, target_cols, target_rows, own_ranges, (own_proj, own_mix), norms[2], True
    )
    enc_two, enc_low = ffn_forward(enc_one, norms[0], enc_up, enc_down, norms[1])
    far_sum, second_low, *far_saved = attend_forward(
        own_sum, norms[2], enc_low, source_cols, target_rows, far_ranges, (far_proj, far_mix), norms[3], False
    )
    valid = jnp.broadcast_to((target_segments >= 0).reshape(-1, 1).astype(f32), (target_low.shape[0], 128))
    final, grad, dec_up_grad, dec_down_grad, norm_four = ffn_turn(
        far_sum, norms[3], dec_up, dec_down, norms[4], cotangent.reshape(-1, width), valid
    )
    grad, grad_enc, far_grad, norm_three = attend_backward(
        grad, far_sum, norms[3], second_low, enc_low, far_saved, source_cols, target_rows, far_ranges,
        (far_proj, far_mix), False, f32
    )
    far_out, dec_up_out, dec_down_out = scatter_offloaded([far_grad, dec_up_grad, dec_down_grad])
    grad_enc, enc_up_grad, enc_down_grad, norm_one = ffn_backward(
        grad_enc, enc_two, norms[1], enc_one, norms[0], enc_up, enc_down
    )
    enc_up_out = scatter_sums(plan, enc_up_grad, 0)
    enc_down_out = scatter_sums(plan, enc_down_grad, 0)
    target_grad, own_grad, norm_two = attend_backward(
        grad, own_sum, norms[2], target_low, None, own_saved, target_cols, target_rows, own_ranges,
        (own_proj, own_mix), True, bf16
    )
    own_out = scatter_sums(plan, own_grad, 1)
    source_grad, enc_grad, norm_zero = attend_backward(
        grad_enc, enc_one, norms[0], source_low, None, enc_saved, source_cols, source_rows, enc_ranges,
        (enc_proj, enc_mix), False, bf16
    )
    enc_out = scatter_sums(plan, enc_grad, 1)
    norm_grad = jnp.stack([norm_zero, norm_one, norm_two, norm_three, norm_four])
    norm_grad = jnp.moveaxis(norm_grad.reshape(5, 2, -1, norm_gain.shape[1]), 2, 0)
    norm_grad = norm_grad.reshape(norm_grad.shape[0], -1).astype(bf16)
    norm_out = scatter_sums(plan, norm_grad, 0).reshape(5, 2, -1)
    return (
        final.reshape(target.shape),
        source_grad.reshape(source.shape),
        target_grad.reshape(target.shape),
        enc_out[:3],
        enc_out[3],
        enc_up_out,
        enc_down_out,
        own_out[:3],
        own_out[3],
        far_out[:3],
        far_out[3],
        dec_up_out,
        dec_down_out,
        norm_out[:, 0],
        norm_out[:, 1],
    )


def solution(mesh):
    return jax.shard_map(
        partial(on_device, exchange_phases(mesh)),
        mesh=mesh,
        in_specs=(
            P(("wide", "narrow"), None, None),
            P(("wide", "narrow"), None, None),
            P(("wide", "narrow"), None),
            P(("wide", "narrow"), None),
            P(None, ("wide", "narrow"), None),
            P(("wide", "narrow"), None),
            P(("wide", "narrow"), None),
            P(("wide", "narrow"), None),
            P(None, ("wide", "narrow"), None),
            P(("wide", "narrow"), None),
            P(None, ("wide", "narrow"), None),
            P(("wide", "narrow"), None),
            P(("wide", "narrow"), None),
            P(("wide", "narrow"), None),
            P(None, ("wide", "narrow")),
            P(None, ("wide", "narrow")),
            P(("wide", "narrow"), None, None),
        ),
        out_specs=(
            P(("wide", "narrow"), None, None),
            P(("wide", "narrow"), None, None),
            P(("wide", "narrow"), None, None),
            P(None, ("wide", "narrow"), None),
            P(("wide", "narrow"), None),
            P(("wide", "narrow"), None),
            P(("wide", "narrow"), None),
            P(None, ("wide", "narrow"), None),
            P(("wide", "narrow"), None),
            P(None, ("wide", "narrow"), None),
            P(("wide", "narrow"), None),
            P(("wide", "narrow"), None),
            P(("wide", "narrow"), None),
            P(None, ("wide", "narrow")),
            P(None, ("wide", "narrow")),
        ),
        check_vma=False,
    )
```

```python
from functools import partial

import jax
import jax.numpy as jnp
from jax import lax
from jax.experimental import pallas as pl
from jax.experimental.pallas import tpu as pltpu
from jax.sharding import PartitionSpec as P

HEADS = 8
norm_eps = 1e-05
masked_score = -1e30
lowest = -3e38
log2_e = 1.4426950408889634
BLOCK = 128
TILE = 256
VMEM_LIMIT = 60 * 2**20
f32 = jnp.float32
bf16 = jnp.bfloat16


def dot(left, right, left_dim=1, right_dim=0):
    dims = (((left_dim,), (right_dim,)), ((), ()))
    return lax.dot_general(left, right, dims, preferred_element_type=f32)


def normalise(resid):
    mean = jnp.mean(resid, axis=-1, keepdims=True)
    centred = resid - mean
    scale_inv = lax.rsqrt(jnp.mean(centred * centred, axis=-1, keepdims=True) + norm_eps)
    return centred * scale_inv, scale_inv


def norm_back(grad, normed, scale_inv, gain):
    scaled = grad * gain
    mean_plain = jnp.mean(scaled, axis=-1, keepdims=True)
    mean_normed = jnp.mean(scaled * normed, axis=-1, keepdims=True)
    return scale_inv * (scaled - mean_plain - normed * mean_normed)


def key_ranges(query_segments, key_segments, causal):
    big = jnp.int32(1 << 30)
    query_order = jnp.where(query_segments < 0, big, query_segments).reshape(-1, BLOCK)
    key_order = jnp.where(key_segments < 0, big, key_segments).reshape(1, -1)
    first = jnp.sum((key_order < query_order[:, :1]).astype(jnp.int32), axis=1)
    stop = jnp.sum((key_order <= query_order[:, -1:]).astype(jnp.int32), axis=1)
    real = jnp.sum((key_order < big).astype(jnp.int32))
    if causal:
        stop = jnp.minimum(stop, (jnp.arange(stop.shape[0]) + 1) * BLOCK)
    start = first // 16 * 16
    tiles = (stop - start + TILE - 1) // TILE
    real_tiles = jnp.maximum((jnp.minimum(stop, real) - start + TILE - 1) // TILE, 0)
    real_tiles = jnp.where(first >= real, 0, real_tiles)
    return jnp.stack([start, tiles, real_tiles]).astype(jnp.int32)


def key_columns(key_segments):
    flat = jnp.pad(key_segments.reshape(-1), (0, TILE), constant_values=-2)
    return jnp.broadcast_to(flat[:, None], (flat.shape[0], 128))


def head_pair_mask():
    lane = lax.broadcasted_iota(jnp.int32, (1, 128), 1)
    return lane < 64


def stack_heads(block, even):
    zero = jnp.zeros_like(block)
    return jnp.concatenate([jnp.where(even, block, zero), jnp.where(even, zero, block)], axis=0)


def tile_bias(bias_ref, key_col_ref, query_row, key_start, query_start, causal):
    allowed = key_col_ref[pl.ds(key_start, TILE), :] == query_row
    if causal:
        key_place = key_start + lax.broadcasted_iota(jnp.int32, (TILE, BLOCK), 0)
        query_place = query_start + lax.broadcasted_iota(jnp.int32, (TILE, BLOCK), 1)
        allowed = allowed & (key_place <= query_place)
    bias_ref[...] = jnp.where(allowed, 0.0, masked_score).astype(f32)


HBM = pl.BlockSpec(memory_space=pltpu.HBM)
VMEM = pl.BlockSpec(memory_space=pltpu.VMEM)
SMEM = pl.BlockSpec(memory_space=pltpu.SMEM)


class Sems:
    def __init__(self, ref):
        self.ref = ref
        self.used = 0

    def take(self, number=1):
        self.used += number
        return self.used - number

    def copy(self, src, dst, place):
        return pltpu.make_async_copy(src, dst, self.ref.at[place])


def span_of(step):
    return pl.ds(step * TILE if isinstance(step, int) else pl.multiple_of(step * TILE, TILE), TILE)


def by_rows(sems, src, dst, steps):
    first = sems.take(steps)
    return lambda step: sems.copy(src.at[span_of(step)], dst.at[span_of(step)], first + step)


def by_columns(sems, src, dst, steps):
    first = sems.take(steps)
    return lambda step: sems.copy(src.at[:, span_of(step)], dst.at[:, span_of(step)], first + step)


def whole(sems, src, dst):
    place = sems.take()
    return lambda: sems.copy(src, dst, place)


def weight_copies(sems, parts, base, start, size, dst, core):
    span = pl.ds(start, size)
    if len(parts) == 1:
        return [whole(sems, parts[0].at[pl.ds(base + start, size)], dst.at[span])]
    return [
        whole(sems, parts[0].at[span], dst.at[span, :, core]),
        whole(sems, parts[1].at[span], dst.at[span, :, 1 - core]),
    ]


def start_all(*copies):
    for copy in copies:
        copy().start()


def wait_all(*copies):
    for copy in copies:
        copy().wait()


def matrix(blocks, index):
    block = blocks[index]
    return block.reshape(block.shape[0] * block.shape[1] * block.shape[2], block.shape[3])


def put_grad(halves, index, value, core):
    value = value.astype(bf16)
    high, low = halves.shape[2:4]
    for major in range(high):
        for side in range(2):
            at = (2 * major + side) * low
            halves[core if side == 0 else 1 - core, index, major] = value[at : at + low]


def forward_kernel(causal, fresh, base, parts, *refs):
    refs = list(refs)
    take = lambda number: [refs.pop(0) for _ in range(number)]
    core_ref, ranges, own_hbm = take(3)
    norm_own, other_hbm = (None, own_hbm) if fresh else take(2)
    key_hbm, query_seg = take(2)
    weights = take(parts)
    (resid_hbm,) = take(1)
    (low_hbm,) = (None,) if fresh else take(1)
    q_hbm, k_hbm, v_hbm, o_hbm, lse_out = take(5)
    w, own, key_col, resid_out, q_out, k_out, v_out, o_out, stacked, bias, acc, peak, total, ref = take(14)
    other, low_out = (own, None) if fresh else take(2)
    sems = Sems(ref)
    core = core_ref[0]
    rows = own.shape[0]
    steps = rows // TILE
    even = head_pair_mask()
    scale = 0.125 * log2_e
    proj_in = weight_copies(sems, weights, base, 0, 3, w, core)
    own_in = by_rows(sems, own_hbm, own, steps)
    other_in = None if fresh else by_rows(sems, other_hbm, other, steps)
    mix_in = weight_copies(sems, weights, base, 3, 1, w, core)
    key_in = whole(sems, key_hbm, key_col)
    start_all(*proj_in)
    for step in range(steps):
        own_in(step).start()
        if not fresh:
            other_in(step).start()
    start_all(key_in, *mix_in)
    q_to = by_rows(sems, q_out, q_hbm, steps)
    k_to = whole(sems, k_out, k_hbm)
    v_to = whole(sems, v_out, v_hbm)
    o_to = by_columns(sems, o_out, o_hbm, steps)
    resid_to = by_rows(sems, resid_out, resid_hbm, steps)
    low_to = None if fresh else by_rows(sems, low_out, low_hbm, steps)
    wait_all(*proj_in)

    def fill(step, carry):
        span = span_of(step)
        own_in(step).wait()
        block = own[span, :]
        if fresh:
            block_low = block
            key_block = block
        else:
            other_in(step).wait()
            normed, _ = normalise(block)
            block_low = (normed * norm_own[0:1, :] + norm_own[1:2, :]).astype(bf16)
            low_out[span, :] = block_low
            low_to(step).start()
            key_block = other[span, :]
        query = dot(block_low, matrix(w, 0)).astype(bf16)
        q_out[span, :] = query
        q_to(step).start()
        for sub in range(TILE // BLOCK):
            for pair in range(4):
                part = query[sub * BLOCK : (sub + 1) * BLOCK, pair * 128 : (pair + 1) * 128]
                stacked[step * (TILE // BLOCK) + sub, pair] = stack_heads(part, even)
        k_out[span, :] = dot(key_block, matrix(w, 1)).astype(bf16)
        v_out[span, :] = dot(key_block, matrix(w, 2)).astype(bf16)
        return carry

    lax.fori_loop(0, steps, fill, 0)
    k_out[rows:, :] = jnp.zeros((TILE, k_out.shape[1]), bf16)
    v_out[rows:, :] = jnp.zeros((TILE, v_out.shape[1]), bf16)
    start_all(k_to, v_to)
    wait_all(key_in)

    def one_block(index, carry):
        start = ranges[0, index]
        tiles = ranges[1, index]
        query_start = pl.multiple_of(index * BLOCK, BLOCK)
        query_row = query_seg[index]
        peak[...] = jnp.full(peak.shape, lowest, f32)
        total[...] = jnp.zeros(total.shape, f32)
        acc[...] = jnp.zeros(acc.shape, f32)

        def one_tile(tile, inner):
            at = pl.multiple_of(start + tile * TILE, 16)
            tile_bias(bias, key_col, query_row, at, query_start, causal)
            for pair in range(4):
                lanes = slice(pair * 128, (pair + 1) * 128)
                scores = dot(k_out[pl.ds(at, TILE), lanes], stacked[index, pair], 1, 1)
                blocked = bias[...]
                scores = scores * scale + jnp.concatenate([blocked, blocked], axis=1)
                before = peak[pair : pair + 1, :]
                above = jnp.maximum(before, jnp.max(scores, axis=0, keepdims=True))
                probs = jnp.exp2(scores - above)
                shrink = jnp.exp2(before - above)
                peak[pair : pair + 1, :] = above
                total[pair : pair + 1, :] = total[pair : pair + 1, :] * shrink + jnp.sum(
                    probs, axis=0, keepdims=True
                )
                mixed = dot(v_out[pl.ds(at, TILE), lanes], probs.astype(bf16), 0, 0)
                top = pair * 128
                acc[top : top + 64, :] = acc[top : top + 64, :] * shrink[:, :128] + mixed[:64, :128]
                acc[top + 64 : top + 128, :] = (
                    acc[top + 64 : top + 128, :] * shrink[:, 128:] + mixed[64:, 128:]
                )
            return inner

        lax.fori_loop(0, tiles, one_tile, 0)
        for pair in range(4):
            inverse = 1.0 / total[pair : pair + 1, :]
            top = pair * 128
            o_out[top : top + 64, pl.ds(query_start, BLOCK)] = (
                acc[top : top + 64, :] * inverse[:, :128]
            ).astype(bf16)
            o_out[top + 64 : top + 128, pl.ds(query_start, BLOCK)] = (
                acc[top + 64 : top + 128, :] * inverse[:, 128:]
            ).astype(bf16)
        lse_out[index] = peak[...] + jnp.log2(total[...])
        return carry

    lax.fori_loop(0, rows // BLOCK, one_block, 0)
    wait_all(*mix_in)

    def finish(step, carry):
        span = span_of(step)
        o_to(step).start()
        block = own[span, :]
        if fresh:
            block = block.astype(f32)
        else:
            normed, _ = normalise(block)
            block = normed * norm_own[0:1, :] + norm_own[1:2, :]
        resid_out[span, :] = block + dot(o_out[:, span], matrix(w, 3), 0, 0)
        resid_to(step).start()
        return carry

    lax.fori_loop(0, steps, finish, 0)
    wait_all(k_to, v_to)
    for step in range(steps):
        q_to(step).wait()
        o_to(step).wait()
        if not fresh:
            low_to(step).wait()
        resid_to(step).wait()


def cost(flops, moved):
    return pl.CostEstimate(flops=int(flops), bytes_accessed=int(moved), transcendentals=0)


def array(shape, dtype):
    return jax.ShapeDtypeStruct(shape, dtype)


def attend_forward(core, own, norm_own, other, key_col, query_seg, ranges, weights, base, causal):
    fresh = norm_own is None
    rows, width = own.shape
    blocks = rows // BLOCK
    high, low = layout_of(weights)
    ins = [own] if fresh else [own, norm_own, other]
    specs = [HBM] if fresh else [HBM, VMEM, HBM]
    ins += [key_col, query_seg, *weights]
    specs += [HBM, VMEM] + [HBM] * len(weights)
    shapes = [array((rows, width), f32)]
    if not fresh:
        shapes.append(array((rows, width), bf16))
    shapes += [
        array((rows, width), bf16),
        array((rows + TILE, width), bf16),
        array((rows + TILE, width), bf16),
        array((width, rows), bf16),
        array((blocks, 4, 2 * BLOCK), f32),
    ]
    scratch = [
        pltpu.VMEM((4, high, 2, low, width), bf16),
        pltpu.VMEM((rows, width), own.dtype),
        pltpu.VMEM((rows + TILE, 128), jnp.int32),
        pltpu.VMEM((rows, width), f32),
        pltpu.VMEM((rows, width), bf16),
        pltpu.VMEM((rows + TILE, width), bf16),
        pltpu.VMEM((rows + TILE, width), bf16),
        pltpu.VMEM((width, rows), bf16),
        pltpu.VMEM((blocks, 4, 2 * BLOCK, 128), bf16),
        pltpu.VMEM((TILE, BLOCK), f32),
        pltpu.VMEM((width, BLOCK), f32),
        pltpu.VMEM((4, 2 * BLOCK), f32),
        pltpu.VMEM((4, 2 * BLOCK), f32),
        pltpu.SemaphoreType.DMA((48,)),
    ]
    if not fresh:
        scratch += [pltpu.VMEM((rows, width), bf16)] * 2
    return pl.pallas_call(
        partial(forward_kernel, causal, fresh, base, len(weights)),
        out_shape=shapes,
        in_specs=[SMEM, SMEM] + specs,
        out_specs=[HBM] * (len(shapes) - 1) + [VMEM],
        scratch_shapes=scratch,
        compiler_params=pltpu.CompilerParams(vmem_limit_bytes=VMEM_LIMIT),
        cost_estimate=cost(20e9, 12e6),
        name="attend_forward",
    )(core, ranges, *ins)


def layout_of(weights):
    shape = weights[0].shape
    return (shape[1], shape[2]) if len(weights) == 2 else (shape[1], shape[3])


def backward_kernel(causal, same, base, parts, *refs):
    refs = list(refs)
    take = lambda number: [refs.pop(0) for _ in range(number)]
    core_ref, ranges, grad_hbm, resid_hbm, norm, own_hbm = take(6)
    other_hbm = None if same else take(1)[0]
    q_hbm, k_hbm, v_hbm, o_hbm, lse, key_hbm, query_seg = take(7)
    weights = take(parts)
    (own_grad_hbm,) = take(1)
    other_grad_hbm = None if same else take(1)[0]
    keep_hbm, send_hbm, norm_grad = take(3)
    (w, grad, resid, own, q_in, k_in, v_in, o_in, key_col, sums, own_grad, halves,
     low, stacked, grad_stacked, inner_rows, bias, acc, dq, dk, dv, ref) = take(22)
    other, other_grad = (own, None) if same else take(2)
    sems = Sems(ref)
    core = core_ref[0]
    rows = own.shape[0]
    steps = rows // TILE
    even = head_pair_mask()
    scale = 0.125 * log2_e

    mix_in = weight_copies(sems, weights, base, 3, 1, w, core)
    grad_in = by_rows(sems, grad_hbm, grad, steps)
    resid_in = by_rows(sems, resid_hbm, resid, steps)
    o_from = by_columns(sems, o_hbm, o_in, steps)
    q_from = by_rows(sems, q_hbm, q_in, steps)
    later = [whole(sems, key_hbm, key_col), whole(sems, k_hbm, k_in), whole(sems, v_hbm, v_in)]
    last = [whole(sems, own_hbm, own)] + weight_copies(sems, weights, base, 0, 3, w, core)
    if not same:
        last.append(whole(sems, other_hbm, other))
    start_all(*mix_in)
    for step in range(steps):
        for chunked in (grad_in, resid_in, o_from, q_from):
            chunked(step).start()
    start_all(*later, *last)
    keep_to = [whole(sems, halves.at[0, index], keep_hbm.at[index]) for index in range(4)]
    send_to = [whole(sems, halves.at[1, index], send_hbm.at[index]) for index in range(4)]
    own_to = by_rows(sems, own_grad, own_grad_hbm, steps)
    other_to = None if same else by_rows(sems, other_grad, other_grad_hbm, steps)

    norm_grad[...] = jnp.zeros(norm_grad.shape, f32)
    dk[...] = jnp.zeros(dk.shape, f32)
    dv[...] = jnp.zeros(dv.shape, f32)
    wait_all(*mix_in)

    def prepare(step, carry):
        span = span_of(step)
        for chunked in (grad_in, resid_in, o_from, q_from):
            chunked(step).wait()
        block = grad[span, :]
        normed, scale_inv = normalise(resid[span, :])
        norm_grad[0:1, :] += jnp.sum(block * normed, axis=0, keepdims=True)
        norm_grad[1:2, :] += jnp.sum(block, axis=0, keepdims=True)
        block = norm_back(block, normed, scale_inv, norm[0:1, :])
        sums[span, :] = block
        block = block.astype(bf16)
        low[span, :] = block
        grad_mixed = dot(block, matrix(w, 3), 1, 1).astype(bf16)
        flipped = dot(matrix(w, 3), block, 1, 1).astype(bf16).astype(f32)
        flipped = flipped * o_in[:, span].astype(f32)
        inner = [jnp.sum(flipped[head * 64 : (head + 1) * 64, :], axis=0, keepdims=True) for head in range(HEADS)]
        query = q_in[span, :]
        for sub in range(TILE // BLOCK):
            spot = step * (TILE // BLOCK) + sub
            part = slice(sub * BLOCK, (sub + 1) * BLOCK)
            rows_of = []
            for pair in range(4):
                lanes = slice(pair * 128, (pair + 1) * 128)
                stacked[spot, pair] = stack_heads(query[part, lanes], even)
                grad_stacked[spot, pair] = stack_heads(grad_mixed[part, lanes], even)
                rows_of.append(jnp.concatenate([inner[2 * pair][:, part], inner[2 * pair + 1][:, part]], axis=1))
            inner_rows[spot] = jnp.concatenate(rows_of, axis=0)
        return carry

    lax.fori_loop(0, steps, prepare, 0)
    put_grad(halves, 3, dot(o_in[...], low[...]), core)
    start_all(keep_to[3], send_to[3])
    wait_all(*later)

    def one_block(index, carry):
        start = ranges[0, index]
        tiles = ranges[2, index]
        query_start = pl.multiple_of(index * BLOCK, BLOCK)
        query_row = query_seg[index]
        acc[...] = jnp.zeros(acc.shape, f32)

        def one_tile(tile, inner):
            at = pl.multiple_of(start + tile * TILE, 16)
            tile_bias(bias, key_col, query_row, at, query_start, causal)
            for pair in range(4):
                lanes = slice(pair * 128, (pair + 1) * 128)
                key = k_in[pl.ds(at, TILE), lanes]
                query = stacked[index, pair]
                grad_out = grad_stacked[index, pair]
                scores = dot(key, query, 1, 1)
                blocked = bias[...]
                scores = scores * scale + jnp.concatenate([blocked, blocked], axis=1)
                probs = jnp.exp2(scores - lse[index, pair : pair + 1, :])
                grad_probs = dot(v_in[pl.ds(at, TILE), lanes], grad_out, 1, 1)
                grad_scores = (probs * (grad_probs - inner_rows[index, pair : pair + 1, :])).astype(bf16)
                dv[pl.ds(at, TILE), lanes] += dot(probs.astype(bf16), grad_out)
                dk[pl.ds(at, TILE), lanes] += dot(grad_scores, query)
                mixed = dot(key, grad_scores, 0, 0)
                top = pair * 128
                acc[top : top + 64, :] += mixed[:64, :128]
                acc[top + 64 : top + 128, :] += mixed[64:, 128:]
            return inner

        lax.fori_loop(0, tiles, one_tile, 0)
        dq[pl.ds(query_start, BLOCK), :] = (acc[...].T * 0.125).astype(bf16)
        return carry

    lax.fori_loop(0, rows // BLOCK, one_block, 0)
    low[...] = (dk[:rows, :] * 0.125).astype(bf16)
    q_in[...] = dv[:rows, :].astype(bf16)
    wait_all(*last)
    for index, (left, right) in enumerate(((own, dq), (other, low), (other, q_in))):
        put_grad(halves, index, dot(left[...], right[...], 0, 0), core)
        start_all(keep_to[index], send_to[index])

    def finish(step, carry):
        span = span_of(step)
        query_side = sums[span, :] + dot(dq[span, :], matrix(w, 0), 1, 1)
        source_side = dot(low[span, :], matrix(w, 1), 1, 1) + dot(q_in[span, :], matrix(w, 2), 1, 1)
        if same:
            own_grad[span, :] = (query_side + source_side).astype(own_grad.dtype)
        else:
            own_grad[span, :] = query_side
            other_grad[span, :] = source_side
            other_to(step).start()
        own_to(step).start()
        return carry

    lax.fori_loop(0, steps, finish, 0)
    wait_all(*keep_to, *send_to)
    for step in range(steps):
        own_to(step).wait()
        if not same:
            other_to(step).wait()


def attend_backward(
    core, grad, resid, norm, own, other, saved, key_col, query_seg, ranges, weights, base, causal, out_dtype, extra=0
):
    same = other is None
    rows, width = own.shape
    blocks = rows // BLOCK
    high, low = layout_of(weights)
    q, k, v, o, lse = saved
    ins = [grad, resid, norm, own] + ([] if same else [other])
    specs = [HBM, HBM, VMEM, HBM] + ([] if same else [HBM])
    ins += [q, k, v, o, lse, key_col, query_seg, *weights]
    specs += [HBM] * 4 + [VMEM, HBM, VMEM] + [HBM] * len(weights)
    shapes = [array((rows, width), out_dtype)]
    if not same:
        shapes.append(array((rows, width), f32))
    shapes += [array((4 + extra, high, low, width), bf16)] * 2
    shapes.append(array((2, width), f32))
    scratch = [
        pltpu.VMEM((4, high, 2, low, width), bf16),
        pltpu.VMEM((rows, width), f32),
        pltpu.VMEM((rows, width), f32),
        pltpu.VMEM((rows, width), bf16),
        pltpu.VMEM((rows, width), bf16),
        pltpu.VMEM((rows + TILE, width), bf16),
        pltpu.VMEM((rows + TILE, width), bf16),
        pltpu.VMEM((width, rows), bf16),
        pltpu.VMEM((rows + TILE, 128), jnp.int32),
        pltpu.VMEM((rows, width), f32),
        pltpu.VMEM((rows, width), out_dtype),
        pltpu.VMEM((2, 4, high, low, width), bf16),
        pltpu.VMEM((rows, width), bf16),
        pltpu.VMEM((blocks, 4, 2 * BLOCK, 128), bf16),
        pltpu.VMEM((blocks, 4, 2 * BLOCK, 128), bf16),
        pltpu.VMEM((blocks, 4, 2 * BLOCK), f32),
        pltpu.VMEM((TILE, BLOCK), f32),
        pltpu.VMEM((width, BLOCK), f32),
        pltpu.VMEM((rows, width), bf16),
        pltpu.VMEM((rows + TILE, width), f32),
        pltpu.VMEM((rows + TILE, width), f32),
        pltpu.SemaphoreType.DMA((64,)),
    ]
    if not same:
        scratch += [pltpu.VMEM((rows, width), bf16), pltpu.VMEM((rows, width), f32)]
    return pl.pallas_call(
        partial(backward_kernel, causal, same, base, len(weights)),
        out_shape=shapes,
        in_specs=[SMEM, SMEM] + specs,
        out_specs=[HBM] * (len(shapes) - 1) + [VMEM],
        scratch_shapes=scratch,
        compiler_params=pltpu.CompilerParams(vmem_limit_bytes=VMEM_LIMIT),
        cost_estimate=cost(25e9, 20e6),
        name="attend_backward",
    )(core, ranges, *ins)


root_two_pi = 0.7978845608028654


def gelu(pre):
    square = pre * pre
    flat = jnp.tanh(pre * (root_two_pi + (root_two_pi * 0.044715) * square))
    return pre * (0.5 + 0.5 * flat), square, flat


def gelu_slope(pre, square, flat):
    half = 0.5 + 0.5 * flat
    inner = (0.5 * root_two_pi) + (1.5 * root_two_pi * 0.044715) * square
    return half + pre * ((1.0 - flat * flat) * inner)


def ffn_forward_kernel(base, parts, *refs):
    refs = list(refs)
    take = lambda number: [refs.pop(0) for _ in range(number)]
    core_ref, resid_hbm, norm_in, norm_out = take(4)
    weights = take(parts)
    resid_to_hbm, low_hbm, w, resid_in, resid_out, low_out, ref = take(7)
    sems = Sems(ref)
    core = core_ref[0]
    steps = resid_in.shape[0] // TILE
    up_in = weight_copies(sems, weights, base, 0, 4, w, core)
    down_in = weight_copies(sems, weights, base, 4, 4, w, core)
    resid_from = by_rows(sems, resid_hbm, resid_in, steps)
    resid_to = by_rows(sems, resid_out, resid_to_hbm, steps)
    low_to = by_rows(sems, low_out, low_hbm, steps)
    resid_from(0).start()
    start_all(*up_in, *down_in)
    for step in range(1, steps):
        resid_from(step).start()
    wait_all(*up_in, *down_in)

    def one_block(step, carry):
        span = span_of(step)
        resid_from(step).wait()
        normed, _ = normalise(resid_in[span, :])
        block = normed * norm_in[0:1, :] + norm_in[1:2, :]
        block_low = block.astype(bf16)
        for chunk in range(4):
            active, _, _ = gelu(dot(block_low, matrix(w, chunk)))
            block = block + dot(active.astype(bf16), matrix(w, 4 + chunk))
        resid_out[span, :] = block
        resid_to(step).start()
        normed, _ = normalise(block)
        low_out[span, :] = (normed * norm_out[0:1, :] + norm_out[1:2, :]).astype(bf16)
        low_to(step).start()
        return carry

    lax.fori_loop(0, steps, one_block, 0)
    for step in range(steps):
        resid_to(step).wait()
        low_to(step).wait()


def ffn_forward(core, resid, norm_in, norm_out, weights, base):
    rows, width = resid.shape
    high, low = layout_of(weights)
    return pl.pallas_call(
        partial(ffn_forward_kernel, base, len(weights)),
        out_shape=[array((rows, width), f32), array((rows, width), bf16)],
        in_specs=[SMEM, HBM, VMEM, VMEM] + [HBM] * len(weights),
        out_specs=[HBM, HBM],
        scratch_shapes=[
            pltpu.VMEM((8, high, 2, low, width), bf16),
            pltpu.VMEM((rows, width), f32),
            pltpu.VMEM((rows, width), f32),
            pltpu.VMEM((rows, width), bf16),
            pltpu.SemaphoreType.DMA((24,)),
        ],
        compiler_params=pltpu.CompilerParams(vmem_limit_bytes=VMEM_LIMIT),
        cost_estimate=cost(9e9, 9e6),
        name="ffn_forward",
    )(core, resid, norm_in, norm_out, *weights)


def ffn_grads(steps, active, grad_low, block_low, grad_pre, halves, keep_hbm, send_hbm, sems, core):
    first = sems.take(16)

    def out(index, side):
        target = send_hbm if side else keep_hbm
        return sems.copy(halves.at[side, index], target.at[index], first + 2 * index + side)

    def weight_part(chunk, carry):
        put_grad(halves, chunk, dot(block_low[...], grad_pre[chunk], 0, 0), core)
        out(chunk, 0).start()
        out(chunk, 1).start()
        put_grad(halves, 4 + chunk, dot(active[chunk], grad_low[...], 0, 0), core)
        out(4 + chunk, 0).start()
        out(4 + chunk, 1).start()
        return carry

    lax.fori_loop(0, 4, weight_part, 0)
    for index in range(8):
        out(index, 0).wait()
        out(index, 1).wait()


def ffn_turn_kernel(base, parts, *refs):
    refs = list(refs)
    take = lambda number: [refs.pop(0) for _ in range(number)]
    core_ref, resid_hbm, norm_in, norm_out, cotangent_hbm, valid_hbm = take(6)
    weights = take(parts)
    final_hbm, grad_hbm, keep_hbm, send_hbm, norm_grad = take(5)
    (w, resid_in, cotangent, valid, final_out, grad_out, halves,
     active, grad_pre, slopes, grad_low, low, ref) = take(13)
    sems = Sems(ref)
    core = core_ref[0]
    steps = resid_in.shape[0] // TILE
    up_in = weight_copies(sems, weights, base, 0, 4, w, core)
    down_in = weight_copies(sems, weights, base, 4, 4, w, core)
    inputs = [
        by_rows(sems, resid_hbm, resid_in, steps),
        by_rows(sems, cotangent_hbm, cotangent, steps),
        by_rows(sems, valid_hbm, valid, steps),
    ]
    final_to = by_rows(sems, final_out, final_hbm, steps)
    grad_to = by_rows(sems, grad_out, grad_hbm, steps)
    for step in range(steps):
        if step == 1:
            start_all(*up_in, *down_in)
        for chunked in inputs:
            chunked(step).start()
    norm_grad[...] = jnp.zeros(norm_grad.shape, f32)
    wait_all(*up_in, *down_in)

    def one_block(step, carry):
        span = span_of(step)
        for chunked in inputs:
            chunked(step).wait()
        normed, _ = normalise(resid_in[span, :])
        block = normed * norm_in[0:1, :] + norm_in[1:2, :]
        block_low = block.astype(bf16)
        low[span, :] = block_low
        for chunk in range(4):
            pre = dot(block_low, matrix(w, chunk))
            value, square, flat = gelu(pre)
            value = value.astype(bf16)
            slopes[chunk] = gelu_slope(pre, square, flat)
            active[chunk, span, :] = value
            block = block + dot(value, matrix(w, 4 + chunk))
        normed, scale_inv = normalise(block)
        final_out[span, :] = (normed * norm_out[0:1, :] + norm_out[1:2, :]).astype(bf16)
        final_to(step).start()
        grad = cotangent[span, :].astype(f32) * jnp.concatenate([valid[span, :]] * 4, axis=1)
        norm_grad[0:1, :] += jnp.sum(grad * normed, axis=0, keepdims=True)
        norm_grad[1:2, :] += jnp.sum(grad, axis=0, keepdims=True)
        grad = norm_back(grad, normed, scale_inv, norm_out[0:1, :])
        block_grad = grad.astype(bf16)
        grad_low[span, :] = block_grad
        for chunk in range(4):
            value = (dot(block_grad, matrix(w, 4 + chunk), 1, 1) * slopes[chunk]).astype(bf16)
            grad_pre[chunk, span, :] = value
            grad = grad + dot(value, matrix(w, chunk), 1, 1)
        grad_out[span, :] = grad
        grad_to(step).start()
        return carry

    lax.fori_loop(0, steps, one_block, 0)
    ffn_grads(steps, active, grad_low, low, grad_pre, halves, keep_hbm, send_hbm, sems, core)
    for step in range(steps):
        final_to(step).wait()
        grad_to(step).wait()


def ffn_turn(core, resid, norm_in, norm_out, cotangent, valid, weights, base):
    rows, width = resid.shape
    high, low = layout_of(weights)
    half = array((8, high, low, width), bf16)
    return pl.pallas_call(
        partial(ffn_turn_kernel, base, len(weights)),
        out_shape=[array((rows, width), bf16), array((rows, width), f32), half, half, array((2, width), f32)],
        in_specs=[SMEM, HBM, VMEM, VMEM, HBM, HBM] + [HBM] * len(weights),
        out_specs=[HBM] * 4 + [VMEM],
        scratch_shapes=[
            pltpu.VMEM((8, high, 2, low, width), bf16),
            pltpu.VMEM((rows, width), f32),
            pltpu.VMEM((rows, width), bf16),
            pltpu.VMEM((rows, 128), f32),
            pltpu.VMEM((rows, width), bf16),
            pltpu.VMEM((rows, width), f32),
            pltpu.VMEM((2, 8, high, low, width), bf16),
            pltpu.VMEM((4, rows, width), bf16),
            pltpu.VMEM((4, rows, width), bf16),
            pltpu.VMEM((4, TILE, width), f32),
            pltpu.VMEM((rows, width), bf16),
            pltpu.VMEM((rows, width), bf16),
            pltpu.SemaphoreType.DMA((48,)),
        ],
        compiler_params=pltpu.CompilerParams(vmem_limit_bytes=VMEM_LIMIT),
        cost_estimate=cost(25e9, 18e6),
        name="ffn_turn",
    )(core, resid, norm_in, norm_out, cotangent, valid, *weights)


def ffn_backward_kernel(base, parts, *refs):
    refs = list(refs)
    take = lambda number: [refs.pop(0) for _ in range(number)]
    core_ref, grad_from_hbm, resid_out_hbm, norm_out, resid_in_hbm, norm_in = take(6)
    weights = take(parts)
    grad_hbm, keep_hbm, send_hbm, norm_grad, early_grad = take(5)
    (w, grad_in, resid_out, resid_in, grad_out, halves, active, grad_pre, grad_low, low, ref) = take(11)
    sems = Sems(ref)
    core = core_ref[0]
    steps = resid_in.shape[0] // TILE
    up_in = weight_copies(sems, weights, base, 0, 4, w, core)
    down_in = weight_copies(sems, weights, base, 4, 4, w, core)
    inputs = [
        by_rows(sems, grad_from_hbm, grad_in, steps),
        by_rows(sems, resid_out_hbm, resid_out, steps),
        by_rows(sems, resid_in_hbm, resid_in, steps),
    ]
    grad_to = by_rows(sems, grad_out, grad_hbm, steps)
    for step in range(steps):
        if step == 1:
            start_all(*up_in, *down_in)
        for chunked in inputs:
            chunked(step).start()
    norm_grad[...] = jnp.zeros(norm_grad.shape, f32)
    early_grad[...] = jnp.zeros(early_grad.shape, f32)
    wait_all(*up_in, *down_in)

    def one_block(step, carry):
        span = span_of(step)
        for chunked in inputs:
            chunked(step).wait()
        early, _ = normalise(resid_in[span, :])
        block_low = (early * norm_in[0:1, :] + norm_in[1:2, :]).astype(bf16)
        low[span, :] = block_low
        normed, scale_inv = normalise(resid_out[span, :])
        grad = grad_in[span, :]
        norm_grad[0:1, :] += jnp.sum(grad * normed, axis=0, keepdims=True)
        norm_grad[1:2, :] += jnp.sum(grad, axis=0, keepdims=True)
        grad = norm_back(grad, normed, scale_inv, norm_out[0:1, :])
        block_grad = grad.astype(bf16)
        grad_low[span, :] = block_grad
        for chunk in range(4):
            pre = dot(block_low, matrix(w, chunk))
            value, square, flat = gelu(pre)
            active[chunk, span, :] = value.astype(bf16)
            slope = gelu_slope(pre, square, flat)
            value = (dot(block_grad, matrix(w, 4 + chunk), 1, 1) * slope).astype(bf16)
            grad_pre[chunk, span, :] = value
            grad = grad + dot(value, matrix(w, chunk), 1, 1)
        grad_out[span, :] = grad
        grad_to(step).start()
        early_grad[0:1, :] += jnp.sum(grad * early, axis=0, keepdims=True)
        early_grad[1:2, :] += jnp.sum(grad, axis=0, keepdims=True)
        return carry

    lax.fori_loop(0, steps, one_block, 0)
    ffn_grads(steps, active, grad_low, low, grad_pre, halves, keep_hbm, send_hbm, sems, core)
    for step in range(steps):
        grad_to(step).wait()


def ffn_backward(core, grad, resid_out, norm_out, resid_in, norm_in, weights, base):
    rows, width = resid_in.shape
    high, low = layout_of(weights)
    half = array((8, high, low, width), bf16)
    norm_shape = array((2, width), f32)
    return pl.pallas_call(
        partial(ffn_backward_kernel, base, len(weights)),
        out_shape=[array((rows, width), f32), half, half, norm_shape, norm_shape],
        in_specs=[SMEM, HBM, HBM, VMEM, HBM, VMEM] + [HBM] * len(weights),
        out_specs=[HBM] * 3 + [VMEM] * 2,
        scratch_shapes=[
            pltpu.VMEM((8, high, 2, low, width), bf16),
            pltpu.VMEM((rows, width), f32),
            pltpu.VMEM((rows, width), f32),
            pltpu.VMEM((rows, width), f32),
            pltpu.VMEM((rows, width), f32),
            pltpu.VMEM((2, 8, high, low, width), bf16),
            pltpu.VMEM((4, rows, width), bf16),
            pltpu.VMEM((4, rows, width), bf16),
            pltpu.VMEM((rows, width), bf16),
            pltpu.VMEM((rows, width), bf16),
            pltpu.SemaphoreType.DMA((48,)),
        ],
        compiler_params=pltpu.CompilerParams(vmem_limit_bytes=VMEM_LIMIT),
        cost_estimate=cost(23e9, 18e6),
        name="ffn_backward",
    )(core, grad, resid_out, norm_out, resid_in, norm_in, *weights)


AXES = ("wide", "narrow")


def exchange_phases(mesh):
    devices = list(mesh.devices.reshape(-1))
    count = len(devices)
    bits = [1 << place for place in range(count.bit_length() - 1)]
    spots = [tuple(getattr(device, "coords", None) or ()) for device in devices]
    core, along, across = [], [], []
    for bit in bits:
        moved = [i for i, (p, q) in enumerate(zip(spots[0], spots[bit])) if p != q]
        if spots[0] and not moved:
            core.append(bit)
        elif moved == [2]:
            along.append(bit)
        else:
            across.append(bit)
    pairs = [across[i : i + 2] for i in range(0, len(across), 2)] + [[bit] for bit in core]
    plain = (count, bits[::-1], [along] + pairs if along else pairs)
    outward = (count, bits[::-1], [[bit] for bit in along] + pairs)
    inward = (count, bits[::-1], [[bit] for bit in along[::-1]] + pairs)
    return plain, outward, inward, len(along)


def halves_of(plan, rows):
    count, order, phases = plan
    block = rows // count
    bits = phases[-1]
    if len(bits) == 1 and (bits[0] * block) % 16 == 0:
        return count // (2 * bits[0]), bits[0] * block, True
    return 1, rows // 2, False


def masks_of(bits):
    masks = [0]
    for bit in bits:
        masks += [mask | bit for mask in masks]
    return masks


def swap(value, count, mask):
    return lax.ppermute(value, AXES, [(i, i ^ mask) for i in range(count)])


def nought_of(value):
    return jnp.minimum(jnp.abs(value[(0,) * value.ndim].astype(f32)), 0.0).astype(jnp.int32)


def spot_of(lead, bits_held, bits, mask, tail, nought=0):
    me = lax.axis_index(AXES) + nought
    spot = [0] * len(lead)
    for bit in bits_held:
        spot.append(jnp.where((me ^ mask) & bit != 0, 1, 0) if bit in bits else 0)
    return spot + [0] * len(tail)


def gather_send(plan, value, phase):
    count, order, phases = plan
    return [swap(value, count, mask) if mask else value for mask in masks_of(phases[phase])]


def gather_join(plan, pieces, phase):
    count, order, phases = plan
    bits = phases[phase]
    held = [bit for group in phases[: phase + 1] for bit in group]
    held = [bit for bit in order if bit in held]
    lead, tail = pieces[0].shape[:1], pieces[0].shape[-2:]
    full = jnp.zeros(lead + (2,) * len(held) + tail, pieces[0].dtype)
    for mask, piece in zip(masks_of(bits), pieces):
        piece = piece.reshape(lead + tuple(1 if bit in bits else 2 for bit in held) + tail)
        full = lax.dynamic_update_slice(full, piece, spot_of(lead, held, bits, mask, tail))
    return full


def scatter_send(plan, parts, phase, nought=0):
    count, order, phases = plan
    bits = phases[phase]
    held = [bit for group in phases[: phase + 1] for bit in group]
    held = [bit for bit in order if bit in held]
    lead, tail = parts[0].shape[:1], parts[0].shape[-2:]
    sizes = lead + tuple(1 if bit in bits else 2 for bit in held) + tail
    pieces = []
    for mask in masks_of(bits):
        total = None
        for part in parts:
            piece = lax.dynamic_slice(part, spot_of(lead, held, bits, mask, tail, nought), sizes)
            if len(parts) > 1:
                piece = piece.astype(f32)
            total = piece if total is None else total + piece
        total = total.astype(bf16).reshape(lead + (2,) * (len(held) - len(bits)) + tail)
        pieces.append(swap(total, count, mask) if mask else total)
    return pieces


def scatter_end(parts, nought=0):
    total = sum(part.astype(f32) for part in parts[1:]) + parts[0].astype(f32)
    return jnp.where(nought == 0, total, 0.0)


def spread(plan, value):
    count, order, phases = plan
    return value.reshape((value.shape[0],) + (2,) * len(order) + (value.shape[1] // count, value.shape[2]))


def weights_send(plan, value, width):
    high, low, split = halves_of(plan, width)
    last = len(plan[2]) - 1
    if not split:
        full = gather_join(plan, gather_send(plan, value, last), last)
        return [full.reshape(-1, high, 2, low, width)]
    return [piece.reshape(-1, high, low, width) for piece in gather_send(plan, value, last)]


def grads_send(plan, keep, send, width):
    count, order, phases = plan
    high, low, split = halves_of(plan, width)
    last = len(phases) - 1
    blocks, rows = keep.shape[0], width // count
    if not split:
        full = jnp.stack([keep, send], axis=2).reshape(blocks, width, width)
        return scatter_send(plan, [spread(plan, full)], last)
    shape = (blocks,) + (2,) * (len(order) - 1) + (rows, width)
    return [keep.reshape(shape), swap(send, count, phases[last][0]).reshape(shape)]


def after(values, *others):
    values, _ = lax.optimization_barrier((values, others))
    return values


def put_norms(plan, halves, norm_grad):
    count, order, phases = plan
    blocks, high, low, width = halves.shape
    rows = width // count
    blocks = -(-10 // rows)
    value = jnp.pad(norm_grad, ((0, blocks * rows - 10), (0, 0))).reshape(blocks, 1, 1, rows, width)
    value = jnp.broadcast_to(value, (blocks, high, low // rows, rows, width)).astype(halves.dtype)
    return lax.dynamic_update_slice(halves, value.reshape(blocks, high, low, width), (4, 0, 0, 0))


def own_lanes(count, value):
    width = value.shape[-1]
    piece = width // count
    value = value.reshape(-1, width)[:10]
    return lax.dynamic_slice(value, (0, lax.axis_index(AXES) * piece), (10, piece)).reshape(5, 2, piece)


def pack_norms(count, norm_gain, norm_bias):
    piece = norm_gain.shape[1]
    width = count * piece
    shard = jnp.stack([norm_gain, norm_bias], axis=1).reshape(10, piece)
    blocks = -(-10 // piece)
    spot = lax.axis_index(AXES) * piece
    full = lax.dynamic_update_slice(jnp.zeros((blocks * piece, width), shard.dtype), shard, (0, spot))
    return full.reshape(blocks, piece, width)


def unpack_norms(count, value):
    blocks, width = value.shape[0], value.shape[2]
    value = value.reshape(blocks, count, -1, width).astype(f32).sum(axis=1)
    return value.reshape(-1, width)[:10].reshape(5, 2, width)


def meet(outputs, *in_flight):
    return lax.optimization_barrier((tuple(outputs),) + in_flight)


def pack_attention(proj, mix):
    return jnp.concatenate([proj, mix[None]])


def pack_ffn(count, up, down):
    rows, width = up.shape[0], down.shape[1]
    up = up.reshape(rows, count, 4, rows).transpose(2, 0, 1, 3).reshape(4, rows, width)
    return jnp.concatenate([up, down.reshape(4, rows, width)])


def unpack_ffn(count, grad):
    rows, width = grad.shape[1:]
    up = grad[:4].reshape(4, rows, count, rows).transpose(1, 2, 0, 3).reshape(rows, 4 * width)
    return up, grad[4:].reshape(4 * rows, width)


def on_device(
    plans,
    source,
    target,
    source_segments,
    target_segments,
    encoder_proj,
    encoder_mix,
    encoder_up,
    encoder_down,
    self_proj,
    self_mix,
    cross_proj,
    cross_mix,
    decoder_up,
    decoder_down,
    norm_gain,
    norm_bias,
    cotangent,
):
    plan, outward, inward, along = plans
    count = plan[0]
    width = source.shape[-1]
    piece = norm_gain.shape[1]
    source_low = source.reshape(-1, width)
    target_low = target.reshape(-1, width)
    last = len(plan[2]) - 1
    high, low, split = halves_of(plan, width)
    if split:
        core = jnp.where(lax.axis_index(AXES) & plan[2][-1][0] != 0, 1, 0).astype(jnp.int32).reshape(1)
    else:
        core = jnp.zeros((1,), jnp.int32)

    enc = pack_attention(encoder_proj, encoder_mix)
    own = pack_attention(self_proj, self_mix)
    rest = jnp.concatenate(
        [
            pack_ffn(count, encoder_up, encoder_down),
            pack_attention(cross_proj, cross_mix),
            pack_norms(count, norm_gain, norm_bias),
        ]
    )
    rest = lax.all_gather(rest, AXES, axis=1, tiled=True)
    dec = pack_ffn(count, decoder_up, decoder_down)

    final = len(outward[2]) - 1
    enc, own, dec = meet(
        gather_send(plan, enc, 0), gather_send(outward, own, 0), gather_send(outward, dec, 0)
    )
    enc = gather_join(plan, enc, 0)
    own = gather_join(outward, own, 0)
    dec = gather_join(outward, dec, 0)
    for phase in range(1, last):
        enc = gather_send(plan, enc, phase)
        if phase < along:
            own = gather_send(outward, own, phase)
            enc, own = meet(enc, own)
            own = gather_join(outward, own, phase)
        enc = gather_join(plan, enc, phase)
    enc = weights_send(plan, enc, width)
    for phase in range(along, final - 1):
        own = gather_join(outward, gather_send(outward, own, phase), phase)
    own = gather_send(outward, own, final - 1)
    dec = gather_send(outward, dec, along - 1)

    source_cols = key_columns(source_segments)
    target_cols = key_columns(target_segments)
    source_rows = source_segments.reshape(-1, 1, BLOCK)
    target_rows = target_segments.reshape(-1, 1, BLOCK)
    enc_ranges = key_ranges(source_segments, source_segments, False)
    own_ranges = key_ranges(target_segments, target_segments, True)
    far_ranges = key_ranges(target_segments, source_segments, False)

    step = attend_forward(
        core, source_low, None, None, source_cols, source_rows, enc_ranges, enc, 0, False
    )
    (enc_one, *enc_saved), own, dec = meet(step, own, dec)
    own = weights_send(outward, gather_join(outward, own, final - 1), width)
    for phase in range(along, final):
        dec = gather_send(outward, gather_join(outward, dec, phase - 1), phase)
    step = attend_forward(
        core, after(target_low, dec[0]), None, None, target_cols, target_rows, own_ranges, own, 0, True
    )
    (own_sum, *own_saved), rest = meet(step, rest)
    norms = unpack_norms(count, rest[12:])
    rest = [rest.reshape(-1, high, 2, low, width)]
    step = ffn_forward(core, enc_one, norms[0], norms[1], rest, 0)
    (enc_two, enc_low), dec = meet(step, dec)
    dec = weights_send(outward, gather_join(outward, dec, final - 1), width)
    step = attend_forward(
        core, after(own_sum, dec[0]), norms[2], enc_low, source_cols, target_rows, far_ranges, rest, 8, False
    )
    (far_sum, second_low, *far_saved), dec = meet(step, dec)
    valid = jnp.broadcast_to((target_segments >= 0).reshape(-1, 1).astype(f32), (target_low.shape[0], 128))
    decoded, grad, dec_keep, dec_send, norm_four = ffn_turn(
        core, far_sum, norms[3], norms[4], cotangent.reshape(-1, width), valid, dec, 0
    )
    def across(parts):
        for phase in range(final - 1, along - 1, -1):
            parts = scatter_send(inward, parts, phase)
        return parts

    dec_parts = across(grads_send(inward, dec_keep, dec_send, width))
    step = attend_backward(
        core, after(grad, dec_parts[0]), far_sum, norms[3], second_low, enc_low, far_saved, source_cols, target_rows,
        far_ranges, rest, 8, False, f32
    )
    (grad, grad_enc, far_keep, far_send, norm_three), dec_parts = meet(step, dec_parts)
    far_parts = grads_send(inward, far_keep, far_send, width)
    dec_parts = scatter_send(inward, dec_parts, along - 1)
    far_parts = across(far_parts)
    step = ffn_backward(
        core, after(grad_enc, far_parts[0], dec_parts[0]), enc_two, norms[1], enc_one, norms[0], rest, 0
    )
    (grad_enc, ffn_keep, ffn_send, norm_one, norm_zero), dec_parts, far_parts = meet(step, dec_parts, far_parts)
    ffn_parts = grads_send(inward, ffn_keep, ffn_send, width)
    for phase in range(along - 2, -1, -1):
        dec_parts = scatter_send(inward, dec_parts, phase)
    far_parts = scatter_send(inward, far_parts, along - 1)
    ffn_parts = across(ffn_parts)
    extra = -(-10 // piece)
    step = attend_backward(
        core, after(grad, dec_parts[0], ffn_parts[0], far_parts[0]), own_sum, norms[2], target_low, None, own_saved,
        target_cols, target_rows, own_ranges, own, 0, True, bf16, extra
    )
    (target_grad, own_keep, own_send, norm_two), dec_parts, far_parts, ffn_parts = meet(
        step, dec_parts, far_parts, ffn_parts
    )
    norm_grad = jnp.concatenate([norm_zero, norm_one, norm_two, norm_three, norm_four])
    own_parts = grads_send(inward, put_norms(plan, own_keep, norm_grad), put_norms(plan, own_send, norm_grad), width)
    for phase in range(along - 2, -1, -1):
        far_parts = scatter_send(inward, far_parts, phase)
    ffn_parts = scatter_send(inward, ffn_parts, along - 1)
    own_parts = across(own_parts)
    step = attend_backward(
        core, after(grad_enc, far_parts[0], ffn_parts[0], own_parts[0]), enc_one, norms[0], source_low, None,
        enc_saved, source_cols, source_rows, enc_ranges, enc, 0, False, bf16
    )
    (source_grad, enc_keep, enc_send, _), far_parts, ffn_parts, own_parts = meet(step, far_parts, ffn_parts, own_parts)
    enc_parts = grads_send(plan, enc_keep, enc_send, width)
    enc_parts = scatter_send(plan, enc_parts, last - 1)
    nought = nought_of(enc_parts[0])
    own_parts = scatter_send(inward, own_parts, along - 1, nought)
    for phase in range(along - 2, -1, -1):
        ffn_parts = scatter_send(inward, ffn_parts, phase, nought)
    for phase in range(last - 2, -1, -1):
        enc_parts = scatter_send(plan, enc_parts, phase)
    for phase in range(along - 2, -1, -1):
        own_parts = scatter_send(inward, own_parts, phase)
    dec_sums, far_sums, ffn_sums, own_sums, enc_sums = [
        scatter_end(parts, nought) for parts in (dec_parts, far_parts, ffn_parts, own_parts, enc_parts)
    ]
    enc_up_out, enc_down_out = unpack_ffn(count, ffn_sums)
    dec_up_out, dec_down_out = unpack_ffn(count, dec_sums)
    norm_out = own_lanes(count, own_sums[4:])
    return (
        decoded.reshape(target.shape),
        source_grad.reshape(source.shape),
        target_grad.reshape(target.shape),
        enc_sums[:3],
        enc_sums[3],
        enc_up_out,
        enc_down_out,
        own_sums[:3],
        own_sums[3],
        far_sums[:3],
        far_sums[3],
        dec_up_out,
        dec_down_out,
        norm_out[:, 0],
        norm_out[:, 1],
    )


def solution(mesh):
    return jax.shard_map(
        partial(on_device, exchange_phases(mesh)),
        mesh=mesh,
        in_specs=(
            P(("wide", "narrow"), None, None),
            P(("wide", "narrow"), None, None),
            P(("wide", "narrow"), None),
            P(("wide", "narrow"), None),
            P(None, ("wide", "narrow"), None),
            P(("wide", "narrow"), None),
            P(("wide", "narrow"), None),
            P(("wide", "narrow"), None),
            P(None, ("wide", "narrow"), None),
            P(("wide", "narrow"), None),
            P(None, ("wide", "narrow"), None),
            P(("wide", "narrow"), None),
            P(("wide", "narrow"), None),
            P(("wide", "narrow"), None),
            P(None, ("wide", "narrow")),
            P(None, ("wide", "narrow")),
            P(("wide", "narrow"), None, None),
        ),
        out_specs=(
            P(("wide", "narrow"), None, None),
            P(("wide", "narrow"), None, None),
            P(("wide", "narrow"), None, None),
            P(None, ("wide", "narrow"), None),
            P(("wide", "narrow"), None),
            P(("wide", "narrow"), None),
            P(("wide", "narrow"), None),
            P(None, ("wide", "narrow"), None),
            P(("wide", "narrow"), None),
            P(None, ("wide", "narrow"), None),
            P(("wide", "narrow"), None),
            P(("wide", "narrow"), None),
            P(("wide", "narrow"), None),
            P(None, ("wide", "narrow")),
            P(None, ("wide", "narrow")),
        ),
        check_vma=False,
    )
```

```python
from functools import partial

import jax
import jax.numpy as jnp
from jax import lax
from jax.experimental import pallas as pl
from jax.experimental.pallas import tpu as pltpu
from jax.sharding import PartitionSpec as P

HEADS = 8
norm_eps = 1e-05
masked_score = -1e30
lowest = -3e38
log2_e = 1.4426950408889634
BLOCK = 128
TILE = 256
VMEM_LIMIT = 60 * 2**20
f32 = jnp.float32
bf16 = jnp.bfloat16


def dot(left, right, left_dim=1, right_dim=0):
    dims = (((left_dim,), (right_dim,)), ((), ()))
    return lax.dot_general(left, right, dims, preferred_element_type=f32)


def normalise(resid):
    mean = jnp.mean(resid, axis=-1, keepdims=True)
    centred = resid - mean
    scale_inv = lax.rsqrt(jnp.mean(centred * centred, axis=-1, keepdims=True) + norm_eps)
    return centred * scale_inv, scale_inv


def norm_back(grad, normed, scale_inv, gain):
    scaled = grad * gain
    mean_plain = jnp.mean(scaled, axis=-1, keepdims=True)
    mean_normed = jnp.mean(scaled * normed, axis=-1, keepdims=True)
    return scale_inv * (scaled - mean_plain - normed * mean_normed)


def key_ranges(query_segments, key_segments, causal):
    big = jnp.int32(1 << 30)
    query_order = jnp.where(query_segments < 0, big, query_segments).reshape(-1, BLOCK)
    key_order = jnp.where(key_segments < 0, big, key_segments).reshape(1, -1)
    first = jnp.sum((key_order < query_order[:, :1]).astype(jnp.int32), axis=1)
    stop = jnp.sum((key_order <= query_order[:, -1:]).astype(jnp.int32), axis=1)
    real = jnp.sum((key_order < big).astype(jnp.int32))
    if causal:
        stop = jnp.minimum(stop, (jnp.arange(stop.shape[0]) + 1) * BLOCK)
    start = first // 16 * 16
    tiles = (stop - start + TILE - 1) // TILE
    real_tiles = jnp.maximum((jnp.minimum(stop, real) - start + TILE - 1) // TILE, 0)
    real_tiles = jnp.where(first >= real, 0, real_tiles)
    return jnp.stack([start, tiles, real_tiles]).astype(jnp.int32)


def key_rows(key_segments):
    flat = jnp.pad(key_segments.reshape(-1), (0, TILE), constant_values=-2)
    return flat.reshape(-1, 1, BLOCK)


def fill_columns(key_col, key_seg):
    for index in range(key_seg.shape[0]):
        key_col[index * BLOCK : (index + 1) * BLOCK, :] = jnp.broadcast_to(key_seg[index], (BLOCK, BLOCK)).T


def head_pair_mask():
    lane = lax.broadcasted_iota(jnp.int32, (1, 128), 1)
    return lane < 64


def stack_heads(block, even):
    zero = jnp.zeros_like(block)
    return jnp.concatenate([jnp.where(even, block, zero), jnp.where(even, zero, block)], axis=0)


def tile_bias(bias_ref, key_col_ref, query_row, key_start, query_start, causal):
    allowed = key_col_ref[pl.ds(key_start, TILE), :] == query_row
    if causal:
        key_place = key_start + lax.broadcasted_iota(jnp.int32, (TILE, BLOCK), 0)
        query_place = query_start + lax.broadcasted_iota(jnp.int32, (TILE, BLOCK), 1)
        allowed = allowed & (key_place <= query_place)
    bias_ref[...] = jnp.where(allowed, 0.0, masked_score).astype(f32)


HBM = pl.BlockSpec(memory_space=pltpu.HBM)
VMEM = pl.BlockSpec(memory_space=pltpu.VMEM)
SMEM = pl.BlockSpec(memory_space=pltpu.SMEM)


class Sems:
    def __init__(self, ref):
        self.ref = ref
        self.used = 0

    def take(self, number=1):
        self.used += number
        return self.used - number

    def copy(self, src, dst, place):
        return pltpu.make_async_copy(src, dst, self.ref.at[place])


def span_of(step):
    return pl.ds(step * TILE if isinstance(step, int) else pl.multiple_of(step * TILE, TILE), TILE)


def by_rows(sems, src, dst, steps):
    first = sems.take(steps)
    return lambda step: sems.copy(src.at[span_of(step)], dst.at[span_of(step)], first + step)


def by_columns(sems, src, dst, steps):
    first = sems.take(steps)
    return lambda step: sems.copy(src.at[:, span_of(step)], dst.at[:, span_of(step)], first + step)


def whole(sems, src, dst):
    place = sems.take()
    return lambda: sems.copy(src, dst, place)


def weight_copies(sems, parts, base, start, size, dst, core):
    span = pl.ds(start, size)
    if len(parts) == 1:
        return [whole(sems, parts[0].at[pl.ds(base + start, size)], dst.at[span])]
    source = pl.ds(base + start, size)
    return [
        whole(sems, parts[0].at[source], dst.at[span, :, core]),
        whole(sems, parts[1].at[source], dst.at[span, :, 1 - core]),
    ]


def block_copies(sems, parts, base, blocks, dst, core):
    return {index: weight_copies(sems, parts, base, index, 1, dst, core) for index in blocks}


def start_all(*copies):
    for copy in copies:
        copy().start()


def wait_all(*copies):
    for copy in copies:
        copy().wait()


def matrix(blocks, index):
    block = blocks[index]
    return block.reshape(block.shape[0] * block.shape[1] * block.shape[2], block.shape[3])


def put_grad(halves, index, value, core):
    value = value.astype(bf16)
    high, low = halves.shape[2:4]
    for major in range(high):
        for side in range(2):
            at = (2 * major + side) * low
            halves[core if side == 0 else 1 - core, index, major] = value[at : at + low]


def forward_kernel(causal, fresh, base, parts, *refs):
    refs = list(refs)
    take = lambda number: [refs.pop(0) for _ in range(number)]
    core_ref, ranges, own_hbm = take(3)
    norm_own, other_hbm = (None, own_hbm) if fresh else take(2)
    key_seg, query_seg = take(2)
    weights = take(parts)
    (resid_hbm,) = take(1)
    (low_hbm,) = (None,) if fresh else take(1)
    q_hbm, k_hbm, v_hbm, o_hbm, lse_out = take(5)
    w, own, key_col, resid_out, q_out, k_out, v_out, o_out, stacked, bias, acc, peak, total, ref = take(14)
    other, low_out = (own, None) if fresh else take(2)
    sems = Sems(ref)
    core = core_ref[0]
    rows = own.shape[0]
    steps = rows // TILE
    even = head_pair_mask()
    scale = 0.125 * log2_e
    proj_in = weight_copies(sems, weights, base, 0, 3, w, core)
    own_in = by_rows(sems, own_hbm, own, steps)
    other_in = None if fresh else by_rows(sems, other_hbm, other, steps)
    mix_in = weight_copies(sems, weights, base, 3, 1, w, core)
    start_all(*proj_in)
    for step in range(steps):
        own_in(step).start()
        if not fresh:
            other_in(step).start()
    start_all(*mix_in)
    fill_columns(key_col, key_seg)
    q_to = by_rows(sems, q_out, q_hbm, steps)
    k_to = whole(sems, k_out, k_hbm)
    v_to = whole(sems, v_out, v_hbm)
    o_to = by_columns(sems, o_out, o_hbm, steps)
    resid_to = by_rows(sems, resid_out, resid_hbm, steps)
    low_to = None if fresh else by_rows(sems, low_out, low_hbm, steps)
    wait_all(*proj_in)

    def fill(step, carry):
        span = span_of(step)
        own_in(step).wait()
        block = own[span, :]
        if fresh:
            block_low = block
            key_block = block
        else:
            other_in(step).wait()
            normed, _ = normalise(block)
            block_low = (normed * norm_own[0:1, :] + norm_own[1:2, :]).astype(bf16)
            low_out[span, :] = block_low
            low_to(step).start()
            key_block = other[span, :]
        query = dot(block_low, matrix(w, 0)).astype(bf16)
        q_out[span, :] = query
        q_to(step).start()
        for sub in range(TILE // BLOCK):
            for pair in range(4):
                part = query[sub * BLOCK : (sub + 1) * BLOCK, pair * 128 : (pair + 1) * 128]
                stacked[step * (TILE // BLOCK) + sub, pair] = stack_heads(part, even)
        k_out[span, :] = dot(key_block, matrix(w, 1)).astype(bf16)
        v_out[span, :] = dot(key_block, matrix(w, 2)).astype(bf16)
        return carry

    lax.fori_loop(0, steps, fill, 0)
    k_out[rows:, :] = jnp.zeros((TILE, k_out.shape[1]), bf16)
    v_out[rows:, :] = jnp.zeros((TILE, v_out.shape[1]), bf16)
    start_all(k_to, v_to)

    def one_block(index, carry):
        start = ranges[0, index]
        tiles = ranges[1, index]
        query_start = pl.multiple_of(index * BLOCK, BLOCK)
        query_row = query_seg[index]
        peak[...] = jnp.full(peak.shape, lowest, f32)
        total[...] = jnp.zeros(total.shape, f32)
        acc[...] = jnp.zeros(acc.shape, f32)

        def one_tile(tile, inner):
            at = pl.multiple_of(start + tile * TILE, 16)
            tile_bias(bias, key_col, query_row, at, query_start, causal)
            span = pl.ds(at, TILE)
            lanes = [slice(pair * 128, (pair + 1) * 128) for pair in range(4)]
            ahead = 4
            raw = [dot(k_out[span, lanes[pair]], stacked[index, pair], 1, 1) for pair in range(ahead)]
            befores = [peak[pair : pair + 1, :] for pair in range(4)]
            totals = [total[pair : pair + 1, :] for pair in range(4)]
            blocked = jnp.concatenate([bias[...]] * 2, axis=1)
            peaks, sums, mixes, shrinks = [], [], [], []
            for pair in range(4):
                scores = raw[pair] * scale + blocked
                above = jnp.maximum(befores[pair], jnp.max(scores, axis=0, keepdims=True))
                probs = jnp.exp2(scores - above)
                shrink = jnp.exp2(befores[pair] - above)
                if pair + ahead < 4:
                    raw.append(dot(k_out[span, lanes[pair + ahead]], stacked[index, pair + ahead], 1, 1))
                sums.append(totals[pair] * shrink + jnp.sum(probs, axis=0, keepdims=True))
                peaks.append(above)
                shrinks.append(shrink)
                mixes.append(dot(v_out[span, lanes[pair]], probs.astype(bf16), 0, 0))
            for pair in range(4):
                peak[pair : pair + 1, :] = peaks[pair]
                total[pair : pair + 1, :] = sums[pair]
                top = pair * 128
                mixed = mixes[pair]
                shrink = shrinks[pair]
                acc[top : top + 64, :] = acc[top : top + 64, :] * shrink[:, :128] + mixed[:64, :128]
                acc[top + 64 : top + 128, :] = (
                    acc[top + 64 : top + 128, :] * shrink[:, 128:] + mixed[64:, 128:]
                )
            return inner

        lax.fori_loop(0, tiles, one_tile, 0)
        for pair in range(4):
            inverse = 1.0 / total[pair : pair + 1, :]
            top = pair * 128
            o_out[top : top + 64, pl.ds(query_start, BLOCK)] = (
                acc[top : top + 64, :] * inverse[:, :128]
            ).astype(bf16)
            o_out[top + 64 : top + 128, pl.ds(query_start, BLOCK)] = (
                acc[top + 64 : top + 128, :] * inverse[:, 128:]
            ).astype(bf16)
        lse_out[index] = peak[...] + jnp.log2(total[...])
        return carry

    lax.fori_loop(0, rows // BLOCK, one_block, 0)
    wait_all(*mix_in)

    def finish(step, carry):
        span = span_of(step)
        o_to(step).start()
        block = own[span, :]
        if fresh:
            block = block.astype(f32)
        else:
            normed, _ = normalise(block)
            block = normed * norm_own[0:1, :] + norm_own[1:2, :]
        resid_out[span, :] = block + dot(o_out[:, span], matrix(w, 3), 0, 0)
        resid_to(step).start()
        return carry

    lax.fori_loop(0, steps, finish, 0)
    wait_all(k_to, v_to)
    for step in range(steps):
        q_to(step).wait()
        o_to(step).wait()
        if not fresh:
            low_to(step).wait()
        resid_to(step).wait()


def cost(flops, moved):
    return pl.CostEstimate(flops=int(flops), bytes_accessed=int(moved), transcendentals=0)


def array(shape, dtype):
    return jax.ShapeDtypeStruct(shape, dtype)


def attend_forward(core, own, norm_own, other, key_col, query_seg, ranges, weights, base, causal):
    fresh = norm_own is None
    rows, width = own.shape
    blocks = rows // BLOCK
    high, low = layout_of(weights)
    ins = [own] if fresh else [own, norm_own, other]
    specs = [HBM] if fresh else [HBM, VMEM, HBM]
    ins += [key_col, query_seg, *weights]
    specs += [VMEM, VMEM] + [HBM] * len(weights)
    shapes = [array((rows, width), f32)]
    if not fresh:
        shapes.append(array((rows, width), bf16))
    shapes += [
        array((rows, width), bf16),
        array((rows + TILE, width), bf16),
        array((rows + TILE, width), bf16),
        array((width, rows), bf16),
        array((blocks, 4, 2 * BLOCK), f32),
    ]
    scratch = [
        pltpu.VMEM((4, high, 2, low, width), bf16),
        pltpu.VMEM((rows, width), own.dtype),
        pltpu.VMEM((rows + TILE, 128), jnp.int32),
        pltpu.VMEM((rows, width), f32),
        pltpu.VMEM((rows, width), bf16),
        pltpu.VMEM((rows + TILE, width), bf16),
        pltpu.VMEM((rows + TILE, width), bf16),
        pltpu.VMEM((width, rows), bf16),
        pltpu.VMEM((blocks, 4, 2 * BLOCK, 128), bf16),
        pltpu.VMEM((TILE, BLOCK), f32),
        pltpu.VMEM((width, BLOCK), f32),
        pltpu.VMEM((4, 2 * BLOCK), f32),
        pltpu.VMEM((4, 2 * BLOCK), f32),
        pltpu.SemaphoreType.DMA((64,)),
    ]
    if not fresh:
        scratch += [pltpu.VMEM((rows, width), bf16)] * 2
    return pl.pallas_call(
        partial(forward_kernel, causal, fresh, base, len(weights)),
        out_shape=shapes,
        in_specs=[SMEM, SMEM] + specs,
        out_specs=[HBM] * (len(shapes) - 1) + [VMEM],
        scratch_shapes=scratch,
        compiler_params=pltpu.CompilerParams(vmem_limit_bytes=VMEM_LIMIT),
        cost_estimate=cost(20e9, 12e6) if fresh else cost(1e9, 1e6),
        name="attend_forward",
    )(core, ranges, *ins)


def layout_of(weights):
    shape = weights[0].shape
    return (shape[1], shape[2]) if len(weights) == 2 else (shape[1], shape[3])


def backward_kernel(causal, same, base, parts, *refs):
    refs = list(refs)
    take = lambda number: [refs.pop(0) for _ in range(number)]
    core_ref, ranges, grad_hbm, resid_hbm, norm, own_hbm = take(6)
    other_hbm = None if same else take(1)[0]
    q_hbm, k_hbm, v_hbm, o_hbm, lse, key_seg, query_seg = take(7)
    weights = take(parts)
    (own_grad_hbm,) = take(1)
    other_grad_hbm = None if same else take(1)[0]
    keep_hbm, send_hbm, norm_grad = take(3)
    (w, grad, resid, own, q_in, k_in, v_in, o_in, key_col, sums, own_grad, halves,
     low, stacked, grad_stacked, inner_rows, bias, acc, dq, dk, dv, ref) = take(22)
    other, other_grad = (own, None) if same else take(2)
    sems = Sems(ref)
    core = core_ref[0]
    rows = own.shape[0]
    steps = rows // TILE
    even = head_pair_mask()
    scale = 0.125 * log2_e

    mix_in = weight_copies(sems, weights, base, 3, 1, w, core)
    grad_in = by_rows(sems, grad_hbm, grad, steps)
    resid_in = by_rows(sems, resid_hbm, resid, steps)
    o_from = by_columns(sems, o_hbm, o_in, steps)
    q_from = by_rows(sems, q_hbm, q_in, steps)
    later = [whole(sems, k_hbm, k_in), whole(sems, v_hbm, v_in)]
    last = [whole(sems, own_hbm, own)] + weight_copies(sems, weights, base, 0, 3, w, core)
    if not same:
        last.append(whole(sems, other_hbm, other))
    start_all(*mix_in)
    for step in range(steps):
        for chunked in (grad_in, resid_in, o_from, q_from):
            chunked(step).start()
    start_all(*later, *last)
    fill_columns(key_col, key_seg)
    keep_to = [whole(sems, halves.at[0, index], keep_hbm.at[index]) for index in range(4)]
    send_to = [whole(sems, halves.at[1, index], send_hbm.at[index]) for index in range(4)]
    own_to = by_rows(sems, own_grad, own_grad_hbm, steps)
    other_to = None if same else by_rows(sems, other_grad, other_grad_hbm, steps)

    norm_grad[...] = jnp.zeros(norm_grad.shape, f32)
    dk[...] = jnp.zeros(dk.shape, f32)
    dv[...] = jnp.zeros(dv.shape, f32)
    wait_all(*mix_in)

    def prepare(step, carry):
        span = span_of(step)
        for chunked in (grad_in, resid_in, o_from, q_from):
            chunked(step).wait()
        block = grad[span, :]
        normed, scale_inv = normalise(resid[span, :])
        norm_grad[0:1, :] += jnp.sum(block * normed, axis=0, keepdims=True)
        norm_grad[1:2, :] += jnp.sum(block, axis=0, keepdims=True)
        block = norm_back(block, normed, scale_inv, norm[0:1, :])
        sums[span, :] = block
        block = block.astype(bf16)
        low[span, :] = block
        grad_mixed = dot(block, matrix(w, 3), 1, 1).astype(bf16)
        flipped = dot(matrix(w, 3), block, 1, 1).astype(bf16).astype(f32)
        flipped = flipped * o_in[:, span].astype(f32)
        inner = [jnp.sum(flipped[head * 64 : (head + 1) * 64, :], axis=0, keepdims=True) for head in range(HEADS)]
        query = q_in[span, :]
        for sub in range(TILE // BLOCK):
            spot = step * (TILE // BLOCK) + sub
            part = slice(sub * BLOCK, (sub + 1) * BLOCK)
            rows_of = []
            for pair in range(4):
                lanes = slice(pair * 128, (pair + 1) * 128)
                stacked[spot, pair] = stack_heads(query[part, lanes], even)
                grad_stacked[spot, pair] = stack_heads(grad_mixed[part, lanes], even)
                rows_of.append(jnp.concatenate([inner[2 * pair][:, part], inner[2 * pair + 1][:, part]], axis=1))
            inner_rows[spot] = jnp.concatenate(rows_of, axis=0)
        return carry

    lax.fori_loop(0, steps, prepare, 0)
    put_grad(halves, 3, dot(o_in[...], low[...]), core)
    start_all(keep_to[3], send_to[3])
    wait_all(*later)

    def one_block(index, carry):
        start = ranges[0, index]
        tiles = ranges[2, index]
        query_start = pl.multiple_of(index * BLOCK, BLOCK)
        query_row = query_seg[index]
        acc[...] = jnp.zeros(acc.shape, f32)

        def one_tile(tile, inner):
            at = pl.multiple_of(start + tile * TILE, 16)
            tile_bias(bias, key_col, query_row, at, query_start, causal)
            span = pl.ds(at, TILE)
            lanes = [slice(pair * 128, (pair + 1) * 128) for pair in range(4)]
            keys = [k_in[span, lanes[pair]] for pair in range(4)]
            queries = [stacked[index, pair] for pair in range(4)]
            grads = [grad_stacked[index, pair] for pair in range(4)]
            blocked = jnp.concatenate([bias[...]] * 2, axis=1)
            raw = [dot(keys[0], queries[0], 1, 1)]
            grad_raw = [dot(v_in[span, lanes[0]], grads[0], 1, 1)]
            dvs, dks, mixes = [], [], []
            for pair in range(4):
                if pair < 3:
                    raw.append(dot(keys[pair + 1], queries[pair + 1], 1, 1))
                    grad_raw.append(dot(v_in[span, lanes[pair + 1]], grads[pair + 1], 1, 1))
                probs = jnp.exp2(raw[pair] * scale + blocked - lse[index, pair : pair + 1, :])
                grad_scores = (probs * (grad_raw[pair] - inner_rows[index, pair : pair + 1, :])).astype(bf16)
                dvs.append(dot(probs.astype(bf16), grads[pair]))
                dks.append(dot(grad_scores, queries[pair]))
                mixes.append(dot(keys[pair], grad_scores, 0, 0))
            dv[span, :] += jnp.concatenate(dvs, axis=1)
            dk[span, :] += jnp.concatenate(dks, axis=1)
            for pair in range(4):
                top = pair * 128
                acc[top : top + 64, :] += mixes[pair][:64, :128]
                acc[top + 64 : top + 128, :] += mixes[pair][64:, 128:]
            return inner

        lax.fori_loop(0, tiles, one_tile, 0)
        dq[pl.ds(query_start, BLOCK), :] = (acc[...].T * 0.125).astype(bf16)
        return carry

    lax.fori_loop(0, rows // BLOCK, one_block, 0)
    low[...] = (dk[:rows, :] * 0.125).astype(bf16)
    q_in[...] = dv[:rows, :].astype(bf16)
    wait_all(*last)
    for index, (left, right) in enumerate(((own, dq), (other, low), (other, q_in))):
        put_grad(halves, index, dot(left[...], right[...], 0, 0), core)
        start_all(keep_to[index], send_to[index])

    def finish(step, carry):
        span = span_of(step)
        query_side = sums[span, :] + dot(dq[span, :], matrix(w, 0), 1, 1)
        source_side = dot(low[span, :], matrix(w, 1), 1, 1) + dot(q_in[span, :], matrix(w, 2), 1, 1)
        if same:
            own_grad[span, :] = (query_side + source_side).astype(own_grad.dtype)
        else:
            own_grad[span, :] = query_side
            other_grad[span, :] = source_side
            other_to(step).start()
        own_to(step).start()
        return carry

    lax.fori_loop(0, steps, finish, 0)
    wait_all(*keep_to, *send_to)
    for step in range(steps):
        own_to(step).wait()
        if not same:
            other_to(step).wait()


def attend_backward(
    core, grad, resid, norm, own, other, saved, key_col, query_seg, ranges, weights, base, causal, out_dtype, extra=0
):
    same = other is None
    rows, width = own.shape
    blocks = rows // BLOCK
    high, low = layout_of(weights)
    q, k, v, o, lse = saved
    ins = [grad, resid, norm, own] + ([] if same else [other])
    specs = [HBM, HBM, VMEM, HBM] + ([] if same else [HBM])
    ins += [q, k, v, o, lse, key_col, query_seg, *weights]
    specs += [HBM] * 4 + [VMEM, VMEM, VMEM] + [HBM] * len(weights)
    shapes = [array((rows, width), out_dtype)]
    if not same:
        shapes.append(array((rows, width), f32))
    shapes += [array((4 + extra, high, low, width), bf16)] * 2
    shapes.append(array((2, width), f32))
    scratch = [
        pltpu.VMEM((4, high, 2, low, width), bf16),
        pltpu.VMEM((rows, width), f32),
        pltpu.VMEM((rows, width), f32),
        pltpu.VMEM((rows, width), bf16),
        pltpu.VMEM((rows, width), bf16),
        pltpu.VMEM((rows + TILE, width), bf16),
        pltpu.VMEM((rows + TILE, width), bf16),
        pltpu.VMEM((width, rows), bf16),
        pltpu.VMEM((rows + TILE, 128), jnp.int32),
        pltpu.VMEM((rows, width), f32),
        pltpu.VMEM((rows, width), out_dtype),
        pltpu.VMEM((2, 4, high, low, width), bf16),
        pltpu.VMEM((rows, width), bf16),
        pltpu.VMEM((blocks, 4, 2 * BLOCK, 128), bf16),
        pltpu.VMEM((blocks, 4, 2 * BLOCK, 128), bf16),
        pltpu.VMEM((blocks, 4, 2 * BLOCK), f32),
        pltpu.VMEM((TILE, BLOCK), f32),
        pltpu.VMEM((width, BLOCK), f32),
        pltpu.VMEM((rows, width), bf16),
        pltpu.VMEM((rows + TILE, width), f32),
        pltpu.VMEM((rows + TILE, width), f32),
        pltpu.SemaphoreType.DMA((64,)),
    ]
    if not same:
        scratch += [pltpu.VMEM((rows, width), bf16), pltpu.VMEM((rows, width), f32)]
    return pl.pallas_call(
        partial(backward_kernel, causal, same, base, len(weights)),
        out_shape=shapes,
        in_specs=[SMEM, SMEM] + specs,
        out_specs=[HBM] * (len(shapes) - 1) + [VMEM],
        scratch_shapes=scratch,
        compiler_params=pltpu.CompilerParams(vmem_limit_bytes=VMEM_LIMIT),
        cost_estimate=cost(25e9, 20e6),
        name="attend_backward",
    )(core, ranges, *ins)


root_two_pi = 0.7978845608028654


def gelu(pre):
    square = pre * pre
    flat = jnp.tanh(pre * (root_two_pi + (root_two_pi * 0.044715) * square))
    return pre * (0.5 + 0.5 * flat), square, flat


def gelu_slope(pre, square, flat):
    half = 0.5 + 0.5 * flat
    inner = (0.5 * root_two_pi) + (1.5 * root_two_pi * 0.044715) * square
    return half + pre * ((1.0 - flat * flat) * inner)


def ffn_forward_kernel(base, parts, *refs):
    refs = list(refs)
    take = lambda number: [refs.pop(0) for _ in range(number)]
    core_ref, resid_hbm, norm_in, norm_out = take(4)
    weights = take(parts)
    resid_to_hbm, low_hbm, w, resid_in, resid_out, low_out, ref = take(7)
    sems = Sems(ref)
    core = core_ref[0]
    steps = resid_in.shape[0] // TILE
    w_in = block_copies(sems, weights, base, range(8), w, core)
    resid_from = by_rows(sems, resid_hbm, resid_in, steps)
    resid_to = by_rows(sems, resid_out, resid_to_hbm, steps)
    low_to = by_rows(sems, low_out, low_hbm, steps)
    resid_from(0).start()
    for index in range(8):
        start_all(*w_in[index])
    for step in range(1, steps):
        resid_from(step).start()

    def one_block(step, first):
        span = span_of(step)
        resid_from(step).wait()
        normed, _ = normalise(resid_in[span, :])
        block = normed * norm_in[0:1, :] + norm_in[1:2, :]
        block_low = block.astype(bf16)
        pres = []
        for chunk in range(4):
            if first:
                wait_all(*w_in[chunk])
            pres.append(dot(block_low, matrix(w, chunk)))
        actives = [gelu(pre)[0].astype(bf16) for pre in pres]
        for chunk in range(4):
            if first:
                wait_all(*w_in[4 + chunk])
            block = block + dot(actives[chunk], matrix(w, 4 + chunk))
        resid_out[span, :] = block
        resid_to(step).start()
        normed, _ = normalise(block)
        low_out[span, :] = (normed * norm_out[0:1, :] + norm_out[1:2, :]).astype(bf16)
        low_to(step).start()
        return 0

    one_block(0, True)
    lax.fori_loop(1, steps, lambda step, carry: one_block(step, False), 0)
    for step in range(steps):
        resid_to(step).wait()
        low_to(step).wait()


def ffn_forward(core, resid, norm_in, norm_out, weights, base):
    rows, width = resid.shape
    high, low = layout_of(weights)
    return pl.pallas_call(
        partial(ffn_forward_kernel, base, len(weights)),
        out_shape=[array((rows, width), f32), array((rows, width), bf16)],
        in_specs=[SMEM, HBM, VMEM, VMEM] + [HBM] * len(weights),
        out_specs=[HBM, HBM],
        scratch_shapes=[
            pltpu.VMEM((8, high, 2, low, width), bf16),
            pltpu.VMEM((rows, width), f32),
            pltpu.VMEM((rows, width), f32),
            pltpu.VMEM((rows, width), bf16),
            pltpu.SemaphoreType.DMA((32,)),
        ],
        compiler_params=pltpu.CompilerParams(vmem_limit_bytes=VMEM_LIMIT),
        cost_estimate=cost(1e9, 1e6),
        name="ffn_forward",
    )(core, resid, norm_in, norm_out, *weights)


def ffn_grads(steps, active, grad_low, block_low, grad_pre, halves, keep_hbm, send_hbm, sems, core):
    first = sems.take(16)

    def out(index, side):
        target = send_hbm if side else keep_hbm
        return sems.copy(halves.at[side, index], target.at[index], first + 2 * index + side)

    def weight_part(chunk, carry):
        put_grad(halves, chunk, dot(block_low[...], grad_pre[chunk], 0, 0), core)
        out(chunk, 0).start()
        out(chunk, 1).start()
        put_grad(halves, 4 + chunk, dot(active[chunk], grad_low[...], 0, 0), core)
        out(4 + chunk, 0).start()
        out(4 + chunk, 1).start()
        return carry

    lax.fori_loop(0, 4, weight_part, 0)
    for index in range(8):
        out(index, 0).wait()
        out(index, 1).wait()


def ffn_turn_kernel(base, parts, *refs):
    refs = list(refs)
    take = lambda number: [refs.pop(0) for _ in range(number)]
    core_ref, resid_hbm, norm_in, norm_out, cotangent_hbm, valid_hbm = take(6)
    weights = take(parts)
    final_hbm, grad_hbm, keep_hbm, send_hbm, norm_grad = take(5)
    (w, resid_in, cotangent, valid, final_out, grad_out, halves,
     active, grad_pre, grad_low, low, ref) = take(12)
    sems = Sems(ref)
    core = core_ref[0]
    steps = resid_in.shape[0] // TILE
    w_in = block_copies(sems, weights, base, range(8), w, core)
    inputs = [
        by_rows(sems, resid_hbm, resid_in, steps),
        by_rows(sems, cotangent_hbm, cotangent, steps),
        by_rows(sems, valid_hbm, valid, steps),
    ]
    final_to = by_rows(sems, final_out, final_hbm, steps)
    grad_to = by_rows(sems, grad_out, grad_hbm, steps)
    for step in range(steps):
        if step == 1:
            for index in range(8):
                start_all(*w_in[index])
        for chunked in inputs:
            chunked(step).start()
    norm_grad[...] = jnp.zeros(norm_grad.shape, f32)

    def one_block(step, first):
        span = span_of(step)
        for chunked in inputs:
            chunked(step).wait()
        normed, _ = normalise(resid_in[span, :])
        block = normed * norm_in[0:1, :] + norm_in[1:2, :]
        block_low = block.astype(bf16)
        pres = []
        for chunk in range(4):
            if first:
                wait_all(*w_in[chunk])
            pres.append(dot(block_low, matrix(w, chunk)))
        actives, slopes = [], []
        for pre in pres:
            value, square, flat = gelu(pre)
            actives.append(value.astype(bf16))
            slopes.append(gelu_slope(pre, square, flat))
        for chunk in range(4):
            if first:
                wait_all(*w_in[4 + chunk])
            block = block + dot(actives[chunk], matrix(w, 4 + chunk))
        normed, scale_inv = normalise(block)
        grad = cotangent[span, :].astype(f32) * jnp.concatenate([valid[span, :]] * 4, axis=1)
        gain_part = jnp.sum(grad * normed, axis=0, keepdims=True)
        bias_part = jnp.sum(grad, axis=0, keepdims=True)
        grad = norm_back(grad, normed, scale_inv, norm_out[0:1, :])
        block_grad = grad.astype(bf16)
        values = [
            (dot(block_grad, matrix(w, 4 + chunk), 1, 1) * slopes[chunk]).astype(bf16) for chunk in range(4)
        ]
        for chunk in range(4):
            grad = grad + dot(values[chunk], matrix(w, chunk), 1, 1)
        grad_out[span, :] = grad
        grad_to(step).start()
        final_out[span, :] = (normed * norm_out[0:1, :] + norm_out[1:2, :]).astype(bf16)
        final_to(step).start()
        norm_grad[0:1, :] += gain_part
        norm_grad[1:2, :] += bias_part
        low[span, :] = block_low
        grad_low[span, :] = block_grad
        for chunk in range(4):
            active[chunk, span, :] = actives[chunk]
            grad_pre[chunk, span, :] = values[chunk]
        return 0

    one_block(0, True)
    lax.fori_loop(1, steps, lambda step, carry: one_block(step, False), 0)
    ffn_grads(steps, active, grad_low, low, grad_pre, halves, keep_hbm, send_hbm, sems, core)
    for step in range(steps):
        final_to(step).wait()
        grad_to(step).wait()


def ffn_turn(core, resid, norm_in, norm_out, cotangent, valid, weights, base):
    rows, width = resid.shape
    high, low = layout_of(weights)
    half = array((8, high, low, width), bf16)
    return pl.pallas_call(
        partial(ffn_turn_kernel, base, len(weights)),
        out_shape=[array((rows, width), bf16), array((rows, width), f32), half, half, array((2, width), f32)],
        in_specs=[SMEM, HBM, VMEM, VMEM, HBM, HBM] + [HBM] * len(weights),
        out_specs=[HBM] * 4 + [VMEM],
        scratch_shapes=[
            pltpu.VMEM((8, high, 2, low, width), bf16),
            pltpu.VMEM((rows, width), f32),
            pltpu.VMEM((rows, width), bf16),
            pltpu.VMEM((rows, 128), f32),
            pltpu.VMEM((rows, width), bf16),
            pltpu.VMEM((rows, width), f32),
            pltpu.VMEM((2, 8, high, low, width), bf16),
            pltpu.VMEM((4, rows, width), bf16),
            pltpu.VMEM((4, rows, width), bf16),
            pltpu.VMEM((rows, width), bf16),
            pltpu.VMEM((rows, width), bf16),
            pltpu.SemaphoreType.DMA((64,)),
        ],
        compiler_params=pltpu.CompilerParams(vmem_limit_bytes=VMEM_LIMIT),
        cost_estimate=cost(25e9, 18e6),
        name="ffn_turn",
    )(core, resid, norm_in, norm_out, cotangent, valid, *weights)


def ffn_backward_kernel(base, parts, *refs):
    refs = list(refs)
    take = lambda number: [refs.pop(0) for _ in range(number)]
    core_ref, grad_from_hbm, resid_out_hbm, norm_out, resid_in_hbm, norm_in = take(6)
    weights = take(parts)
    grad_hbm, keep_hbm, send_hbm, norm_grad, early_grad = take(5)
    (w, grad_in, resid_out, resid_in, grad_out, halves, active, grad_pre, grad_low, low, ref) = take(11)
    sems = Sems(ref)
    core = core_ref[0]
    steps = resid_in.shape[0] // TILE
    w_in = block_copies(sems, weights, base, range(8), w, core)
    inputs = [
        by_rows(sems, grad_from_hbm, grad_in, steps),
        by_rows(sems, resid_out_hbm, resid_out, steps),
        by_rows(sems, resid_in_hbm, resid_in, steps),
    ]
    grad_to = by_rows(sems, grad_out, grad_hbm, steps)
    for step in range(steps):
        if step == 1:
            for index in (0, 4, 1, 5, 2, 6, 3, 7):
                start_all(*w_in[index])
        for chunked in inputs:
            chunked(step).start()
    norm_grad[...] = jnp.zeros(norm_grad.shape, f32)
    early_grad[...] = jnp.zeros(early_grad.shape, f32)

    def one_block(step, first):
        span = span_of(step)
        for chunked in inputs:
            chunked(step).wait()
        early, _ = normalise(resid_in[span, :])
        block_low = (early * norm_in[0:1, :] + norm_in[1:2, :]).astype(bf16)
        normed, scale_inv = normalise(resid_out[span, :])
        grad = grad_in[span, :]
        gain_part = jnp.sum(grad * normed, axis=0, keepdims=True)
        bias_part = jnp.sum(grad, axis=0, keepdims=True)
        grad = norm_back(grad, normed, scale_inv, norm_out[0:1, :])
        block_grad = grad.astype(bf16)
        pres, backs, actives, values = [], [], [], []
        for chunk in range(4):
            if first:
                wait_all(*w_in[chunk], *w_in[4 + chunk])
            pres.append(dot(block_low, matrix(w, chunk)))
            backs.append(dot(block_grad, matrix(w, 4 + chunk), 1, 1))
        for pre, back in zip(pres, backs):
            value, square, flat = gelu(pre)
            actives.append(value.astype(bf16))
            values.append((back * gelu_slope(pre, square, flat)).astype(bf16))
        for chunk in range(4):
            grad = grad + dot(values[chunk], matrix(w, chunk), 1, 1)
        grad_out[span, :] = grad
        grad_to(step).start()
        norm_grad[0:1, :] += gain_part
        norm_grad[1:2, :] += bias_part
        early_grad[0:1, :] += jnp.sum(grad * early, axis=0, keepdims=True)
        early_grad[1:2, :] += jnp.sum(grad, axis=0, keepdims=True)
        low[span, :] = block_low
        grad_low[span, :] = block_grad
        for chunk in range(4):
            active[chunk, span, :] = actives[chunk]
            grad_pre[chunk, span, :] = values[chunk]
        return 0

    one_block(0, True)
    lax.fori_loop(1, steps, lambda step, carry: one_block(step, False), 0)
    ffn_grads(steps, active, grad_low, low, grad_pre, halves, keep_hbm, send_hbm, sems, core)
    for step in range(steps):
        grad_to(step).wait()


def ffn_backward(core, grad, resid_out, norm_out, resid_in, norm_in, weights, base):
    rows, width = resid_in.shape
    high, low = layout_of(weights)
    half = array((8, high, low, width), bf16)
    norm_shape = array((2, width), f32)
    return pl.pallas_call(
        partial(ffn_backward_kernel, base, len(weights)),
        out_shape=[array((rows, width), f32), half, half, norm_shape, norm_shape],
        in_specs=[SMEM, HBM, HBM, VMEM, HBM, VMEM] + [HBM] * len(weights),
        out_specs=[HBM] * 3 + [VMEM] * 2,
        scratch_shapes=[
            pltpu.VMEM((8, high, 2, low, width), bf16),
            pltpu.VMEM((rows, width), f32),
            pltpu.VMEM((rows, width), f32),
            pltpu.VMEM((rows, width), f32),
            pltpu.VMEM((rows, width), f32),
            pltpu.VMEM((2, 8, high, low, width), bf16),
            pltpu.VMEM((4, rows, width), bf16),
            pltpu.VMEM((4, rows, width), bf16),
            pltpu.VMEM((rows, width), bf16),
            pltpu.VMEM((rows, width), bf16),
            pltpu.SemaphoreType.DMA((64,)),
        ],
        compiler_params=pltpu.CompilerParams(vmem_limit_bytes=VMEM_LIMIT),
        cost_estimate=cost(23e9, 18e6),
        name="ffn_backward",
    )(core, grad, resid_out, norm_out, resid_in, norm_in, *weights)


AXES = ("wide", "narrow")


def exchange_phases(mesh):
    devices = list(mesh.devices.reshape(-1))
    count = len(devices)
    bits = [1 << place for place in range(count.bit_length() - 1)]
    spots = [tuple(getattr(device, "coords", None) or ()) for device in devices]
    core, along, across = [], [], []
    for bit in bits:
        moved = [i for i, (p, q) in enumerate(zip(spots[0], spots[bit])) if p != q]
        if spots[0] and not moved:
            core.append(bit)
        elif moved == [2]:
            along.append(bit)
        else:
            across.append(bit)
    pairs = [across[i : i + 2] for i in range(0, len(across), 2)] + [[bit] for bit in core]
    plain = (count, bits[::-1], [along] + pairs if along else pairs)
    outward = (count, bits[::-1], [[bit] for bit in along] + pairs)
    inward = (count, bits[::-1], [[bit] for bit in along[::-1]] + pairs)
    return plain, outward, inward, len(along)


def halves_of(plan, rows):
    count, order, phases = plan
    block = rows // count
    bits = phases[-1]
    if len(bits) == 1 and (bits[0] * block) % 16 == 0:
        return count // (2 * bits[0]), bits[0] * block, True
    return 1, rows // 2, False


def masks_of(bits):
    masks = [0]
    for bit in bits:
        masks += [mask | bit for mask in masks]
    return masks


def swap(value, count, mask):
    return lax.ppermute(value, AXES, [(i, i ^ mask) for i in range(count)])


def nought_of(value):
    return jnp.minimum(jnp.abs(value[(0,) * value.ndim].astype(f32)), 0.0).astype(jnp.int32)


def noughts_of(values):
    return sum(nought_of(value) for value in values)


def spot_of(lead, bits_held, bits, mask, tail, nought=0):
    me = lax.axis_index(AXES) + nought
    spot = [0] * len(lead)
    for bit in bits_held:
        spot.append(jnp.where((me ^ mask) & bit != 0, 1, 0) if bit in bits else 0)
    return spot + [0] * len(tail)


def gather_send(plan, value, phase):
    count, order, phases = plan
    return [swap(value, count, mask) if mask else value for mask in masks_of(phases[phase])]


def gather_join(plan, pieces, phase, nought=0):
    count, order, phases = plan
    bits = phases[phase]
    held = [bit for group in phases[: phase + 1] for bit in group]
    held = [bit for bit in order if bit in held]
    lead, tail = pieces[0].shape[:1], pieces[0].shape[-2:]
    full = jnp.zeros(lead + (2,) * len(held) + tail, pieces[0].dtype)
    for mask, piece in zip(masks_of(bits), pieces):
        piece = piece.reshape(lead + tuple(1 if bit in bits else 2 for bit in held) + tail)
        full = lax.dynamic_update_slice(full, piece, spot_of(lead, held, bits, mask, tail, nought))
    return full


def scatter_send(plan, parts, phase, nought=0, summed=None):
    count, order, phases = plan
    bits = phases[phase]
    held = [bit for group in phases[: phase + 1] for bit in group]
    held = [bit for bit in order if bit in held]
    lead, tail = parts[0].shape[:1], parts[0].shape[-2:]
    sizes = lead + tuple(1 if bit in bits else 2 for bit in held) + tail
    pieces = []
    for mask in masks_of(bits):
        total = None
        for part in parts:
            piece = lax.dynamic_slice(part, spot_of(lead, held, bits, mask, tail, nought), sizes)
            if len(parts) > 1:
                piece = piece.astype(f32)
            total = piece if total is None else total + piece
        total = total.astype(bf16).reshape(lead + (2,) * (len(held) - len(bits)) + tail)
        if summed is not None:
            summed.append(total)
        pieces.append(swap(total, count, mask) if mask else total)
    return pieces


def scatter_end(parts, nought=0):
    total = sum(part.astype(f32) for part in parts[1:]) + parts[0].astype(f32)
    return jnp.where(nought == 0, total, 0.0)


def spread(plan, value):
    count, order, phases = plan
    return value.reshape((value.shape[0],) + (2,) * len(order) + (value.shape[1] // count, value.shape[2]))


def weights_send(plan, value, width):
    high, low, split = halves_of(plan, width)
    last = len(plan[2]) - 1
    if not split:
        full = gather_join(plan, gather_send(plan, value, last), last)
        return [full.reshape(-1, high, 2, low, width)]
    return [piece.reshape(-1, high, low, width) for piece in gather_send(plan, value, last)]


def grads_send(plan, keep, send, width):
    count, order, phases = plan
    high, low, split = halves_of(plan, width)
    last = len(phases) - 1
    blocks, rows = keep.shape[0], width // count
    if not split:
        full = jnp.stack([keep, send], axis=2).reshape(blocks, width, width)
        return scatter_send(plan, [spread(plan, full)], last)
    shape = (blocks,) + (2,) * (len(order) - 1) + (rows, width)
    return [keep.reshape(shape), swap(send, count, phases[last][0]).reshape(shape)]


def after(values, *others):
    values, _ = lax.optimization_barrier((values, others))
    return values


def put_norms(plan, halves, norm_grad):
    count, order, phases = plan
    blocks, high, low, width = halves.shape
    rows = width // count
    blocks = -(-10 // rows)
    value = jnp.pad(norm_grad, ((0, blocks * rows - 10), (0, 0))).reshape(blocks, 1, 1, rows, width)
    value = jnp.broadcast_to(value, (blocks, high, low // rows, rows, width)).astype(halves.dtype)
    return lax.dynamic_update_slice(halves, value.reshape(blocks, high, low, width), (4, 0, 0, 0))


def own_lanes(count, value):
    width = value.shape[-1]
    piece = width // count
    value = value.reshape(-1, width)[:10]
    return lax.dynamic_slice(value, (0, lax.axis_index(AXES) * piece), (10, piece)).reshape(5, 2, piece)


def pack_norms(count, norm_gain, norm_bias):
    piece = norm_gain.shape[1]
    width = count * piece
    shard = jnp.stack([norm_gain, norm_bias], axis=1).reshape(10, piece)
    blocks = -(-10 // piece)
    spot = lax.axis_index(AXES) * piece
    full = lax.dynamic_update_slice(jnp.zeros((blocks * piece, width), shard.dtype), shard, (0, spot))
    return full.reshape(blocks, piece, width)


def unpack_norms(piece, parts, start):
    width = parts[0].shape[-1]
    total = 0.0
    for part in parts:
        total = total + part[start:].reshape(part.shape[0] - start, -1, piece, width).astype(f32).sum(axis=1)
    return total.reshape(-1, width)[:10].reshape(5, 2, width)


def meet(outputs, *in_flight):
    return lax.optimization_barrier((tuple(outputs),) + in_flight)


def pack_attention(proj, mix):
    return jnp.concatenate([proj, mix[None]])


def pack_ffn(count, up, down):
    rows, width = up.shape[0], down.shape[1]
    up = up.reshape(rows, count, 4, rows).transpose(2, 0, 1, 3).reshape(4, rows, width)
    return jnp.concatenate([up, down.reshape(4, rows, width)])


def unpack_ffn(count, grad):
    rows, width = grad.shape[1:]
    up = grad[:4].reshape(4, rows, count, rows).transpose(1, 2, 0, 3).reshape(rows, 4 * width)
    return up, grad[4:].reshape(4 * rows, width)


def on_device(
    plans,
    source,
    target,
    source_segments,
    target_segments,
    encoder_proj,
    encoder_mix,
    encoder_up,
    encoder_down,
    self_proj,
    self_mix,
    cross_proj,
    cross_mix,
    decoder_up,
    decoder_down,
    norm_gain,
    norm_bias,
    cotangent,
):
    plan, outward, inward, along = plans
    count = plan[0]
    width = source.shape[-1]
    piece = norm_gain.shape[1]
    source_low = source.reshape(-1, width)
    target_low = target.reshape(-1, width)
    last = len(plan[2]) - 1
    high, low, split = halves_of(plan, width)
    if split:
        core = jnp.where(lax.axis_index(AXES) & plan[2][-1][0] != 0, 1, 0).astype(jnp.int32).reshape(1)
    else:
        core = jnp.zeros((1,), jnp.int32)

    enc = pack_attention(encoder_proj, encoder_mix)
    own = pack_attention(self_proj, self_mix)
    rest = jnp.concatenate(
        [
            pack_ffn(count, encoder_up, encoder_down),
            pack_attention(cross_proj, cross_mix),
            pack_norms(count, norm_gain, norm_bias),
        ]
    )
    rest = lax.all_gather(rest, AXES, axis=1, tiled=True)
    dec = pack_ffn(count, decoder_up, decoder_down)

    final = len(outward[2]) - 1
    source_cols = key_rows(source_segments)
    target_cols = key_rows(target_segments)
    source_rows = source_segments.reshape(-1, 1, BLOCK)
    target_rows = target_segments.reshape(-1, 1, BLOCK)
    enc_ranges = key_ranges(source_segments, source_segments, False)
    own_ranges = key_ranges(target_segments, target_segments, True)
    far_ranges = key_ranges(target_segments, source_segments, False)
    valid = jnp.broadcast_to((target_segments >= 0).reshape(-1, 1).astype(f32), (target_low.shape[0], 128))
    nought = noughts_of((enc_ranges, own_ranges, far_ranges, valid))

    enc, own, dec = meet(
        gather_send(plan, enc, 0), gather_send(outward, own, 0), gather_send(outward, dec, 0)
    )
    enc = gather_join(plan, enc, 0)
    own = gather_join(outward, own, 0)
    dec = gather_join(outward, dec, 0)
    for phase in range(1, last):
        enc = gather_send(plan, enc, phase)
        if phase < along:
            own = gather_send(outward, own, phase)
            enc, own = meet(enc, own)
            own = gather_join(outward, own, phase)
        enc = gather_join(plan, enc, phase, nought)
    enc = weights_send(plan, enc, width)
    for phase in range(along, final - 1):
        own = gather_join(outward, gather_send(outward, own, phase), phase)
    own = gather_send(outward, own, final - 1)
    dec = gather_send(outward, dec, along - 1)

    step = attend_forward(
        core, source_low, None, None, source_cols, source_rows, enc_ranges, enc, 0, False
    )
    (enc_one, *enc_saved), own, dec = meet(step, own, dec)
    own = weights_send(outward, gather_join(outward, own, final - 1), width)
    step = attend_forward(
        core, target_low, None, None, target_cols, target_rows, own_ranges, own, 0, True
    )
    (own_sum, *own_saved), rest = meet(step, rest)
    norms = unpack_norms(piece, [rest[12:]], 0)
    rest = [rest.reshape(-1, high, 2, low, width)]
    for phase in range(along, final):
        dec = gather_send(outward, gather_join(outward, dec, phase - 1, nought_of(norms) if phase == along else 0), phase)
    enc_two, enc_low = ffn_forward(core, enc_one, norms[0], norms[1], rest, 0)
    step = attend_forward(
        core, own_sum, norms[2], enc_low, source_cols, target_rows, far_ranges, rest, 8, False
    )
    (far_sum, second_low, *far_saved), dec = meet(step, dec)
    dec = weights_send(outward, gather_join(outward, dec, final - 1), width)
    decoded, grad, dec_keep, dec_send, norm_four = ffn_turn(
        core, far_sum, norms[3], norms[4], cotangent.reshape(-1, width), valid, dec, 0
    )
    def across(parts):
        for phase in range(final - 1, along - 1, -1):
            parts = scatter_send(inward, parts, phase)
        return parts

    dec_parts = across(grads_send(inward, dec_keep, dec_send, width))
    step = attend_backward(
        core, after(grad, dec_parts[0]), far_sum, norms[3], second_low, enc_low, far_saved, source_cols, target_rows,
        far_ranges, rest, 8, False, f32
    )
    (grad, grad_enc, far_keep, far_send, norm_three), dec_parts = meet(step, dec_parts)
    far_parts = grads_send(inward, far_keep, far_send, width)
    dec_parts = scatter_send(inward, dec_parts, along - 1)
    far_parts = across(far_parts)
    step = ffn_backward(
        core, after(grad_enc, far_parts[0], dec_parts[0]), enc_two, norms[1], enc_one, norms[0], rest, 0
    )
    (grad_enc, ffn_keep, ffn_send, norm_one, norm_zero), dec_parts, far_parts = meet(step, dec_parts, far_parts)
    ffn_parts = grads_send(inward, ffn_keep, ffn_send, width)
    for phase in range(along - 2, -1, -1):
        dec_parts = scatter_send(inward, dec_parts, phase)
    far_parts = scatter_send(inward, far_parts, along - 1)
    ffn_parts = across(ffn_parts)
    extra = -(-10 // piece)
    step = attend_backward(
        core, after(grad, dec_parts[0], ffn_parts[0], far_parts[0]), own_sum, norms[2], target_low, None, own_saved,
        target_cols, target_rows, own_ranges, own, 0, True, bf16, extra
    )
    (target_grad, own_keep, own_send, norm_two), dec_parts, far_parts, ffn_parts = meet(
        step, dec_parts, far_parts, ffn_parts
    )
    norm_grad = jnp.concatenate([norm_zero, norm_one, norm_two, norm_three, norm_four])
    own_parts = grads_send(inward, put_norms(plan, own_keep, norm_grad), put_norms(plan, own_send, norm_grad), width)
    for phase in range(along - 2, -1, -1):
        far_parts = scatter_send(inward, far_parts, phase)
    ffn_parts = scatter_send(inward, ffn_parts, along - 1)
    own_parts = across(own_parts)
    step = attend_backward(
        core, after(grad_enc, far_parts[0], ffn_parts[0], own_parts[0]), enc_one, norms[0], source_low, None,
        enc_saved, source_cols, source_rows, enc_ranges, enc, 0, False, bf16
    )
    (source_grad, enc_keep, enc_send, _), far_parts, ffn_parts, own_parts = meet(step, far_parts, ffn_parts, own_parts)
    enc_parts = grads_send(plan, enc_keep, enc_send, width)
    enc_parts = scatter_send(plan, enc_parts, last - 1)
    nought = nought_of(enc_parts[0])
    own_parts = scatter_send(inward, own_parts, along - 1, nought)
    for phase in range(along - 2, -1, -1):
        ffn_parts = scatter_send(inward, ffn_parts, phase, nought)
    for phase in range(last - 2, -1, -1):
        enc_parts = scatter_send(plan, enc_parts, phase)
    for phase in range(along - 2, -1, -1):
        own_parts = scatter_send(inward, own_parts, phase)
    dec_sums, far_sums, ffn_sums, own_sums, enc_sums = [
        scatter_end(parts, nought) for parts in (dec_parts, far_parts, ffn_parts, own_parts, enc_parts)
    ]
    enc_up_out, enc_down_out = unpack_ffn(count, ffn_sums)
    dec_up_out, dec_down_out = unpack_ffn(count, dec_sums)
    norm_out = own_lanes(count, own_sums[4:])
    return (
        decoded.reshape(target.shape),
        source_grad.reshape(source.shape),
        target_grad.reshape(target.shape),
        enc_sums[:3],
        enc_sums[3],
        enc_up_out,
        enc_down_out,
        own_sums[:3],
        own_sums[3],
        far_sums[:3],
        far_sums[3],
        dec_up_out,
        dec_down_out,
        norm_out[:, 0],
        norm_out[:, 1],
    )


def solution(mesh):
    return jax.shard_map(
        partial(on_device, exchange_phases(mesh)),
        mesh=mesh,
        in_specs=(
            P(("wide", "narrow"), None, None),
            P(("wide", "narrow"), None, None),
            P(("wide", "narrow"), None),
            P(("wide", "narrow"), None),
            P(None, ("wide", "narrow"), None),
            P(("wide", "narrow"), None),
            P(("wide", "narrow"), None),
            P(("wide", "narrow"), None),
            P(None, ("wide", "narrow"), None),
            P(("wide", "narrow"), None),
            P(None, ("wide", "narrow"), None),
            P(("wide", "narrow"), None),
            P(("wide", "narrow"), None),
            P(("wide", "narrow"), None),
            P(None, ("wide", "narrow")),
            P(None, ("wide", "narrow")),
            P(("wide", "narrow"), None, None),
        ),
        out_specs=(
            P(("wide", "narrow"), None, None),
            P(("wide", "narrow"), None, None),
            P(("wide", "narrow"), None, None),
            P(None, ("wide", "narrow"), None),
            P(("wide", "narrow"), None),
            P(("wide", "narrow"), None),
            P(("wide", "narrow"), None),
            P(None, ("wide", "narrow"), None),
            P(("wide", "narrow"), None),
            P(None, ("wide", "narrow"), None),
            P(("wide", "narrow"), None),
            P(("wide", "narrow"), None),
            P(("wide", "narrow"), None),
            P(None, ("wide", "narrow")),
            P(None, ("wide", "narrow")),
        ),
        check_vma=False,
    )
```

```python
from functools import partial

import jax
import jax.numpy as jnp
from jax import lax
from jax.experimental import pallas as pl
from jax.experimental.pallas import tpu as pltpu
from jax.sharding import PartitionSpec as P

HEADS = 8
norm_eps = 1e-05
masked_score = -1e30
lowest = -3e38
log2_e = 1.4426950408889634
BLOCK = 128
TILE = 256
VMEM_LIMIT = 60 * 2**20
f32 = jnp.float32
bf16 = jnp.bfloat16


def dot(left, right, left_dim=1, right_dim=0):
    dims = (((left_dim,), (right_dim,)), ((), ()))
    return lax.dot_general(left, right, dims, preferred_element_type=f32)


def normalise(resid):
    mean = jnp.mean(resid, axis=-1, keepdims=True)
    centred = resid - mean
    scale_inv = lax.rsqrt(jnp.mean(centred * centred, axis=-1, keepdims=True) + norm_eps)
    return centred * scale_inv, scale_inv


def norm_back(grad, normed, scale_inv, gain):
    scaled = grad * gain
    mean_plain = jnp.mean(scaled, axis=-1, keepdims=True)
    mean_normed = jnp.mean(scaled * normed, axis=-1, keepdims=True)
    return scale_inv * (scaled - mean_plain - normed * mean_normed)


def key_ranges(query_segments, key_segments, causal):
    big = jnp.int32(1 << 30)
    query_order = jnp.where(query_segments < 0, big, query_segments).reshape(-1, BLOCK)
    key_order = jnp.where(key_segments < 0, big, key_segments).reshape(1, -1)
    first = jnp.sum((key_order < query_order[:, :1]).astype(jnp.int32), axis=1)
    stop = jnp.sum((key_order <= query_order[:, -1:]).astype(jnp.int32), axis=1)
    real = jnp.sum((key_order < big).astype(jnp.int32))
    if causal:
        stop = jnp.minimum(stop, (jnp.arange(stop.shape[0]) + 1) * BLOCK)
    start = first // 16 * 16
    units = (stop - start + BLOCK - 1) // BLOCK
    real_units = jnp.maximum((jnp.minimum(stop, real) - start + BLOCK - 1) // BLOCK, 0)
    real_units = jnp.where(first >= real, 0, real_units)
    return jnp.stack([start, units // 2, units % 2, real_units // 2, real_units % 2]).astype(jnp.int32)


def key_rows(key_segments):
    flat = jnp.pad(key_segments.reshape(-1), (0, TILE), constant_values=-2)
    return flat.reshape(-1, 1, BLOCK)


def fill_columns(key_col, key_seg):
    for index in range(key_seg.shape[0]):
        key_col[index * BLOCK : (index + 1) * BLOCK, :] = jnp.broadcast_to(key_seg[index], (BLOCK, BLOCK)).T


def head_pair_mask():
    lane = lax.broadcasted_iota(jnp.int32, (1, 128), 1)
    return lane < 64


def stack_heads(block, even):
    zero = jnp.zeros_like(block)
    return jnp.concatenate([jnp.where(even, block, zero), jnp.where(even, zero, block)], axis=0)


def tile_bias(bias_ref, key_col_ref, query_row, key_start, query_start, causal, size):
    allowed = key_col_ref[pl.ds(key_start, size), :] == query_row
    if causal:
        key_place = key_start + lax.broadcasted_iota(jnp.int32, (size, BLOCK), 0)
        query_place = query_start + lax.broadcasted_iota(jnp.int32, (size, BLOCK), 1)
        allowed = allowed & (key_place <= query_place)
    bias_ref[:size, :] = jnp.where(allowed, 0.0, masked_score).astype(f32)


HBM = pl.BlockSpec(memory_space=pltpu.HBM)
VMEM = pl.BlockSpec(memory_space=pltpu.VMEM)
SMEM = pl.BlockSpec(memory_space=pltpu.SMEM)


class Sems:
    def __init__(self, ref):
        self.ref = ref
        self.used = 0

    def take(self, number=1):
        self.used += number
        return self.used - number

    def copy(self, src, dst, place):
        return pltpu.make_async_copy(src, dst, self.ref.at[place])


def span_of(step):
    return pl.ds(step * TILE if isinstance(step, int) else pl.multiple_of(step * TILE, TILE), TILE)


def by_rows(sems, src, dst, steps):
    first = sems.take(steps)
    return lambda step: sems.copy(src.at[span_of(step)], dst.at[span_of(step)], first + step)


def by_columns(sems, src, dst, steps):
    first = sems.take(steps)
    return lambda step: sems.copy(src.at[:, span_of(step)], dst.at[:, span_of(step)], first + step)


def whole(sems, src, dst):
    place = sems.take()
    return lambda: sems.copy(src, dst, place)


def weight_copies(sems, parts, base, start, size, dst, core):
    span = pl.ds(start, size)
    if len(parts) == 1:
        return [whole(sems, parts[0].at[pl.ds(base + start, size)], dst.at[span])]
    source = pl.ds(base + start, size)
    return [
        whole(sems, parts[0].at[source], dst.at[span, :, core]),
        whole(sems, parts[1].at[source], dst.at[span, :, 1 - core]),
    ]


def block_copies(sems, parts, base, blocks, dst, core):
    return {index: weight_copies(sems, parts, base, index, 1, dst, core) for index in blocks}


def start_all(*copies):
    for copy in copies:
        copy().start()


def wait_all(*copies):
    for copy in copies:
        copy().wait()


def matrix(blocks, index):
    block = blocks[index]
    return block.reshape(block.shape[0] * block.shape[1] * block.shape[2], block.shape[3])


def put_grad(halves, index, value, core):
    value = value.astype(bf16)
    high, low = halves.shape[2:4]
    for major in range(high):
        for side in range(2):
            at = (2 * major + side) * low
            halves[core if side == 0 else 1 - core, index, major] = value[at : at + low]


def forward_kernel(causal, fresh, base, parts, *refs):
    refs = list(refs)
    take = lambda number: [refs.pop(0) for _ in range(number)]
    core_ref, ranges, own_hbm = take(3)
    norm_own, other_hbm = (None, own_hbm) if fresh else take(2)
    key_seg, query_seg = take(2)
    weights = take(parts)
    (resid_hbm,) = take(1)
    (low_hbm,) = (None,) if fresh else take(1)
    q_hbm, k_hbm, v_hbm, o_hbm, lse_out = take(5)
    w, own, key_col, resid_out, q_out, k_out, v_out, o_out, stacked, bias, acc, peak, total, ref = take(14)
    other, low_out = (own, None) if fresh else take(2)
    sems = Sems(ref)
    core = core_ref[0]
    rows = own.shape[0]
    steps = rows // TILE
    even = head_pair_mask()
    scale = 0.125 * log2_e
    proj_in = weight_copies(sems, weights, base, 0, 3, w, core)
    own_in = by_rows(sems, own_hbm, own, steps)
    other_in = None if fresh else by_rows(sems, other_hbm, other, steps)
    mix_in = weight_copies(sems, weights, base, 3, 1, w, core)
    start_all(*proj_in)
    for step in range(steps):
        own_in(step).start()
        if not fresh:
            other_in(step).start()
    start_all(*mix_in)
    fill_columns(key_col, key_seg)
    q_to = by_rows(sems, q_out, q_hbm, steps)
    k_to = whole(sems, k_out, k_hbm)
    v_to = whole(sems, v_out, v_hbm)
    o_to = by_columns(sems, o_out, o_hbm, steps)
    resid_to = by_rows(sems, resid_out, resid_hbm, steps)
    low_to = None if fresh else by_rows(sems, low_out, low_hbm, steps)
    wait_all(*proj_in)

    def fill(step, carry):
        span = span_of(step)
        own_in(step).wait()
        block = own[span, :]
        if fresh:
            block_low = block
            key_block = block
        else:
            other_in(step).wait()
            normed, _ = normalise(block)
            block_low = (normed * norm_own[0:1, :] + norm_own[1:2, :]).astype(bf16)
            low_out[span, :] = block_low
            low_to(step).start()
            key_block = other[span, :]
        query = dot(block_low, matrix(w, 0)).astype(bf16)
        key = dot(key_block, matrix(w, 1)).astype(bf16)
        value = dot(key_block, matrix(w, 2)).astype(bf16)
        q_out[span, :] = query
        q_to(step).start()
        k_out[span, :] = key
        v_out[span, :] = value
        for sub in range(TILE // BLOCK):
            for pair in range(4):
                part = query[sub * BLOCK : (sub + 1) * BLOCK, pair * 128 : (pair + 1) * 128]
                stacked[step * (TILE // BLOCK) + sub, pair] = stack_heads(part, even)
        return carry

    lax.fori_loop(0, steps, fill, 0)
    k_out[rows:, :] = jnp.zeros((TILE, k_out.shape[1]), bf16)
    v_out[rows:, :] = jnp.zeros((TILE, v_out.shape[1]), bf16)
    start_all(k_to, v_to)

    def one_block(index, carry):
        start = ranges[0, index]
        tiles = ranges[1, index]
        halves_left = ranges[2, index]
        query_start = pl.multiple_of(index * BLOCK, BLOCK)
        query_row = query_seg[index]
        peak[...] = jnp.full(peak.shape, lowest, f32)
        total[...] = jnp.zeros(total.shape, f32)
        acc[...] = jnp.zeros(acc.shape, f32)

        def one_tile(at, size):
            at = pl.multiple_of(at, 16)
            tile_bias(bias, key_col, query_row, at, query_start, causal, size)
            span = pl.ds(at, size)
            lanes = [slice(pair * 128, (pair + 1) * 128) for pair in range(4)]
            ahead = 4
            raw = [dot(k_out[span, lanes[pair]], stacked[index, pair], 1, 1) for pair in range(ahead)]
            befores = [peak[pair : pair + 1, :] for pair in range(4)]
            totals = [total[pair : pair + 1, :] for pair in range(4)]
            blocked = jnp.concatenate([bias[:size, :]] * 2, axis=1)
            peaks, sums, mixes, shrinks = [], [], [], []
            for pair in range(4):
                scores = raw[pair] * scale + blocked
                above = jnp.maximum(befores[pair], jnp.max(scores, axis=0, keepdims=True))
                probs = jnp.exp2(scores - above)
                shrink = jnp.exp2(befores[pair] - above)
                if pair + ahead < 4:
                    raw.append(dot(k_out[span, lanes[pair + ahead]], stacked[index, pair + ahead], 1, 1))
                sums.append(totals[pair] * shrink + jnp.sum(probs, axis=0, keepdims=True))
                peaks.append(above)
                shrinks.append(shrink)
                mixes.append(dot(v_out[span, lanes[pair]], probs.astype(bf16), 0, 0))
            for pair in range(4):
                peak[pair : pair + 1, :] = peaks[pair]
                total[pair : pair + 1, :] = sums[pair]
                top = pair * 128
                mixed = mixes[pair]
                shrink = shrinks[pair]
                acc[top : top + 64, :] = acc[top : top + 64, :] * shrink[:, :128] + mixed[:64, :128]
                acc[top + 64 : top + 128, :] = (
                    acc[top + 64 : top + 128, :] * shrink[:, 128:] + mixed[64:, 128:]
                )
            return 0

        lax.fori_loop(0, tiles, lambda tile, inner: one_tile(start + tile * TILE, TILE), 0)
        lax.fori_loop(0, halves_left, lambda tile, inner: one_tile(start + tiles * TILE, BLOCK), 0)
        for pair in range(4):
            inverse = 1.0 / total[pair : pair + 1, :]
            top = pair * 128
            o_out[top : top + 64, pl.ds(query_start, BLOCK)] = (
                acc[top : top + 64, :] * inverse[:, :128]
            ).astype(bf16)
            o_out[top + 64 : top + 128, pl.ds(query_start, BLOCK)] = (
                acc[top + 64 : top + 128, :] * inverse[:, 128:]
            ).astype(bf16)
        lse_out[index] = peak[...] + jnp.log2(total[...])
        return carry

    lax.fori_loop(0, rows // BLOCK, one_block, 0)
    wait_all(*mix_in)

    def finish(step, carry):
        span = span_of(step)
        o_to(step).start()
        block = own[span, :]
        if fresh:
            block = block.astype(f32)
        else:
            normed, _ = normalise(block)
            block = normed * norm_own[0:1, :] + norm_own[1:2, :]
        resid_out[span, :] = block + dot(o_out[:, span], matrix(w, 3), 0, 0)
        resid_to(step).start()
        return carry

    lax.fori_loop(0, steps, finish, 0)
    wait_all(k_to, v_to)
    for step in range(steps):
        q_to(step).wait()
        o_to(step).wait()
        if not fresh:
            low_to(step).wait()
        resid_to(step).wait()


def cost(flops, moved):
    return pl.CostEstimate(flops=int(flops), bytes_accessed=int(moved), transcendentals=0)


def array(shape, dtype):
    return jax.ShapeDtypeStruct(shape, dtype)


def attend_forward(core, own, norm_own, other, key_col, query_seg, ranges, weights, base, causal):
    fresh = norm_own is None
    rows, width = own.shape
    blocks = rows // BLOCK
    high, low = layout_of(weights)
    ins = [own] if fresh else [own, norm_own, other]
    specs = [HBM] if fresh else [HBM, VMEM, HBM]
    ins += [key_col, query_seg, *weights]
    specs += [VMEM, VMEM] + [HBM] * len(weights)
    shapes = [array((rows, width), f32)]
    if not fresh:
        shapes.append(array((rows, width), bf16))
    shapes += [
        array((rows, width), bf16),
        array((rows + TILE, width), bf16),
        array((rows + TILE, width), bf16),
        array((width, rows), bf16),
        array((blocks, 4, 2 * BLOCK), f32),
    ]
    scratch = [
        pltpu.VMEM((4, high, 2, low, width), bf16),
        pltpu.VMEM((rows, width), own.dtype),
        pltpu.VMEM((rows + TILE, 128), jnp.int32),
        pltpu.VMEM((rows, width), f32),
        pltpu.VMEM((rows, width), bf16),
        pltpu.VMEM((rows + TILE, width), bf16),
        pltpu.VMEM((rows + TILE, width), bf16),
        pltpu.VMEM((width, rows), bf16),
        pltpu.VMEM((blocks, 4, 2 * BLOCK, 128), bf16),
        pltpu.VMEM((TILE, BLOCK), f32),
        pltpu.VMEM((width, BLOCK), f32),
        pltpu.VMEM((4, 2 * BLOCK), f32),
        pltpu.VMEM((4, 2 * BLOCK), f32),
        pltpu.SemaphoreType.DMA((64,)),
    ]
    if not fresh:
        scratch += [pltpu.VMEM((rows, width), bf16)] * 2
    return pl.pallas_call(
        partial(forward_kernel, causal, fresh, base, len(weights)),
        out_shape=shapes,
        in_specs=[SMEM, SMEM] + specs,
        out_specs=[HBM] * (len(shapes) - 1) + [VMEM],
        scratch_shapes=scratch,
        compiler_params=pltpu.CompilerParams(vmem_limit_bytes=VMEM_LIMIT),
        cost_estimate=cost(20e9, 12e6) if fresh else cost(1e9, 1e6),
        name="attend_forward",
    )(core, ranges, *ins)


def layout_of(weights):
    shape = weights[0].shape
    return (shape[1], shape[2]) if len(weights) == 2 else (shape[1], shape[3])


def backward_kernel(causal, same, base, parts, *refs):
    refs = list(refs)
    take = lambda number: [refs.pop(0) for _ in range(number)]
    core_ref, ranges, grad_hbm, resid_hbm, norm, own_hbm = take(6)
    other_hbm = None if same else take(1)[0]
    q_hbm, k_hbm, v_hbm, o_hbm, lse, key_seg, query_seg = take(7)
    weights = take(parts)
    (own_grad_hbm,) = take(1)
    other_grad_hbm = None if same else take(1)[0]
    keep_hbm, send_hbm, norm_grad = take(3)
    (w, grad, resid, own, q_in, k_in, v_in, o_in, key_col, sums, own_grad, halves,
     low, stacked, grad_stacked, inner_rows, bias, acc, dq, dk, dv, ref) = take(22)
    other, other_grad = (own, None) if same else take(2)
    sems = Sems(ref)
    core = core_ref[0]
    rows = own.shape[0]
    steps = rows // TILE
    even = head_pair_mask()
    scale = 0.125 * log2_e

    mix_in = weight_copies(sems, weights, base, 3, 1, w, core)
    grad_in = by_rows(sems, grad_hbm, grad, steps)
    resid_in = by_rows(sems, resid_hbm, resid, steps)
    o_from = by_columns(sems, o_hbm, o_in, steps)
    q_from = by_rows(sems, q_hbm, q_in, steps)
    later = [whole(sems, k_hbm, k_in), whole(sems, v_hbm, v_in)]
    last = [whole(sems, own_hbm, own)] + weight_copies(sems, weights, base, 0, 3, w, core)
    if not same:
        last.append(whole(sems, other_hbm, other))
    start_all(*mix_in)
    for step in range(steps):
        for chunked in (grad_in, resid_in, o_from, q_from):
            chunked(step).start()
    start_all(*later, *last)
    fill_columns(key_col, key_seg)
    keep_to = [whole(sems, halves.at[0, index], keep_hbm.at[index]) for index in range(4)]
    send_to = [whole(sems, halves.at[1, index], send_hbm.at[index]) for index in range(4)]
    own_to = by_rows(sems, own_grad, own_grad_hbm, steps)
    other_to = None if same else by_rows(sems, other_grad, other_grad_hbm, steps)

    norm_grad[...] = jnp.zeros(norm_grad.shape, f32)
    dk[...] = jnp.zeros(dk.shape, f32)
    dv[...] = jnp.zeros(dv.shape, f32)
    wait_all(*mix_in)

    def prepare(step, carry):
        span = span_of(step)
        for chunked in (grad_in, resid_in, o_from, q_from):
            chunked(step).wait()
        block = grad[span, :]
        normed, scale_inv = normalise(resid[span, :])
        norm_grad[0:1, :] += jnp.sum(block * normed, axis=0, keepdims=True)
        norm_grad[1:2, :] += jnp.sum(block, axis=0, keepdims=True)
        block = norm_back(block, normed, scale_inv, norm[0:1, :])
        whole_block = block
        block = block.astype(bf16)
        grad_mixed = dot(block, matrix(w, 3), 1, 1).astype(bf16)
        flipped = dot(matrix(w, 3), block, 1, 1).astype(bf16).astype(f32)
        sums[span, :] = whole_block
        low[span, :] = block
        flipped = flipped * o_in[:, span].astype(f32)
        inner = [jnp.sum(flipped[head * 64 : (head + 1) * 64, :], axis=0, keepdims=True) for head in range(HEADS)]
        query = q_in[span, :]
        for sub in range(TILE // BLOCK):
            spot = step * (TILE // BLOCK) + sub
            part = slice(sub * BLOCK, (sub + 1) * BLOCK)
            rows_of = []
            for pair in range(4):
                lanes = slice(pair * 128, (pair + 1) * 128)
                stacked[spot, pair] = stack_heads(query[part, lanes], even)
                grad_stacked[spot, pair] = stack_heads(grad_mixed[part, lanes], even)
                rows_of.append(jnp.concatenate([inner[2 * pair][:, part], inner[2 * pair + 1][:, part]], axis=1))
            inner_rows[spot] = jnp.concatenate(rows_of, axis=0)
        return carry

    lax.fori_loop(0, steps, prepare, 0)
    put_grad(halves, 3, dot(o_in[...], low[...]), core)
    start_all(keep_to[3], send_to[3])
    wait_all(*later)

    def one_block(index, carry):
        start = ranges[0, index]
        tiles = ranges[3, index]
        halves_left = ranges[4, index]
        query_start = pl.multiple_of(index * BLOCK, BLOCK)
        query_row = query_seg[index]
        acc[...] = jnp.zeros(acc.shape, f32)

        def one_tile(at, size):
            at = pl.multiple_of(at, 16)
            tile_bias(bias, key_col, query_row, at, query_start, causal, size)
            span = pl.ds(at, size)
            lanes = [slice(pair * 128, (pair + 1) * 128) for pair in range(4)]
            keys = [k_in[span, lanes[pair]] for pair in range(4)]
            queries = [stacked[index, pair] for pair in range(4)]
            grads = [grad_stacked[index, pair] for pair in range(4)]
            blocked = jnp.concatenate([bias[:size, :]] * 2, axis=1)
            raw = [dot(keys[0], queries[0], 1, 1)]
            grad_raw = [dot(v_in[span, lanes[0]], grads[0], 1, 1)]
            dvs, dks, mixes = [], [], []
            for pair in range(4):
                if pair < 3:
                    raw.append(dot(keys[pair + 1], queries[pair + 1], 1, 1))
                    grad_raw.append(dot(v_in[span, lanes[pair + 1]], grads[pair + 1], 1, 1))
                probs = jnp.exp2(raw[pair] * scale + blocked - lse[index, pair : pair + 1, :])
                grad_scores = (probs * (grad_raw[pair] - inner_rows[index, pair : pair + 1, :])).astype(bf16)
                dvs.append(dot(probs.astype(bf16), grads[pair]))
                dks.append(dot(grad_scores, queries[pair]))
                mixes.append(dot(keys[pair], grad_scores, 0, 0))
            dv[span, :] += jnp.concatenate(dvs, axis=1)
            dk[span, :] += jnp.concatenate(dks, axis=1)
            for pair in range(4):
                top = pair * 128
                acc[top : top + 64, :] += mixes[pair][:64, :128]
                acc[top + 64 : top + 128, :] += mixes[pair][64:, 128:]
            return 0

        lax.fori_loop(0, tiles, lambda tile, inner: one_tile(start + tile * TILE, TILE), 0)
        lax.fori_loop(0, halves_left, lambda tile, inner: one_tile(start + tiles * TILE, BLOCK), 0)
        dq[pl.ds(query_start, BLOCK), : acc.shape[0]] = (acc[...].T * 0.125).astype(bf16)
        return carry

    lax.fori_loop(0, rows // BLOCK, one_block, 0)
    width = own.shape[1]
    dq[:, width : 2 * width] = (dk[:rows, :] * 0.125).astype(bf16)
    dq[:, 2 * width :] = dv[:rows, :].astype(bf16)
    wait_all(*last)
    groups = ((own, 0, 3),) if same else ((own, 0, 1), (other, 1, 3))
    for left, first, stop in groups:
        value = dot(left[...], dq[:, first * width : stop * width], 0, 0)
        for index in range(first, stop):
            place = (index - first) * width
            put_grad(halves, index, value[:, place : place + width], core)
            start_all(keep_to[index], send_to[index])

    def finish(step, carry):
        span = span_of(step)
        query_side = sums[span, :] + dot(dq[span, :width], matrix(w, 0), 1, 1)
        source_side = dot(dq[span, width : 2 * width], matrix(w, 1), 1, 1)
        source_side = source_side + dot(dq[span, 2 * width :], matrix(w, 2), 1, 1)
        if same:
            own_grad[span, :] = (query_side + source_side).astype(own_grad.dtype)
        else:
            own_grad[span, :] = query_side
            other_grad[span, :] = source_side
            other_to(step).start()
        own_to(step).start()
        return carry

    lax.fori_loop(0, steps, finish, 0)
    wait_all(*keep_to, *send_to)
    for step in range(steps):
        own_to(step).wait()
        if not same:
            other_to(step).wait()


def attend_backward(
    core, grad, resid, norm, own, other, saved, key_col, query_seg, ranges, weights, base, causal, out_dtype, extra=0
):
    same = other is None
    rows, width = own.shape
    blocks = rows // BLOCK
    high, low = layout_of(weights)
    q, k, v, o, lse = saved
    ins = [grad, resid, norm, own] + ([] if same else [other])
    specs = [HBM, HBM, VMEM, HBM] + ([] if same else [HBM])
    ins += [q, k, v, o, lse, key_col, query_seg, *weights]
    specs += [HBM] * 4 + [VMEM, VMEM, VMEM] + [HBM] * len(weights)
    shapes = [array((rows, width), out_dtype)]
    if not same:
        shapes.append(array((rows, width), f32))
    shapes += [array((4 + extra, high, low, width), bf16)] * 2
    shapes.append(array((2, width), f32))
    scratch = [
        pltpu.VMEM((4, high, 2, low, width), bf16),
        pltpu.VMEM((rows, width), f32),
        pltpu.VMEM((rows, width), f32),
        pltpu.VMEM((rows, width), bf16),
        pltpu.VMEM((rows, width), bf16),
        pltpu.VMEM((rows + TILE, width), bf16),
        pltpu.VMEM((rows + TILE, width), bf16),
        pltpu.VMEM((width, rows), bf16),
        pltpu.VMEM((rows + TILE, 128), jnp.int32),
        pltpu.VMEM((rows, width), f32),
        pltpu.VMEM((rows, width), out_dtype),
        pltpu.VMEM((2, 4, high, low, width), bf16),
        pltpu.VMEM((rows, width), bf16),
        pltpu.VMEM((blocks, 4, 2 * BLOCK, 128), bf16),
        pltpu.VMEM((blocks, 4, 2 * BLOCK, 128), bf16),
        pltpu.VMEM((blocks, 4, 2 * BLOCK), f32),
        pltpu.VMEM((TILE, BLOCK), f32),
        pltpu.VMEM((width, BLOCK), f32),
        pltpu.VMEM((rows, 3 * width), bf16),
        pltpu.VMEM((rows + TILE, width), f32),
        pltpu.VMEM((rows + TILE, width), f32),
        pltpu.SemaphoreType.DMA((64,)),
    ]
    if not same:
        scratch += [pltpu.VMEM((rows, width), bf16), pltpu.VMEM((rows, width), f32)]
    return pl.pallas_call(
        partial(backward_kernel, causal, same, base, len(weights)),
        out_shape=shapes,
        in_specs=[SMEM, SMEM] + specs,
        out_specs=[HBM] * (len(shapes) - 1) + [VMEM],
        scratch_shapes=scratch,
        compiler_params=pltpu.CompilerParams(vmem_limit_bytes=VMEM_LIMIT),
        cost_estimate=cost(25e9, 20e6),
        name="attend_backward",
    )(core, ranges, *ins)


root_two_pi = 0.7978845608028654


def gelu(pre):
    square = pre * pre
    flat = jnp.tanh(pre * (root_two_pi + (root_two_pi * 0.044715) * square))
    return pre * (0.5 + 0.5 * flat), square, flat


def gelu_slope(pre, square, flat):
    half = 0.5 + 0.5 * flat
    inner = (0.5 * root_two_pi) + (1.5 * root_two_pi * 0.044715) * square
    return half + pre * ((1.0 - flat * flat) * inner)


def ffn_forward_kernel(base, parts, *refs):
    refs = list(refs)
    take = lambda number: [refs.pop(0) for _ in range(number)]
    core_ref, resid_hbm, norm_in, norm_out = take(4)
    weights = take(parts)
    resid_to_hbm, low_hbm, w, resid_in, resid_out, low_out, ref = take(7)
    sems = Sems(ref)
    core = core_ref[0]
    steps = resid_in.shape[0] // TILE
    w_in = block_copies(sems, weights, base, range(8), w, core)
    resid_from = by_rows(sems, resid_hbm, resid_in, steps)
    resid_to = by_rows(sems, resid_out, resid_to_hbm, steps)
    low_to = by_rows(sems, low_out, low_hbm, steps)
    resid_from(0).start()
    for index in range(8):
        start_all(*w_in[index])
    for step in range(1, steps):
        resid_from(step).start()

    def one_block(step, first):
        span = span_of(step)
        resid_from(step).wait()
        normed, _ = normalise(resid_in[span, :])
        block = normed * norm_in[0:1, :] + norm_in[1:2, :]
        block_low = block.astype(bf16)
        pres = []
        for chunk in range(4):
            if first:
                wait_all(*w_in[chunk])
            pres.append(dot(block_low, matrix(w, chunk)))
        actives = [gelu(pre)[0].astype(bf16) for pre in pres]
        for chunk in range(4):
            if first:
                wait_all(*w_in[4 + chunk])
            block = block + dot(actives[chunk], matrix(w, 4 + chunk))
        resid_out[span, :] = block
        resid_to(step).start()
        normed, _ = normalise(block)
        low_out[span, :] = (normed * norm_out[0:1, :] + norm_out[1:2, :]).astype(bf16)
        low_to(step).start()
        return 0

    one_block(0, True)
    lax.fori_loop(1, steps, lambda step, carry: one_block(step, False), 0)
    for step in range(steps):
        resid_to(step).wait()
        low_to(step).wait()


def ffn_forward(core, resid, norm_in, norm_out, weights, base):
    rows, width = resid.shape
    high, low = layout_of(weights)
    return pl.pallas_call(
        partial(ffn_forward_kernel, base, len(weights)),
        out_shape=[array((rows, width), f32), array((rows, width), bf16)],
        in_specs=[SMEM, HBM, VMEM, VMEM] + [HBM] * len(weights),
        out_specs=[HBM, HBM],
        scratch_shapes=[
            pltpu.VMEM((8, high, 2, low, width), bf16),
            pltpu.VMEM((rows, width), f32),
            pltpu.VMEM((rows, width), f32),
            pltpu.VMEM((rows, width), bf16),
            pltpu.SemaphoreType.DMA((32,)),
        ],
        compiler_params=pltpu.CompilerParams(vmem_limit_bytes=VMEM_LIMIT),
        cost_estimate=cost(1e9, 1e6),
        name="ffn_forward",
    )(core, resid, norm_in, norm_out, *weights)


def ffn_grads(steps, active, grad_low, block_low, grad_pre, halves, keep_hbm, send_hbm, sems, core):
    first = sems.take(16)

    def out(index, side):
        target = send_hbm if side else keep_hbm
        return sems.copy(halves.at[side, index], target.at[index], first + 2 * index + side)

    def weight_part(chunk, carry):
        put_grad(halves, chunk, dot(block_low[...], grad_pre[chunk], 0, 0), core)
        out(chunk, 0).start()
        out(chunk, 1).start()
        put_grad(halves, 4 + chunk, dot(active[chunk], grad_low[...], 0, 0), core)
        out(4 + chunk, 0).start()
        out(4 + chunk, 1).start()
        return carry

    lax.fori_loop(0, 4, weight_part, 0)
    for index in range(8):
        out(index, 0).wait()
        out(index, 1).wait()


def ffn_turn_kernel(base, parts, *refs):
    refs = list(refs)
    take = lambda number: [refs.pop(0) for _ in range(number)]
    core_ref, resid_hbm, norm_in, norm_out, cotangent_hbm, segments = take(6)
    weights = take(parts)
    final_hbm, grad_hbm, keep_hbm, send_hbm, norm_grad = take(5)
    (w, resid_in, cotangent, valid, final_out, grad_out, halves,
     active, grad_pre, grad_low, low, ref) = take(12)
    sems = Sems(ref)
    core = core_ref[0]
    steps = resid_in.shape[0] // TILE
    w_in = block_copies(sems, weights, base, range(8), w, core)
    inputs = [
        by_rows(sems, resid_hbm, resid_in, steps),
        by_rows(sems, cotangent_hbm, cotangent, steps),
    ]
    final_to = by_rows(sems, final_out, final_hbm, steps)
    grad_to = by_rows(sems, grad_out, grad_hbm, steps)
    for step in range(steps):
        if step == 1:
            for index in range(8):
                start_all(*w_in[index])
        for chunked in inputs:
            chunked(step).start()
    fill_columns(valid, segments)
    norm_grad[...] = jnp.zeros(norm_grad.shape, f32)

    def one_block(step, first):
        span = span_of(step)
        for chunked in inputs:
            chunked(step).wait()
        normed, _ = normalise(resid_in[span, :])
        block = normed * norm_in[0:1, :] + norm_in[1:2, :]
        block_low = block.astype(bf16)
        pres = []
        for chunk in range(4):
            if first:
                wait_all(*w_in[chunk])
            pres.append(dot(block_low, matrix(w, chunk)))
        actives, slopes = [], []
        for pre in pres:
            value, square, flat = gelu(pre)
            actives.append(value.astype(bf16))
            slopes.append(gelu_slope(pre, square, flat))
        for chunk in range(4):
            if first:
                wait_all(*w_in[4 + chunk])
            block = block + dot(actives[chunk], matrix(w, 4 + chunk))
        normed, scale_inv = normalise(block)
        grad = cotangent[span, :].astype(f32) * jnp.concatenate([(valid[span, :] >= 0).astype(f32)] * 4, axis=1)
        gain_part = jnp.sum(grad * normed, axis=0, keepdims=True)
        bias_part = jnp.sum(grad, axis=0, keepdims=True)
        grad = norm_back(grad, normed, scale_inv, norm_out[0:1, :])
        block_grad = grad.astype(bf16)
        values = [
            (dot(block_grad, matrix(w, 4 + chunk), 1, 1) * slopes[chunk]).astype(bf16) for chunk in range(4)
        ]
        for chunk in range(4):
            grad = grad + dot(values[chunk], matrix(w, chunk), 1, 1)
        grad_out[span, :] = grad
        grad_to(step).start()
        final_out[span, :] = (normed * norm_out[0:1, :] + norm_out[1:2, :]).astype(bf16)
        final_to(step).start()
        norm_grad[0:1, :] += gain_part
        norm_grad[1:2, :] += bias_part
        low[span, :] = block_low
        grad_low[span, :] = block_grad
        for chunk in range(4):
            active[chunk, span, :] = actives[chunk]
            grad_pre[chunk, span, :] = values[chunk]
        return 0

    one_block(0, True)
    lax.fori_loop(1, steps, lambda step, carry: one_block(step, False), 0)
    ffn_grads(steps, active, grad_low, low, grad_pre, halves, keep_hbm, send_hbm, sems, core)
    for step in range(steps):
        final_to(step).wait()
        grad_to(step).wait()


def ffn_turn(core, resid, norm_in, norm_out, cotangent, segments, weights, base):
    rows, width = resid.shape
    high, low = layout_of(weights)
    half = array((8, high, low, width), bf16)
    return pl.pallas_call(
        partial(ffn_turn_kernel, base, len(weights)),
        out_shape=[array((rows, width), bf16), array((rows, width), f32), half, half, array((2, width), f32)],
        in_specs=[SMEM, HBM, VMEM, VMEM, HBM, VMEM] + [HBM] * len(weights),
        out_specs=[HBM] * 4 + [VMEM],
        scratch_shapes=[
            pltpu.VMEM((8, high, 2, low, width), bf16),
            pltpu.VMEM((rows, width), f32),
            pltpu.VMEM((rows, width), bf16),
            pltpu.VMEM((rows + TILE, 128), jnp.int32),
            pltpu.VMEM((rows, width), bf16),
            pltpu.VMEM((rows, width), f32),
            pltpu.VMEM((2, 8, high, low, width), bf16),
            pltpu.VMEM((4, rows, width), bf16),
            pltpu.VMEM((4, rows, width), bf16),
            pltpu.VMEM((rows, width), bf16),
            pltpu.VMEM((rows, width), bf16),
            pltpu.SemaphoreType.DMA((64,)),
        ],
        compiler_params=pltpu.CompilerParams(vmem_limit_bytes=VMEM_LIMIT),
        cost_estimate=cost(25e9, 18e6),
        name="ffn_turn",
    )(core, resid, norm_in, norm_out, cotangent, segments, *weights)


def ffn_backward_kernel(base, parts, *refs):
    refs = list(refs)
    take = lambda number: [refs.pop(0) for _ in range(number)]
    core_ref, grad_from_hbm, resid_out_hbm, norm_out, resid_in_hbm, norm_in = take(6)
    weights = take(parts)
    grad_hbm, keep_hbm, send_hbm, norm_grad, early_grad = take(5)
    (w, grad_in, resid_out, resid_in, grad_out, halves, active, grad_pre, grad_low, low, ref) = take(11)
    sems = Sems(ref)
    core = core_ref[0]
    steps = resid_in.shape[0] // TILE
    w_in = block_copies(sems, weights, base, range(8), w, core)
    inputs = [
        by_rows(sems, grad_from_hbm, grad_in, steps),
        by_rows(sems, resid_out_hbm, resid_out, steps),
        by_rows(sems, resid_in_hbm, resid_in, steps),
    ]
    grad_to = by_rows(sems, grad_out, grad_hbm, steps)
    for step in range(steps):
        if step == 1:
            for index in (0, 4, 1, 5, 2, 6, 3, 7):
                start_all(*w_in[index])
        for chunked in inputs:
            chunked(step).start()
    norm_grad[...] = jnp.zeros(norm_grad.shape, f32)
    early_grad[...] = jnp.zeros(early_grad.shape, f32)

    def one_block(step, first):
        span = span_of(step)
        for chunked in inputs:
            chunked(step).wait()
        early, _ = normalise(resid_in[span, :])
        block_low = (early * norm_in[0:1, :] + norm_in[1:2, :]).astype(bf16)
        normed, scale_inv = normalise(resid_out[span, :])
        grad = grad_in[span, :]
        gain_part = jnp.sum(grad * normed, axis=0, keepdims=True)
        bias_part = jnp.sum(grad, axis=0, keepdims=True)
        grad = norm_back(grad, normed, scale_inv, norm_out[0:1, :])
        block_grad = grad.astype(bf16)
        pres, backs, actives, values = [], [], [], []
        for chunk in range(4):
            if first:
                wait_all(*w_in[chunk], *w_in[4 + chunk])
            pres.append(dot(block_low, matrix(w, chunk)))
            backs.append(dot(block_grad, matrix(w, 4 + chunk), 1, 1))
        for pre, back in zip(pres, backs):
            value, square, flat = gelu(pre)
            actives.append(value.astype(bf16))
            values.append((back * gelu_slope(pre, square, flat)).astype(bf16))
        for chunk in range(4):
            grad = grad + dot(values[chunk], matrix(w, chunk), 1, 1)
        grad_out[span, :] = grad
        grad_to(step).start()
        norm_grad[0:1, :] += gain_part
        norm_grad[1:2, :] += bias_part
        early_grad[0:1, :] += jnp.sum(grad * early, axis=0, keepdims=True)
        early_grad[1:2, :] += jnp.sum(grad, axis=0, keepdims=True)
        low[span, :] = block_low
        grad_low[span, :] = block_grad
        for chunk in range(4):
            active[chunk, span, :] = actives[chunk]
            grad_pre[chunk, span, :] = values[chunk]
        return 0

    one_block(0, True)
    lax.fori_loop(1, steps, lambda step, carry: one_block(step, False), 0)
    ffn_grads(steps, active, grad_low, low, grad_pre, halves, keep_hbm, send_hbm, sems, core)
    for step in range(steps):
        grad_to(step).wait()


def ffn_backward(core, grad, resid_out, norm_out, resid_in, norm_in, weights, base):
    rows, width = resid_in.shape
    high, low = layout_of(weights)
    half = array((8, high, low, width), bf16)
    norm_shape = array((2, width), f32)
    return pl.pallas_call(
        partial(ffn_backward_kernel, base, len(weights)),
        out_shape=[array((rows, width), f32), half, half, norm_shape, norm_shape],
        in_specs=[SMEM, HBM, HBM, VMEM, HBM, VMEM] + [HBM] * len(weights),
        out_specs=[HBM] * 3 + [VMEM] * 2,
        scratch_shapes=[
            pltpu.VMEM((8, high, 2, low, width), bf16),
            pltpu.VMEM((rows, width), f32),
            pltpu.VMEM((rows, width), f32),
            pltpu.VMEM((rows, width), f32),
            pltpu.VMEM((rows, width), f32),
            pltpu.VMEM((2, 8, high, low, width), bf16),
            pltpu.VMEM((4, rows, width), bf16),
            pltpu.VMEM((4, rows, width), bf16),
            pltpu.VMEM((rows, width), bf16),
            pltpu.VMEM((rows, width), bf16),
            pltpu.SemaphoreType.DMA((64,)),
        ],
        compiler_params=pltpu.CompilerParams(vmem_limit_bytes=VMEM_LIMIT),
        cost_estimate=cost(23e9, 18e6),
        name="ffn_backward",
    )(core, grad, resid_out, norm_out, resid_in, norm_in, *weights)


AXES = ("wide", "narrow")


def exchange_phases(mesh):
    devices = list(mesh.devices.reshape(-1))
    count = len(devices)
    bits = [1 << place for place in range(count.bit_length() - 1)]
    spots = [tuple(getattr(device, "coords", None) or ()) for device in devices]
    core, along, across = [], [], []
    for bit in bits:
        moved = [i for i, (p, q) in enumerate(zip(spots[0], spots[bit])) if p != q]
        if spots[0] and not moved:
            core.append(bit)
        elif moved == [2]:
            along.append(bit)
        else:
            across.append(bit)
    pairs = [across[i : i + 2] for i in range(0, len(across), 2)] + [[bit] for bit in core]
    plain = (count, bits[::-1], [along] + pairs if along else pairs)
    outward = (count, bits[::-1], [[bit] for bit in along] + pairs)
    inward = (count, bits[::-1], [[bit] for bit in along[::-1]] + pairs)
    return plain, outward, inward, len(along)


def halves_of(plan, rows):
    count, order, phases = plan
    block = rows // count
    bits = phases[-1]
    if len(bits) == 1 and (bits[0] * block) % 16 == 0:
        return count // (2 * bits[0]), bits[0] * block, True
    return 1, rows // 2, False


def masks_of(bits):
    masks = [0]
    for bit in bits:
        masks += [mask | bit for mask in masks]
    return masks


def swap(value, count, mask):
    return lax.ppermute(value, AXES, [(i, i ^ mask) for i in range(count)])


def nought_of(value):
    return jnp.minimum(jnp.abs(value[(0,) * value.ndim].astype(f32)), 0.0).astype(jnp.int32)


def noughts_of(values):
    return sum(nought_of(value) for value in values)


def spot_of(lead, bits_held, bits, mask, tail, nought=0):
    me = lax.axis_index(AXES) + nought
    spot = [0] * len(lead)
    for bit in bits_held:
        spot.append(jnp.where((me ^ mask) & bit != 0, 1, 0) if bit in bits else 0)
    return spot + [0] * len(tail)


def gather_send(plan, value, phase):
    count, order, phases = plan
    return [swap(value, count, mask) if mask else value for mask in masks_of(phases[phase])]


def gather_join(plan, pieces, phase, nought=0):
    count, order, phases = plan
    bits = phases[phase]
    held = [bit for group in phases[: phase + 1] for bit in group]
    held = [bit for bit in order if bit in held]
    lead, tail = pieces[0].shape[:1], pieces[0].shape[-2:]
    full = jnp.zeros(lead + (2,) * len(held) + tail, pieces[0].dtype)
    for mask, piece in zip(masks_of(bits), pieces):
        piece = piece.reshape(lead + tuple(1 if bit in bits else 2 for bit in held) + tail)
        full = lax.dynamic_update_slice(full, piece, spot_of(lead, held, bits, mask, tail, nought))
    return full


def scatter_send(plan, parts, phase, nought=0, summed=None):
    count, order, phases = plan
    bits = phases[phase]
    held = [bit for group in phases[: phase + 1] for bit in group]
    held = [bit for bit in order if bit in held]
    lead, tail = parts[0].shape[:1], parts[0].shape[-2:]
    sizes = lead + tuple(1 if bit in bits else 2 for bit in held) + tail
    pieces = []
    for mask in masks_of(bits):
        total = None
        for part in parts:
            piece = lax.dynamic_slice(part, spot_of(lead, held, bits, mask, tail, nought), sizes)
            if len(parts) > 1:
                piece = piece.astype(f32)
            total = piece if total is None else total + piece
        total = total.astype(bf16).reshape(lead + (2,) * (len(held) - len(bits)) + tail)
        if summed is not None:
            summed.append(total)
        pieces.append(swap(total, count, mask) if mask else total)
    return pieces


def scatter_end(parts, nought=0):
    total = sum(part.astype(f32) for part in parts[1:]) + parts[0].astype(f32)
    return jnp.where(nought == 0, total, 0.0)


def spread(plan, value):
    count, order, phases = plan
    return value.reshape((value.shape[0],) + (2,) * len(order) + (value.shape[1] // count, value.shape[2]))


def weights_send(plan, value, width):
    high, low, split = halves_of(plan, width)
    last = len(plan[2]) - 1
    if not split:
        full = gather_join(plan, gather_send(plan, value, last), last)
        return [full.reshape(-1, high, 2, low, width)]
    return [piece.reshape(-1, high, low, width) for piece in gather_send(plan, value, last)]


def grads_send(plan, keep, send, width):
    count, order, phases = plan
    high, low, split = halves_of(plan, width)
    last = len(phases) - 1
    blocks, rows = keep.shape[0], width // count
    if not split:
        full = jnp.stack([keep, send], axis=2).reshape(blocks, width, width)
        return scatter_send(plan, [spread(plan, full)], last)
    shape = (blocks,) + (2,) * (len(order) - 1) + (rows, width)
    return [keep.reshape(shape), swap(send, count, phases[last][0]).reshape(shape)]


def after(values, *others):
    values, _ = lax.optimization_barrier((values, others))
    return values


def put_norms(plan, halves, norm_grad):
    count, order, phases = plan
    blocks, high, low, width = halves.shape
    rows = width // count
    blocks = -(-10 // rows)
    value = jnp.pad(norm_grad, ((0, blocks * rows - 10), (0, 0))).reshape(blocks, 1, 1, rows, width)
    value = jnp.broadcast_to(value, (blocks, high, low // rows, rows, width)).astype(halves.dtype)
    return lax.dynamic_update_slice(halves, value.reshape(blocks, high, low, width), (4, 0, 0, 0))


def own_lanes(count, value):
    width = value.shape[-1]
    piece = width // count
    value = value.reshape(-1, width)[:10]
    return lax.dynamic_slice(value, (0, lax.axis_index(AXES) * piece), (10, piece)).reshape(5, 2, piece)


def pack_norms(count, norm_gain, norm_bias):
    piece = norm_gain.shape[1]
    width = count * piece
    shard = jnp.stack([norm_gain, norm_bias], axis=1).reshape(10, piece)
    blocks = -(-10 // piece)
    spot = lax.axis_index(AXES) * piece
    full = lax.dynamic_update_slice(jnp.zeros((blocks * piece, width), shard.dtype), shard, (0, spot))
    return full.reshape(blocks, piece, width)


def unpack_norms(piece, parts, start):
    width = parts[0].shape[-1]
    total = 0.0
    for part in parts:
        total = total + part[start:].reshape(part.shape[0] - start, -1, piece, width).astype(f32).sum(axis=1)
    return total.reshape(-1, width)[:10].reshape(5, 2, width)


def meet(outputs, *in_flight):
    return lax.optimization_barrier((tuple(outputs),) + in_flight)


def pack_attention(proj, mix):
    return jnp.concatenate([proj, mix[None]])


def pack_ffn(count, up, down):
    rows, width = up.shape[0], down.shape[1]
    up = up.reshape(rows, count, 4, rows).transpose(2, 0, 1, 3).reshape(4, rows, width)
    return jnp.concatenate([up, down.reshape(4, rows, width)])


def unpack_ffn(count, up, down):
    rows, width = up.shape[1:]
    up = up.reshape(4, rows, count, rows).transpose(1, 2, 0, 3).reshape(rows, 4 * width)
    return up, down.reshape(4 * rows, width)


def on_device(
    plans,
    source,
    target,
    source_segments,
    target_segments,
    encoder_proj,
    encoder_mix,
    encoder_up,
    encoder_down,
    self_proj,
    self_mix,
    cross_proj,
    cross_mix,
    decoder_up,
    decoder_down,
    norm_gain,
    norm_bias,
    cotangent,
):
    plan, outward, inward, along = plans
    count = plan[0]
    width = source.shape[-1]
    piece = norm_gain.shape[1]
    source_low = source.reshape(-1, width)
    target_low = target.reshape(-1, width)
    last = len(plan[2]) - 1
    high, low, split = halves_of(plan, width)
    if split:
        core = jnp.where(lax.axis_index(AXES) & plan[2][-1][0] != 0, 1, 0).astype(jnp.int32).reshape(1)
    else:
        core = jnp.zeros((1,), jnp.int32)

    enc = pack_attention(encoder_proj, encoder_mix)
    own = pack_attention(self_proj, self_mix)
    rest = jnp.concatenate(
        [
            pack_ffn(count, encoder_up, encoder_down),
            pack_attention(cross_proj, cross_mix),
            pack_norms(count, norm_gain, norm_bias),
        ]
    )
    rest = lax.all_gather(rest, AXES, axis=1, tiled=True)
    dec = pack_ffn(count, decoder_up, decoder_down)

    final = len(outward[2]) - 1
    source_cols = key_rows(source_segments)
    target_cols = key_rows(target_segments)
    source_rows = source_segments.reshape(-1, 1, BLOCK)
    target_rows = target_segments.reshape(-1, 1, BLOCK)
    enc_ranges = key_ranges(source_segments, source_segments, False)
    own_ranges = key_ranges(target_segments, target_segments, True)
    far_ranges = key_ranges(target_segments, source_segments, False)
    nought = noughts_of((enc_ranges, own_ranges, far_ranges))

    enc, own, dec = meet(
        gather_send(plan, enc, 0), gather_send(outward, own, 0), gather_send(outward, dec, 0)
    )
    enc = gather_join(plan, enc, 0)
    own = gather_join(outward, own, 0)
    dec = gather_join(outward, dec, 0)
    for phase in range(1, last):
        enc = gather_send(plan, enc, phase)
        if phase < along:
            own = gather_send(outward, own, phase)
            enc, own = meet(enc, own)
            own = gather_join(outward, own, phase)
        enc = gather_join(plan, enc, phase, nought)
    enc = weights_send(plan, enc, width)
    for phase in range(along, final - 1):
        own = gather_join(outward, gather_send(outward, own, phase), phase)
    own = gather_send(outward, own, final - 1)
    dec = gather_send(outward, dec, along - 1)

    step = attend_forward(
        core, source_low, None, None, source_cols, source_rows, enc_ranges, enc, 0, False
    )
    (enc_one, *enc_saved), own, dec = meet(step, own, dec)
    own = weights_send(outward, gather_join(outward, own, final - 1), width)
    step = attend_forward(
        core, target_low, None, None, target_cols, target_rows, own_ranges, own, 0, True
    )
    (own_sum, *own_saved), rest = meet(step, rest)
    norms = unpack_norms(piece, [rest[12:]], 0)
    rest = [rest.reshape(-1, high, 2, low, width)]
    for phase in range(along, final):
        dec = gather_send(outward, gather_join(outward, dec, phase - 1, nought_of(norms) if phase == along else 0), phase)
    enc_two, enc_low = ffn_forward(core, enc_one, norms[0], norms[1], rest, 0)
    step = attend_forward(
        core, own_sum, norms[2], enc_low, source_cols, target_rows, far_ranges, rest, 8, False
    )
    (far_sum, second_low, *far_saved), dec = meet(step, dec)
    dec = weights_send(outward, gather_join(outward, dec, final - 1), width)
    decoded, grad, dec_keep, dec_send, norm_four = ffn_turn(
        core, far_sum, norms[3], norms[4], cotangent.reshape(-1, width), target_cols, dec, 0
    )
    def across(parts):
        for phase in range(final - 1, along - 1, -1):
            parts = scatter_send(inward, parts, phase)
        return parts

    dec_parts = across(grads_send(inward, dec_keep, dec_send, width))
    step = attend_backward(
        core, after(grad, dec_parts[0]), far_sum, norms[3], second_low, enc_low, far_saved, source_cols, target_rows,
        far_ranges, rest, 8, False, f32
    )
    (grad, grad_enc, far_keep, far_send, norm_three), dec_parts = meet(step, dec_parts)
    far_parts = grads_send(inward, far_keep, far_send, width)
    dec_parts = scatter_send(inward, dec_parts, along - 1)
    far_parts = across(far_parts)
    step = ffn_backward(
        core, after(grad_enc, far_parts[0], dec_parts[0]), enc_two, norms[1], enc_one, norms[0], rest, 0
    )
    (grad_enc, ffn_keep, ffn_send, norm_one, norm_zero), dec_parts, far_parts = meet(step, dec_parts, far_parts)
    ffn_parts = grads_send(inward, ffn_keep, ffn_send, width)
    for phase in range(along - 2, -1, -1):
        dec_parts = scatter_send(inward, dec_parts, phase)
    far_parts = scatter_send(inward, far_parts, along - 1)
    ffn_parts = across(ffn_parts)
    extra = -(-10 // piece)
    step = attend_backward(
        core, after(grad, dec_parts[0], ffn_parts[0], far_parts[0]), own_sum, norms[2], target_low, None, own_saved,
        target_cols, target_rows, own_ranges, own, 0, True, bf16, extra
    )
    (target_grad, own_keep, own_send, norm_two), dec_parts, far_parts, ffn_parts = meet(
        step, dec_parts, far_parts, ffn_parts
    )
    norm_grad = jnp.concatenate([norm_zero, norm_one, norm_two, norm_three, norm_four])
    own_parts = grads_send(inward, put_norms(plan, own_keep, norm_grad), put_norms(plan, own_send, norm_grad), width)
    for phase in range(along - 2, -1, -1):
        far_parts = scatter_send(inward, far_parts, phase)
    ffn_parts = scatter_send(inward, ffn_parts, along - 1)
    own_parts = across(own_parts)
    step = attend_backward(
        core, after(grad_enc, far_parts[0], ffn_parts[0], own_parts[0]), enc_one, norms[0], source_low, None,
        enc_saved, source_cols, source_rows, enc_ranges, enc, 0, False, bf16
    )
    (source_grad, enc_keep, enc_send, _), far_parts, ffn_parts, own_parts = meet(step, far_parts, ffn_parts, own_parts)
    enc_parts = grads_send(plan, enc_keep, enc_send, width)
    enc_parts = scatter_send(plan, enc_parts, last - 1)
    nought = nought_of(enc_parts[0])
    own_parts = scatter_send(inward, own_parts, along - 1, nought)
    for phase in range(along - 2, -1, -1):
        ffn_parts = scatter_send(inward, ffn_parts, phase, nought)
    for phase in range(last - 2, -1, -1):
        enc_parts = scatter_send(plan, enc_parts, phase)
    for phase in range(along - 2, -1, -1):
        own_parts = scatter_send(inward, own_parts, phase)
    def ends(parts, start, stop):
        return scatter_end([part[start:stop] for part in parts], nought)

    enc_up_out, enc_down_out = unpack_ffn(count, ends(ffn_parts, 0, 4), ends(ffn_parts, 4, 8))
    dec_up_out, dec_down_out = unpack_ffn(count, ends(dec_parts, 0, 4), ends(dec_parts, 4, 8))
    norm_out = own_lanes(count, ends(own_parts, 4, 4 + extra))
    return (
        decoded.reshape(target.shape),
        source_grad.reshape(source.shape),
        target_grad.reshape(target.shape),
        ends(enc_parts, 0, 3),
        ends(enc_parts, 3, 4)[0],
        enc_up_out,
        enc_down_out,
        ends(own_parts, 0, 3),
        ends(own_parts, 3, 4)[0],
        ends(far_parts, 0, 3),
        ends(far_parts, 3, 4)[0],
        dec_up_out,
        dec_down_out,
        norm_out[:, 0],
        norm_out[:, 1],
    )


def solution(mesh):
    return jax.shard_map(
        partial(on_device, exchange_phases(mesh)),
        mesh=mesh,
        in_specs=(
            P(("wide", "narrow"), None, None),
            P(("wide", "narrow"), None, None),
            P(("wide", "narrow"), None),
            P(("wide", "narrow"), None),
            P(None, ("wide", "narrow"), None),
            P(("wide", "narrow"), None),
            P(("wide", "narrow"), None),
            P(("wide", "narrow"), None),
            P(None, ("wide", "narrow"), None),
            P(("wide", "narrow"), None),
            P(None, ("wide", "narrow"), None),
            P(("wide", "narrow"), None),
            P(("wide", "narrow"), None),
            P(("wide", "narrow"), None),
            P(None, ("wide", "narrow")),
            P(None, ("wide", "narrow")),
            P(("wide", "narrow"), None, None),
        ),
        out_specs=(
            P(("wide", "narrow"), None, None),
            P(("wide", "narrow"), None, None),
            P(("wide", "narrow"), None, None),
            P(None, ("wide", "narrow"), None),
            P(("wide", "narrow"), None),
            P(("wide", "narrow"), None),
            P(("wide", "narrow"), None),
            P(None, ("wide", "narrow"), None),
            P(("wide", "narrow"), None),
            P(None, ("wide", "narrow"), None),
            P(("wide", "narrow"), None),
            P(("wide", "narrow"), None),
            P(("wide", "narrow"), None),
            P(None, ("wide", "narrow")),
            P(None, ("wide", "narrow")),
        ),
        check_vma=False,
    )
```
